32 devices in a mesh: pb: 4 (over z), ka: 4 (over y, core), ha: 2 (over x).
Axes of the slice: x: 2, y: 2, z: 4, core: 2. Of those that a mesh axis runs over, the one named last changes fastest.
Arguments:
- queries: bfloat16 [4096, 4096], P('pb', 'ha'), may hold values from -512 to 512
- keys: bfloat16 [8, 4, 128, 512], P('pb', 'ka', None, 'ha'), may hold values from -6 to 6
- values: bfloat16 [8, 4, 128, 512], P('pb', 'ka', None, 'ha'), may hold values from -6 to 6
- q_order: int32 [32], P('pb'), may hold values from 0 to 31, as said below
- block_mask: int32 [32, 32], P('pb'), may hold values from 0 to 1, as said below
Outputs:
- attended: bfloat16 [4096, 4096], P(('pb', 'ka'), 'ha')
The draws below stay inside these ranges and needn't reach their ends.
Inputs may be any that keep to these rules, and one draw needn't show every extreme that they name: `q_order`: slots 2m and 2m+1 hold query blocks i and 31 - i for some i, in either order; every block sits in exactly one slot. block_mask[s, b] is 1 only where b <= q_order[s], and block_mask[s, q_order[s]] is 1. For every m and every r below 4, slots 2m and 2m+1 together list at most 4 key blocks b with b % 4 == r, and exactly 4 for some m and r in every draw.
All inputs are finite; a program needn't handle non-finite values.
Results may differ from the reference program's by a relative error of at most 0.0042.
Values may be sent and summed in bfloat16 or wider, within the bound.
No kernel may reach another device: no remote copies, remote signals or barrier semaphores. Data moves between devices by JAX's collectives and lax.ppermute only.
A program may use at most 128 MiB of HBM per device.

```python
import math
import jax
import jax.numpy as jnp
from jax import lax

HEAD_DIM = 128
Q_HEADS = 32
KV_HEADS = 4
BLOCK = 128
NBLOCKS = 32
TOKENS = 4096
RESIDUES = 4
PAIR_CAP = 4


def pairing_order(key):
    base = jax.random.fold_in(key, 101)
    half_count = NBLOCKS // 2
    early = jax.random.permutation(jax.random.fold_in(base, 1), half_count).astype(jnp.int32)
    flipped = jax.random.randint(jax.random.fold_in(base, 2), (half_count,), 0, 2)
    late = NBLOCKS - 1 - early
    first = jnp.where(flipped == 0, early, late)
    second = jnp.where(flipped == 0, late, early)
    return jnp.stack([first, second], axis=1).reshape(NBLOCKS).astype(jnp.int32)


def listed_blocks(key):
    order = pairing_order(key)
    base = jax.random.fold_in(key, 202)
    half_count = NBLOCKS // 2
    class_blocks = NBLOCKS // RESIDUES
    pair_blocks = order.reshape(half_count, 2)
    rows_t = jnp.arange(class_blocks, dtype=jnp.int32)
    rows_r = jnp.arange(RESIDUES, dtype=jnp.int32)
    block_ids = rows_t[:, None] * RESIDUES + rows_r[None, :]
    target = pair_blocks[:, :, None, None]
    usable = block_ids[None, None] <= target
    diagonal = block_ids[None, None] == target
    noise = jax.random.randint(jax.random.fold_in(base, 1), (half_count, 2, class_blocks, RESIDUES), 0, 2 ** 20)
    priority = jnp.where(diagonal, 2 ** 21, jnp.where(usable, noise, -1)).astype(jnp.int32)
    span_size = 2 * class_blocks
    grouped = jnp.transpose(priority, (0, 3, 1, 2)).reshape(half_count, RESIDUES, span_size)
    distinct = grouped * span_size + jnp.arange(span_size, dtype=jnp.int32)
    ranking = jnp.argsort(-distinct, axis=-1)
    placing = jnp.argsort(ranking, axis=-1)
    wanted = jax.random.randint(jax.random.fold_in(base, 2), (half_count, RESIDUES), PAIR_CAP // 2, PAIR_CAP + 1)
    forced = jax.random.randint(jax.random.fold_in(base, 3), (), 0, half_count * RESIDUES)
    flat_ids = jnp.arange(half_count * RESIDUES, dtype=jnp.int32).reshape(half_count, RESIDUES)
    wanted = jnp.where(flat_ids == forced, PAIR_CAP, wanted)
    chosen = placing < wanted[:, :, None]
    chosen = chosen.reshape(half_count, RESIDUES, 2, class_blocks).transpose(0, 2, 3, 1)
    return chosen.reshape(NBLOCKS, NBLOCKS).astype(jnp.int32)


def key_field(key):
    base = jax.random.fold_in(key, 303)
    shape = (NBLOCKS, BLOCK, KV_HEADS, HEAD_DIM)
    field = jnp.clip(jax.random.normal(jax.random.fold_in(base, 1), shape, jnp.float32), -6.0, 6.0)
    return field


def draw_queries(key, part):
    base = jax.random.fold_in(key, 404)
    shape = (NBLOCKS, BLOCK, KV_HEADS, Q_HEADS // KV_HEADS, HEAD_DIM)
    field = jnp.clip(jax.random.normal(jax.random.fold_in(base, 1), shape, jnp.float32), -6.0, 6.0)
    return field.reshape(NBLOCKS * BLOCK, Q_HEADS * HEAD_DIM).astype(jnp.bfloat16)


def draw_keys(key, part):
    field = key_field(key)
    return field.reshape(NBLOCKS // RESIDUES, RESIDUES, BLOCK, KV_HEADS * HEAD_DIM).astype(jnp.bfloat16)


def draw_q_order(key, part):
    return pairing_order(key)


def draw_block_mask(key, part):
    return listed_blocks(key)


def steps_of(rng, shape, shards, smallest, largest):
    loudness, own = 1.0, jax.random.fold_in(rng, 6)
    for dim, blocks in shards:
        steps = jnp.exp(jax.random.uniform(jax.random.fold_in(own, dim), (blocks,), jnp.float32, smallest / len(shards), largest / len(shards)))
        loudness = loudness * jnp.repeat(steps, shape[dim] // blocks).reshape([-1 if axis == dim else 1 for axis in range(len(shape))])
    return loudness


def normal_values(key, dims, spread, reach, cuts=(), kind=jnp.bfloat16):
    factor_of = steps_of(key, dims, cuts, -0.22, 0.18) if cuts else 1.0
    result = jax.random.normal(key, dims, jnp.float32) * spread * factor_of
    return jnp.minimum(jnp.maximum(result, -reach), reach).astype(kind)


def setup_inputs(seed: int = 0) -> dict:
    seeds = jax.random.split(jax.random.key(seed), 6)
    queries = draw_queries(jax.random.fold_in(seeds[5], 71), 0)
    keys = draw_keys(jax.random.fold_in(seeds[5], 71), 0)
    values = normal_values(seeds[2], (NBLOCKS // RESIDUES, RESIDUES, BLOCK, KV_HEADS * HEAD_DIM), 1.0, 6.0, ((0, 4), (1, 4), (3, 2)))
    q_order = draw_q_order(jax.random.fold_in(seeds[5], 71), 0)
    block_mask = draw_block_mask(jax.random.fold_in(seeds[5], 71), 0)
    return {"queries": queries, "keys": keys, "values": values, "q_order": q_order, "block_mask": block_mask}


masked_score = -1e+30

def compact(listed, entry_count):
    running = jnp.cumsum(listed, axis=1)
    span_size = listed.shape[1]
    ranks = jnp.arange(entry_count, dtype=jnp.int32)
    picked = (listed[:, None, :] == 1) & (running[:, None, :] == ranks[None, :, None] + 1)
    places = jnp.arange(span_size, dtype=jnp.int32)
    position = lax.optimization_barrier(jnp.sum(jnp.where(picked, places[None, None, :], 0), axis=2)).astype(jnp.int32)
    living = jnp.any(picked, axis=2)
    return (position, living)

def reference(queries, keys, values, q_order, block_mask):
    head_width = HEAD_DIM
    group_size = Q_HEADS // KV_HEADS
    key_pool = keys.reshape(NBLOCKS, BLOCK, KV_HEADS, head_width).astype(jnp.float32)
    value_pool = values.reshape(NBLOCKS, BLOCK, KV_HEADS, head_width).astype(jnp.float32)
    query_units = queries.reshape(NBLOCKS // 2, 2, BLOCK, KV_HEADS, group_size, head_width)
    listed = block_mask.reshape(NBLOCKS // 2, 2 * NBLOCKS)
    pair_blocks = q_order.reshape(NBLOCKS // 2, 2)
    entry_count = PAIR_CAP * RESIDUES
    causal = jnp.arange(BLOCK)[:, None] >= jnp.arange(BLOCK)[None, :]

    def one_pair(unit_args):
        query_unit, flags, query_blocks = unit_args
        position, living = compact(flags[None, :], entry_count)
        position = position[0]
        living = living[0]
        owners = position // NBLOCKS
        key_block = position % NBLOCKS
        query_rows = jnp.take(query_unit.astype(jnp.float32), owners, axis=0)
        key_rows = jnp.take(key_pool, key_block, axis=0)
        value_rows = jnp.take(value_pool, key_block, axis=0)
        scores = jnp.einsum('eigxd,ejgd->egxij', query_rows, key_rows, precision=lax.Precision.HIGHEST)
        scores = scores * (1.0 / math.sqrt(head_width))
        diagonal = key_block == jnp.take(query_blocks, owners, axis=0)
        allowed = living[:, None, None, None, None] & (jnp.logical_not(diagonal)[:, None, None, None, None] | causal[None, None, None])
        scores = jnp.where(allowed, scores, masked_score)
        row_peak = lax.optimization_barrier(jnp.max(scores, axis=4))
        belongs = owners[:, None] == jnp.arange(2)[None, :]
        slot_peak = lax.optimization_barrier(jnp.max(jnp.where(belongs[:, :, None, None, None], row_peak[:, None], masked_score), axis=0))
        top_rows = jnp.take(slot_peak, owners, axis=0)
        weights = jnp.where(allowed, jnp.exp(scores - top_rows[..., None]), 0.0)
        rounded = lax.optimization_barrier(weights.astype(jnp.bfloat16)).astype(jnp.float32)
        partial_sum = jnp.einsum('egxij,ejgd->eigxd', rounded, value_rows, precision=lax.Precision.HIGHEST)
        belongs_f = belongs.astype(jnp.float32)
        numerator = jnp.einsum('es,eigxd->sigxd', belongs_f, partial_sum, precision=lax.Precision.HIGHEST)
        denominator = jnp.einsum('es,egxij->sigx', belongs_f, weights, precision=lax.Precision.HIGHEST)
        attended = numerator / denominator[..., None]
        return attended.astype(jnp.bfloat16).reshape(2 * BLOCK, Q_HEADS * head_width)
    outputs = lax.map(one_pair, (query_units, listed, pair_blocks))
    return outputs.reshape(TOKENS, Q_HEADS * head_width)
```

```python
import functools
import math

import jax
import jax.numpy as jnp
from jax import lax
from jax.experimental import pallas as pl
from jax.experimental.pallas import tpu as pltpu
from jax.sharding import PartitionSpec as P

HEAD_DIM = 128
HEADS_AT_ONCE = 4
MASKED = -1e30


def shift(array, axis, size, step):
    return lax.ppermute(array, axis, [(i, (i + step) % size) for i in range(size)])


def swap_in_ring(array, axis, size, cores, step, core_step):
    rings = size // cores
    pairs = []
    for ring in range(rings):
        for core in range(cores):
            to = ((ring + step) % rings) * cores + (core + core_step) % cores
            pairs.append((ring * cores + core, to))
    return lax.ppermute(array, axis, pairs)


def attend(
    sizes, order_ref, mask_ref, queries_ref, *refs
):
    pb, ka, cores, sources = sizes
    pieces = refs[: 2 * sources]
    out_ref, q_buf, k_pool, v_pool, scores, listed, sems = refs[2 * sources :]
    blocks_total, block_rows, kv_width = k_pool.shape
    kv_local = kv_width // HEAD_DIM
    group = queries_ref.shape[1] // kv_width
    class_local = pieces[0].shape[0]
    own_slots = q_buf.shape[0] // block_rows
    rings = ka // cores
    p_at, k_at = lax.axis_index("pb"), lax.axis_index("ka")
    ring_at, core_at = k_at // cores, k_at % cores

    copies = []
    q_copy = pltpu.make_async_copy(
        queries_ref.at[pl.ds(pl.multiple_of(k_at * q_buf.shape[0], block_rows), q_buf.shape[0])],
        q_buf,
        sems.at[0],
    )
    q_copy.start()
    copies.append(q_copy)
    index = 0
    for z in range(pb):
        for y in range(rings):
            for c in range(cores):
                source_p = lax.rem(p_at + (pb - z), pb)
                source_ring = lax.rem(ring_at + (rings - y), rings)
                source_core = lax.rem(core_at + (cores - c), cores)
                residue = source_ring * cores + source_core
                for t in range(class_local):
                    block = (source_p * class_local + t) * ka + residue
                    for which, pool in ((0, k_pool), (1, v_pool)):
                        copy = pltpu.make_async_copy(
                            pieces[2 * index + which].at[t, 0],
                            pool.at[block],
                            sems.at[1 + (2 * index + which) * class_local + t],
                        )
                        copy.start()
                        copies.append(copy)
                index += 1

    counts = []
    for s in range(own_slots):
        row = k_at * own_slots + s
        own_block = order_ref[row]
        listed[s, 0] = own_block

        def place(b, count):
            listed[s, count] = b
            return count + jnp.where(b == own_block, 0, mask_ref[row, b])

        counts.append(lax.fori_loop(0, blocks_total, place, 1))

    for copy in copies:
        copy.wait()

    scale = math.log2(math.e) / math.sqrt(HEAD_DIM)
    heads = min(HEADS_AT_ONCE, group)
    rows = heads * block_rows
    row_id = lax.broadcasted_iota(jnp.int32, (block_rows, block_rows), 0)
    col_id = lax.broadcasted_iota(jnp.int32, (block_rows, block_rows), 1)
    causal = jnp.concatenate([col_id <= row_id] * heads, axis=0)

    def dot_t(a, b):
        return lax.dot_general(a, b, (((1,), (1,)), ((), ())), preferred_element_type=jnp.float32)

    for s in range(own_slots):
        count = counts[s]
        odd = lax.rem(count, 2)
        for g in range(kv_local):
            columns = slice(g * HEAD_DIM, (g + 1) * HEAD_DIM)
            for first in range(0, group, heads):
                q_rows = jnp.concatenate(
                    [
                        q_buf[
                            s * block_rows : (s + 1) * block_rows,
                            (g * group + x) * HEAD_DIM : (g * group + x + 1) * HEAD_DIM,
                        ]
                        for x in range(first, first + heads)
                    ],
                    axis=0,
                )

                own = dot_t(q_rows, k_pool[listed[s, 0], :, columns])
                own = jnp.where(causal, own, MASKED)
                scores[0] = own

                def score_pair(u, top):
                    e = 1 + 2 * u
                    keys = jnp.concatenate(
                        [k_pool[listed[s, e], :, columns], k_pool[listed[s, e + 1], :, columns]],
                        axis=0,
                    )
                    pair = dot_t(q_rows, keys)
                    one, two = pair[:, :block_rows], pair[:, block_rows:]
                    scores[e] = one
                    scores[e + 1] = two
                    return jnp.maximum(top, jnp.maximum(one, two))

                pairs = (count - 1) // 2
                top = lax.fori_loop(0, pairs, score_pair, own)

                def score_last(top):
                    last = dot_t(q_rows, k_pool[listed[s, count - 1], :, columns])
                    scores[count - 1] = last
                    return jnp.maximum(top, last)

                top = lax.cond(odd == 0, score_last, lambda top: top, top)
                peak = jnp.max(top, axis=1, keepdims=True)

                def weigh(e):
                    return jnp.exp2((scores[e] - peak) * scale)

                def sum_pair(u, carry):
                    total, numerator = carry
                    e = 2 * u + odd
                    one, two = weigh(e), weigh(e + 1)
                    weights = jnp.concatenate(
                        [one.astype(jnp.bfloat16), two.astype(jnp.bfloat16)], axis=1
                    )
                    rows_v = jnp.concatenate(
                        [v_pool[listed[s, e], :, columns], v_pool[listed[s, e + 1], :, columns]],
                        axis=0,
                    )
                    return (
                        total + (one + two),
                        numerator + jnp.dot(weights, rows_v, preferred_element_type=jnp.float32),
                    )

                def sum_first():
                    one = weigh(0)
                    return one, jnp.dot(
                        one.astype(jnp.bfloat16),
                        v_pool[listed[s, 0], :, columns],
                        preferred_element_type=jnp.float32,
                    )

                zero = jnp.zeros((rows, block_rows), jnp.float32)
                zero_n = jnp.zeros((rows, HEAD_DIM), jnp.float32)
                carry = lax.cond(odd == 1, sum_first, lambda: (zero, zero_n))
                total, numerator = lax.fori_loop(0, count // 2, sum_pair, carry)
                result = numerator / jnp.sum(total, axis=1, keepdims=True)
                result = result.astype(jnp.bfloat16)
                for x in range(heads):
                    head = g * group + first + x
                    out_ref[
                        s * block_rows : (s + 1) * block_rows,
                        head * HEAD_DIM : (head + 1) * HEAD_DIM,
                    ] = result[x * block_rows : (x + 1) * block_rows]


def on_device(queries, keys, values, q_order, block_mask):
    pb, ka = lax.axis_size("pb"), lax.axis_size("ka")
    cores = 2 if ka % 2 == 0 else 1
    rings = ka // cores
    class_local, _, block_rows, kv_width = keys.shape
    block_total = block_mask.shape[1]
    slots = queries.shape[0] // block_rows
    own_slots = slots // ka

    pieces = []
    near = (keys, values)
    for z in range(pb):
        if z:
            near = tuple(shift(array, "pb", pb, 1) for array in near)
        ring = near
        for y in range(rings):
            if y:
                ring = tuple(swap_in_ring(array, "ka", ka, cores, 1, 0) for array in ring)
            here = ring
            for c in range(cores):
                if c:
                    here = tuple(swap_in_ring(array, "ka", ka, cores, 0, 1) for array in here)
                pieces.extend(here)

    sources = pb * ka
    kernel = functools.partial(attend, (pb, ka, cores, sources))
    group = queries.shape[1] // kv_width
    rows = min(HEADS_AT_ONCE, group) * block_rows
    width = queries.shape[1]
    return pl.pallas_call(
        kernel,
        out_shape=jax.ShapeDtypeStruct((own_slots * block_rows, width), jnp.bfloat16),
        in_specs=[pl.BlockSpec(memory_space=pltpu.SMEM)] * 2
        + [pl.BlockSpec(memory_space=pl.ANY)] * (1 + 2 * sources),
        out_specs=pl.BlockSpec(memory_space=pltpu.VMEM),
        scratch_shapes=[
            pltpu.VMEM((own_slots * block_rows, width), jnp.bfloat16),
            pltpu.VMEM((block_total, block_rows, kv_width), jnp.bfloat16),
            pltpu.VMEM((block_total, block_rows, kv_width), jnp.bfloat16),
            pltpu.VMEM((block_total // 2, rows, block_rows), jnp.float32),
            pltpu.SMEM((own_slots, block_total + 1), jnp.int32),
            pltpu.SemaphoreType.DMA((1 + 2 * sources * class_local,)),
        ],
        compiler_params=pltpu.CompilerParams(vmem_limit_bytes=56 * 1024 * 1024),
    )(q_order, block_mask, queries, *pieces)


def solution(mesh):
    in_specs = (
        P("pb", "ha"),
        P("pb", "ka", None, "ha"),
        P("pb", "ka", None, "ha"),
        P("pb"),
        P("pb", None),
    )
    out_specs = P(("pb", "ka"), "ha")
    return jax.shard_map(
        on_device, mesh=mesh, in_specs=in_specs, out_specs=out_specs, check_vma=False
    )
```

```python
import functools
import math

import jax
import jax.numpy as jnp
from jax import lax
from jax.experimental import pallas as pl
from jax.experimental.pallas import tpu as pltpu
from jax.sharding import PartitionSpec as P

HEAD_DIM = 128
MASKED = -1e30
STAGES = 4


def shift(array, axis, size, step):
    return lax.ppermute(array, axis, [(i, (i + step) % size) for i in range(size)])


def turn(array, size, cores, ring_step, core_step):
    rings = size // cores
    pairs = []
    for ring in range(rings):
        for core in range(cores):
            to = ((ring + ring_step) % rings) * cores + (core + core_step) % cores
            pairs.append((ring * cores + core, to))
    return lax.ppermute(array, "ka", pairs)


def dot(a, b, b_dim):
    return lax.dot_general(a, b, (((1,), (b_dim,)), ((), ())), preferred_element_type=jnp.float32)


def attend_stage(plan, first, last, order_ref, mask_ref, q_ref, *refs):
    pb, ka, cores, places = plan
    count = len(places)
    keys, values = refs[:count], refs[count : 2 * count]
    refs = refs[2 * count :]
    if not first:
        old_refs, refs = refs[:3], refs[3:]
    if last:
        out_ref, refs = refs[0], refs[1:]
    acc, top, total, k_pool, v_pool, bias = refs[:6]
    own_slots, kv_local, rows, _ = acc.shape
    held, _, block_rows, _ = keys[0].shape
    group = rows // block_rows
    rings = ka // cores
    p_at, k_at = lax.axis_index("pb"), lax.axis_index("ka")
    ring_at, core_at = k_at // cores, lax.rem(k_at, cores)
    scale = math.log2(math.e) / math.sqrt(HEAD_DIM)

    blocks = []
    for hops, y, c in places:
        ring = lax.rem(ring_at + (rings - y), rings)
        core = lax.rem(core_at + (cores - c), cores)
        class_local = held // len(hops)
        for z in hops:
            source = lax.rem(p_at + (pb - z), pb)
            for t in range(class_local):
                blocks.append((source * class_local + t) * ka + ring * cores + core)

    if first:
        acc[...] = jnp.zeros(acc.shape, acc.dtype)
        total[...] = jnp.zeros(total.shape, total.dtype)
        top[...] = jnp.full(top.shape, MASKED, top.dtype)
    else:
        for new, old in zip((acc, top, total), old_refs):
            new[...] = old[...]

    row_id = lax.broadcasted_iota(jnp.int32, (block_rows, block_rows), 0)
    col_id = lax.broadcasted_iota(jnp.int32, (block_rows, block_rows), 1)

    def fill(s):
        row = k_at * own_slots + s
        own = order_ref[row]
        listed = [mask_ref[row, block] for block in blocks]
        size = functools.reduce(lambda a, b: a + b, listed)
        done = jnp.int32(0)
        has_own = jnp.int32(0)
        for at, block in enumerate(blocks):
            piece, t = at // held, at % held
            is_own = block == own
            place = jnp.where(is_own, size - 1, done)

            @pl.when(listed[at] == 1)
            def _():
                k_pool[place] = keys[piece][t, 0]
                v_pool[place] = values[piece][t, 0]

            done = done + jnp.where(is_own, 0, listed[at])
            has_own = has_own + jnp.where(is_own, listed[at], 0)

        @pl.when(lax.rem(size, 2) == 1)
        def _():
            k_pool[size] = jnp.zeros(k_pool.shape[1:], k_pool.dtype)
            v_pool[size] = jnp.zeros(v_pool.shape[1:], v_pool.dtype)

        return size, has_own

    def unit(s, size, has_own, u):
        for half in range(2):
            entry = 2 * u + half
            reach = jnp.where(entry >= size, -block_rows, block_rows)
            reach = jnp.where((entry == size - 1) & (has_own == 1), 0, reach)
            bias[:, half * block_rows : (half + 1) * block_rows] = jnp.where(
                col_id <= row_id + reach, 0.0, MASKED
            )
        for g in range(kv_local):
            columns = slice(g * HEAD_DIM, (g + 1) * HEAD_DIM)
            k_pair = jnp.concatenate(
                [k_pool[2 * u, :, columns], k_pool[2 * u + 1, :, columns]], axis=0
            )
            v_pair = jnp.concatenate(
                [v_pool[2 * u, :, columns], v_pool[2 * u + 1, :, columns]], axis=0
            )
            q_rows = jnp.concatenate(
                [
                    q_ref[
                        pl.ds(pl.multiple_of(s * block_rows, block_rows), block_rows),
                        (g * group + x) * HEAD_DIM : (g * group + x + 1) * HEAD_DIM,
                    ]
                    for x in range(group)
                ],
                axis=0,
            )
            scores = dot(q_rows, k_pair, 1)
            weights = []
            shrinks = []
            for x in range(group):
                span = slice(x * block_rows, (x + 1) * block_rows)
                score = scores[span] + bias[...]
                halves = score[:, :block_rows], score[:, block_rows:]
                peak = jnp.max(jnp.maximum(*halves), axis=1, keepdims=True)
                old = top[s, g, span]
                new = jnp.maximum(old, peak)
                top[s, g, span] = new
                shrink = jnp.exp2((old - new) * scale)
                one, two = (jnp.exp2((half - new) * scale) for half in halves)
                total[s, g, span] = total[s, g, span] * shrink + (one + two)
                weights.append(
                    jnp.concatenate([one.astype(jnp.bfloat16), two.astype(jnp.bfloat16)], axis=1)
                )
                shrinks.append(shrink)
            added = dot(jnp.concatenate(weights, axis=0), v_pair, 0)
            for x in range(group):
                span = slice(x * block_rows, (x + 1) * block_rows)
                acc[s, g, span] = acc[s, g, span] * shrinks[x] + added[span]

    for s in range(own_slots):
        size, has_own = fill(s)

        def one_unit(u, carry, s=s, size=size, has_own=has_own):
            unit(s, size, has_own, u)
            return carry

        lax.fori_loop(0, (size + 1) // 2, one_unit, 0)
        if last:
            for g in range(kv_local):
                for x in range(group):
                    span = slice(x * block_rows, (x + 1) * block_rows)
                    under = jnp.sum(total[s, g, span], axis=1, keepdims=True)
                    out_ref[
                        s * block_rows : (s + 1) * block_rows,
                        (g * group + x) * HEAD_DIM : (g * group + x + 1) * HEAD_DIM,
                    ] = (acc[s, g, span] / under).astype(out_ref.dtype)


def on_device(queries, keys, values, q_order, block_mask):
    pb, ka = lax.axis_size("pb"), lax.axis_size("ka")
    cores = 2 if ka % 2 == 0 else 1
    rings = ka // cores
    class_local, _, block_rows, kv_width = keys.shape
    kv_local = kv_width // HEAD_DIM
    width = queries.shape[1]
    group = width // kv_width
    own_slots = queries.shape[0] // block_rows // ka
    own_rows = own_slots * block_rows
    own_queries = lax.dynamic_slice_in_dim(
        queries, lax.axis_index("ka") * own_rows, own_rows, axis=0
    )

    state_shape = jax.ShapeDtypeStruct((own_slots, kv_local, group * block_rows, HEAD_DIM), jnp.float32)
    vmem = pl.BlockSpec(memory_space=pltpu.VMEM)
    smem = pl.BlockSpec(memory_space=pltpu.SMEM)
    stages = min(STAGES, pb)
    sources = pb // stages
    near = (keys, values)
    state = ()
    for stage in range(stages):
        places, pieces, nears = [], [], []
        hops = range(stage * sources, (stage + 1) * sources)
        for z in hops:
            if z:
                near = tuple(shift(array, "pb", pb, 1) for array in near)
            nears.append(near)
        ring = nears[0]
        if sources > 1:
            ring = tuple(jnp.concatenate(arrays, axis=0) for arrays in zip(*nears))
        for y in range(rings):
            if y:
                ring = tuple(turn(array, ka, cores, 1, 0) for array in ring)
            here = ring
            for c in range(cores):
                if c:
                    here = tuple(turn(array, ka, cores, 0, 1) for array in here)
                places.append((hops, y, c))
                pieces.append(here)
        first, last = stage == 0, stage == stages - 1
        held = len(places) * sources * class_local
        held += held % 2
        pools = [pltpu.VMEM((held, block_rows, kv_width), jnp.bfloat16)] * 2
        pools.append(pltpu.VMEM((block_rows, 2 * block_rows), jnp.float32))
        if last:
            outs = jax.ShapeDtypeStruct((own_rows, width), jnp.bfloat16)
            out_specs = vmem
            scratch = [pltpu.VMEM(state_shape.shape, state_shape.dtype)] * 3 + pools
        else:
            outs = (state_shape,) * 3
            out_specs = (vmem,) * 3
            scratch = pools
        state = pl.pallas_call(
            functools.partial(attend_stage, (pb, ka, cores, places), first, last),
            out_shape=outs,
            in_specs=[smem] * 2 + [vmem] * (1 + 2 * len(places) + len(state)),
            out_specs=out_specs,
            scratch_shapes=scratch,
            compiler_params=pltpu.CompilerParams(vmem_limit_bytes=40 * 1024 * 1024),
            cost_estimate=pl.CostEstimate(
                flops=2**30, bytes_accessed=2**22, transcendentals=2**20
            ),
        )(
            q_order,
            block_mask,
            own_queries,
            *[piece[0] for piece in pieces],
            *[piece[1] for piece in pieces],
            *state,
        )
    return state


def solution(mesh):
    in_specs = (
        P("pb", "ha"),
        P("pb", "ka", None, "ha"),
        P("pb", "ka", None, "ha"),
        P("pb"),
        P("pb", None),
    )
    out_specs = P(("pb", "ka"), "ha")
    return jax.shard_map(
        on_device, mesh=mesh, in_specs=in_specs, out_specs=out_specs, check_vma=False
    )
```

```python
import functools
import math

import jax
import jax.numpy as jnp
from jax import lax
from jax.experimental import pallas as pl
from jax.experimental.pallas import tpu as pltpu
from jax.sharding import PartitionSpec as P

HEAD_DIM = 128
MASKED = -1e30
STAGES = 4
REACH = 3


def shift(array, axis, size, step):
    return lax.ppermute(array, axis, [(i, (i + step) % size) for i in range(size)])


def turn(array, size, cores, ring_step, core_step):
    rings = size // cores
    pairs = []
    for ring in range(rings):
        for core in range(cores):
            to = ((ring + ring_step) % rings) * cores + (core + core_step) % cores
            pairs.append((ring * cores + core, to))
    return lax.ppermute(array, "ka", pairs)


def dot(a, b, b_dim):
    return lax.dot_general(a, b, (((1,), (b_dim,)), ((), ())), preferred_element_type=jnp.float32)


def attend_stage(plan, first, last, order_ref, mask_ref, q_in, *refs):
    pb, ka, cores, places = plan
    count = len(places)
    pieces, refs = refs[:count], refs[count:]
    if not first:
        old_refs, refs = refs[:3], refs[3:]
    if not last:
        refs = refs[1:]
    if first:
        q_ref, refs = refs[0], refs[1:]
    else:
        q_ref = q_in
    if last:
        out_ref, refs = refs[0], refs[1:]
    acc, top, total, k_pool, v_pool, bias = refs[:6]
    own_slots, kv_local, rows, _ = acc.shape
    held, block_rows, _ = pieces[0].shape
    held = held // 2
    group = rows // block_rows
    rings = ka // cores
    p_at, k_at = lax.axis_index("pb"), lax.axis_index("ka")
    ring_at, core_at = k_at // cores, lax.rem(k_at, cores)
    scale = math.log2(math.e) / math.sqrt(HEAD_DIM)

    blocks = []
    for hops, y, c in places:
        ring = lax.rem(ring_at + (rings - y), rings)
        core = lax.rem(core_at + (cores - c), cores)
        class_local = held // len(hops)
        for z in hops:
            source = lax.rem(p_at + (pb - z), pb)
            for t in range(class_local):
                blocks.append((source * class_local + t) * ka + ring * cores + core)

    if first:
        own_rows = own_slots * block_rows
        q_copy = pltpu.make_async_copy(
            q_in.at[pl.ds(pl.multiple_of(k_at * own_rows, block_rows), own_rows)], q_ref, refs[6]
        )
        q_copy.start()
        acc[...] = jnp.zeros(acc.shape, acc.dtype)
        total[...] = jnp.zeros(total.shape, total.dtype)
        top[...] = jnp.full(top.shape, MASKED, top.dtype)
    else:
        for new, old in zip((acc, top, total), old_refs):
            new[...] = old[...]

    if first:
        q_copy.wait()
    row_id = lax.broadcasted_iota(jnp.int32, (block_rows, block_rows), 0)
    col_id = lax.broadcasted_iota(jnp.int32, (block_rows, block_rows), 1)

    def fill(s):
        row = k_at * own_slots + s
        own = order_ref[row]
        listed = [mask_ref[row, block] for block in blocks]
        size = functools.reduce(lambda a, b: a + b, listed)
        done = jnp.int32(0)
        has_own = jnp.int32(0)
        for at, block in enumerate(blocks):
            piece, t = at // held, at % held
            is_own = block == own
            place = jnp.where(is_own, size - 1, done)

            @pl.when(listed[at] == 1)
            def _():
                k_pool[place] = pieces[piece][t]
                v_pool[place] = pieces[piece][held + t]

            done = done + jnp.where(is_own, 0, listed[at])
            has_own = has_own + jnp.where(is_own, listed[at], 0)

        @pl.when(lax.rem(size, 2) == 1)
        def _():
            k_pool[size] = jnp.zeros(k_pool.shape[1:], k_pool.dtype)
            v_pool[size] = jnp.zeros(v_pool.shape[1:], v_pool.dtype)

        return size, has_own

    def unit(s, size, has_own, u):
        for half in range(2):
            entry = 2 * u + half
            reach = jnp.where(entry >= size, -block_rows, block_rows)
            reach = jnp.where((entry == size - 1) & (has_own == 1), 0, reach)
            bias[:, half * block_rows : (half + 1) * block_rows] = jnp.where(
                col_id <= row_id + reach, 0.0, MASKED
            )
        for g in range(kv_local):
            columns = slice(g * HEAD_DIM, (g + 1) * HEAD_DIM)
            k_pair = jnp.concatenate(
                [k_pool[2 * u, :, columns], k_pool[2 * u + 1, :, columns]], axis=0
            )
            v_pair = jnp.concatenate(
                [v_pool[2 * u, :, columns], v_pool[2 * u + 1, :, columns]], axis=0
            )
            q_rows = jnp.concatenate(
                [
                    q_ref[
                        pl.ds(pl.multiple_of(s * block_rows, block_rows), block_rows),
                        (g * group + x) * HEAD_DIM : (g * group + x + 1) * HEAD_DIM,
                    ]
                    for x in range(group)
                ],
                axis=0,
            )
            scores = dot(q_rows, k_pair, 1)
            weights = []
            shrinks = []
            for x in range(group):
                span = slice(x * block_rows, (x + 1) * block_rows)
                score = scores[span] + bias[...]
                halves = score[:, :block_rows], score[:, block_rows:]
                peak = jnp.max(jnp.maximum(*halves), axis=1, keepdims=True)
                old = top[s, g, span]
                new = jnp.maximum(old, peak)
                top[s, g, span] = new
                shrink = jnp.exp2((old - new) * scale)
                one, two = (jnp.exp2((half - new) * scale) for half in halves)
                total[s, g, span] = total[s, g, span] * shrink + (one + two)
                weights.append(
                    jnp.concatenate([one.astype(jnp.bfloat16), two.astype(jnp.bfloat16)], axis=1)
                )
                shrinks.append(shrink)
            added = dot(jnp.concatenate(weights, axis=0), v_pair, 0)
            for x in range(group):
                span = slice(x * block_rows, (x + 1) * block_rows)
                acc[s, g, span] = acc[s, g, span] * shrinks[x] + added[span]

    for s in range(own_slots):
        size, has_own = fill(s)

        def one_unit(u, carry, s=s, size=size, has_own=has_own):
            unit(s, size, has_own, u)
            return carry

        lax.fori_loop(0, (size + 1) // 2, one_unit, 0)
        if last:
            for g in range(kv_local):
                for x in range(group):
                    span = slice(x * block_rows, (x + 1) * block_rows)
                    under = jnp.sum(total[s, g, span], axis=1, keepdims=True)
                    out_ref[
                        s * block_rows : (s + 1) * block_rows,
                        (g * group + x) * HEAD_DIM : (g * group + x + 1) * HEAD_DIM,
                    ] = (acc[s, g, span] / under).astype(out_ref.dtype)


def on_device(queries, keys, values, q_order, block_mask):
    pb, ka = lax.axis_size("pb"), lax.axis_size("ka")
    cores = 2 if ka % 2 == 0 else 1
    rings = ka // cores
    class_local, _, block_rows, kv_width = keys.shape
    kv_local = kv_width // HEAD_DIM
    width = queries.shape[1]
    group = width // kv_width
    own_slots = queries.shape[0] // block_rows // ka
    own_rows = own_slots * block_rows
    state_shape = jax.ShapeDtypeStruct((own_slots, kv_local, group * block_rows, HEAD_DIM), jnp.float32)
    vmem = pl.BlockSpec(memory_space=pltpu.VMEM)
    smem = pl.BlockSpec(memory_space=pltpu.SMEM)
    hbm = pl.BlockSpec(memory_space=pltpu.HBM)
    stages = min(STAGES, pb)
    sources = pb // stages
    q_shape = jax.ShapeDtypeStruct((own_rows, width), queries.dtype)
    own = jnp.concatenate([keys, values], axis=0)
    own = own.reshape(own.shape[0], block_rows, kv_width)
    nears = [own]
    for z in range(1, pb):
        hop = (z - 1) % REACH + 1
        nears.append(shift(nears[z - hop], "pb", pb, hop))
    rings_of = []
    for stage in range(stages):
        nears_here = nears[stage * sources : (stage + 1) * sources]
        if sources == 1:
            rings_of.append(nears_here[0])
        else:
            rings_of.append(
                jnp.concatenate(
                    [array[:class_local] for array in nears_here]
                    + [array[class_local:] for array in nears_here],
                    axis=0,
                )
            )

    state, own_queries = (), queries
    for stage in range(stages):
        hops = range(stage * sources, (stage + 1) * sources)
        places, pieces = [], []
        ring = rings_of[stage]
        for y in range(rings):
            if y:
                ring = turn(ring, ka, cores, 1, 0)
            here = ring
            for c in range(cores):
                if c:
                    here = turn(here, ka, cores, 0, 1)
                places.append((hops, y, c))
                pieces.append(here)
        first, last = stage == 0, stage == stages - 1
        ahead = [] if last else [rings_of[stage + 1]]
        held = len(places) * sources * class_local
        held += held % 2
        scratch = [pltpu.VMEM((held, block_rows, kv_width), jnp.bfloat16)] * 2
        scratch.append(pltpu.VMEM((block_rows, 2 * block_rows), jnp.float32))
        if first:
            scratch.append(pltpu.SemaphoreType.DMA)
        if last:
            outs = [q_shape]
            scratch = [pltpu.VMEM(state_shape.shape, state_shape.dtype)] * 3 + scratch
        else:
            outs = [q_shape] * first + [state_shape] * 3
        results = pl.pallas_call(
            functools.partial(attend_stage, (pb, ka, cores, places), first, last),
            out_shape=outs,
            in_specs=[smem] * 2
            + [hbm if first else vmem]
            + [vmem] * (len(places) + len(state))
            + [pl.BlockSpec(memory_space=pl.ANY)] * len(ahead),
            out_specs=[vmem] * len(outs),
            scratch_shapes=scratch,
            compiler_params=pltpu.CompilerParams(vmem_limit_bytes=20 * 1024 * 1024),
            cost_estimate=pl.CostEstimate(
                flops=2**31, bytes_accessed=2**22, transcendentals=2**20
            ),
        )(q_order, block_mask, own_queries, *pieces, *state, *ahead)
        if first:
            own_queries, results = results[0], results[1:]
        state = results
    return state[0]


def solution(mesh):
    in_specs = (
        P("pb", "ha"),
        P("pb", "ka", None, "ha"),
        P("pb", "ka", None, "ha"),
        P("pb"),
        P("pb", None),
    )
    out_specs = P(("pb", "ka"), "ha")
    return jax.shard_map(
        on_device, mesh=mesh, in_specs=in_specs, out_specs=out_specs, check_vma=False
    )
```

```python
import functools
import math

import jax
import jax.numpy as jnp
from jax import lax
from jax.experimental import pallas as pl
from jax.experimental.pallas import tpu as pltpu
from jax.sharding import PartitionSpec as P

HEAD_DIM = 128
MASKED = -1e30
STAGES = 4


def folded(size):
    return list(range(0, size, 2)) + list(range(1, size, 2))[::-1]


def along_ring(array, size):
    ring = folded(size)
    return lax.ppermute(array, "pb", [(ring[i], ring[(i + 1) % size]) for i in range(size)])


def ring_source(at, size, hops):
    place = jnp.where(at % 2 == 0, at // 2, size - 1 - at // 2)
    place = lax.rem(place + (size - hops), size)
    return jnp.where(place < (size + 1) // 2, 2 * place, 2 * (size - 1 - place) + 1)


def turn(array, size, cores, ring_step, core_step):
    rings = size // cores
    pairs = []
    for ring in range(rings):
        for core in range(cores):
            to = ((ring + ring_step) % rings) * cores + (core + core_step) % cores
            pairs.append((ring * cores + core, to))
    return lax.ppermute(array, "ka", pairs)


def dot(a, b, b_dim):
    return lax.dot_general(a, b, (((1,), (b_dim,)), ((), ())), preferred_element_type=jnp.float32)


def attend_stage(plan, first, last, table_ref, q_ref, *refs):
    pb, ka, cores, places, slots, turned = plan
    count = len(places)
    pieces, refs = refs[:count], refs[count:]
    if not first:
        old_refs, refs = refs[:3], refs[3:]
    if not last:
        refs = refs[1:]
    if last:
        out_ref, refs = refs[0], refs[1:]
    acc, top, total, k_pool, v_pool, bias = refs[:6]
    rows = acc.shape[1]
    held, block_rows, _ = pieces[0].shape
    held = held // 2
    group = rows // block_rows
    rings = ka // cores
    own_slots = slots // cores
    p_at, k_at = lax.axis_index("pb"), lax.axis_index("ka")
    ring_at, core_at = k_at // cores, lax.rem(k_at, cores)
    scale = math.log2(math.e) / math.sqrt(HEAD_DIM)

    blocks = []
    for hops, y, c in places:
        ring = lax.rem(ring_at + (rings - y), rings)
        core = lax.rem(core_at + (cores - c), cores)
        class_local = held // len(hops)
        for z in hops:
            source = ring_source(p_at, pb, z)
            for t in range(class_local):
                blocks.append((source * class_local + t) * ka + ring * cores + core)

    if first:
        acc[...] = jnp.zeros(acc.shape, acc.dtype)
        total[...] = jnp.zeros(total.shape, total.dtype)
        top[...] = jnp.full(top.shape, MASKED, top.dtype)

    row_id = lax.broadcasted_iota(jnp.int32, (block_rows, block_rows), 0)
    col_id = lax.broadcasted_iota(jnp.int32, (block_rows, block_rows), 1)

    def fill(row):
        own = table_ref[row, 0]
        listed = [table_ref[row, 1 + block] for block in blocks]
        size = functools.reduce(lambda a, b: a + b, listed)
        done = jnp.int32(0)
        has_own = jnp.int32(0)
        for at, block in enumerate(blocks):
            piece, t = at // held, at % held
            is_own = block == own
            place = jnp.where(is_own, size - 1, done)

            @pl.when(listed[at] == 1)
            def _():
                k_pool[place] = pieces[piece][t]
                v_pool[place] = pieces[piece][held + t]

            done = done + jnp.where(is_own, 0, listed[at])
            has_own = has_own + jnp.where(is_own, listed[at], 0)

        @pl.when(lax.rem(size, 2) == 1)
        def _():
            k_pool[size] = jnp.zeros(k_pool.shape[1:], k_pool.dtype)
            v_pool[size] = jnp.zeros(v_pool.shape[1:], v_pool.dtype)

        return size, has_own

    def unit(s, at, size, has_own, u):
        for half in range(2):
            entry = 2 * u + half
            reach = jnp.where(entry >= size, -block_rows, block_rows)
            reach = jnp.where((entry == size - 1) & (has_own == 1), 0, reach)
            bias[:, half * block_rows : (half + 1) * block_rows] = jnp.where(
                col_id <= row_id + reach, 0.0, MASKED
            )
        k_pair = jnp.concatenate([k_pool[2 * u], k_pool[2 * u + 1]], axis=0)
        v_pair = jnp.concatenate([v_pool[2 * u], v_pool[2 * u + 1]], axis=0)
        q_rows = jnp.concatenate(
            [
                q_ref[
                    pl.ds(pl.multiple_of(s * block_rows, block_rows), block_rows),
                    x * HEAD_DIM : (x + 1) * HEAD_DIM,
                ]
                for x in range(group)
            ],
            axis=0,
        )
        scores = dot(q_rows, k_pair, 1)
        weights = []
        shrinks = []
        for x in range(group):
            span = slice(x * block_rows, (x + 1) * block_rows)
            score = scores[span] + bias[...]
            halves = score[:, :block_rows], score[:, block_rows:]
            peak = jnp.max(jnp.maximum(*halves), axis=1, keepdims=True)
            old = top[at, span]
            new = jnp.maximum(old, peak)
            top[at, span] = new
            shrink = jnp.exp2((old - new) * scale)
            one, two = (jnp.exp2((half - new) * scale) for half in halves)
            total[at, span] = total[at, span] * shrink + (one + two)
            weights.append(
                jnp.concatenate([one.astype(jnp.bfloat16), two.astype(jnp.bfloat16)], axis=1)
            )
            shrinks.append(shrink)
        added = dot(jnp.concatenate(weights, axis=0), v_pair, 0)
        for x in range(group):
            span = slice(x * block_rows, (x + 1) * block_rows)
            acc[at, span] = acc[at, span] * shrinks[x] + added[span]

    for at in range(acc.shape[0]):
        if last:
            s = lax.rem(core_at + turned, cores) * own_slots + at
        else:
            s = at
        if not first:
            for new, old in zip((acc, top, total), old_refs):
                new[at] = old[s]
        size, has_own = fill(ring_at * slots + s)

        def one_unit(u, carry, s=s, at=at, size=size, has_own=has_own):
            unit(s, at, size, has_own, u)
            return carry

        lax.fori_loop(0, (size + 1) // 2, one_unit, 0)
        if last:
            for x in range(group):
                span = slice(x * block_rows, (x + 1) * block_rows)
                under = jnp.sum(total[at, span], axis=1, keepdims=True)
                out_ref[
                    at * block_rows : (at + 1) * block_rows, x * HEAD_DIM : (x + 1) * HEAD_DIM
                ] = (acc[at, span] / under).astype(out_ref.dtype)


def split(cores, keys_ref, values_ref, *refs):
    outs, sems = refs[:cores], refs[cores]
    count = keys_ref.shape[0]
    width = outs[0].shape[2]
    core = lax.rem(lax.axis_index("ka"), cores)
    copies = []
    for i, out in enumerate(outs):
        at = pl.multiple_of(lax.rem(core + i, cores) * width, HEAD_DIM)
        for j, ref in enumerate((keys_ref, values_ref)):
            copy = pltpu.make_async_copy(
                ref.at[:, 0, :, pl.ds(at, width)],
                out.at[pl.ds(j * count, count)],
                sems.at[2 * i + j],
            )
            copy.start()
            copies.append(copy)
    for copy in copies:
        copy.wait()


def fetch(cores, queries_ref, out_ref, sem):
    rows, width = out_ref.shape
    at = lax.axis_index("ka")
    copy = pltpu.make_async_copy(
        queries_ref.at[
            pl.ds(pl.multiple_of(at // cores * rows, HEAD_DIM), rows),
            pl.ds(pl.multiple_of(lax.rem(at, cores) * width, HEAD_DIM), width),
        ],
        out_ref,
        sem,
    )
    copy.start()
    copy.wait()


def join(cores, own_ref, other_ref, out_ref, sems):
    width = own_ref.shape[1]
    core = lax.rem(lax.axis_index("ka"), cores)
    copies = []
    for i, ref in enumerate((own_ref, other_ref)):
        at = lax.rem(core + (cores - i), cores) * width
        copy = pltpu.make_async_copy(
            ref, out_ref.at[:, pl.ds(pl.multiple_of(at, HEAD_DIM), width)], sems.at[i]
        )
        copy.start()
        copies.append(copy)
    for copy in copies:
        copy.wait()


def on_device(queries, keys, values, q_order, block_mask):
    pb, ka = lax.axis_size("pb"), lax.axis_size("ka")
    class_local, _, block_rows, kv_width = keys.shape
    cores = 2 if ka % 2 == 0 and kv_width == 2 * HEAD_DIM else 1
    rings = ka // cores
    head_width = kv_width // cores
    width = queries.shape[1] // cores
    rows = width // head_width * block_rows
    own_slots = queries.shape[0] // block_rows // ka
    slots = own_slots * cores

    vmem = pl.BlockSpec(memory_space=pltpu.VMEM)
    smem = pl.BlockSpec(memory_space=pltpu.SMEM)
    hbm = pl.BlockSpec(memory_space=pltpu.HBM)
    anywhere = pl.BlockSpec(memory_space=pl.ANY)
    stages = min(STAGES, pb)
    sources = pb // stages

    table = jnp.concatenate([q_order[:, None], block_mask], axis=1)
    part = jax.ShapeDtypeStruct((2 * class_local, block_rows, head_width), keys.dtype)
    starts = pl.pallas_call(
        functools.partial(split, cores),
        out_shape=[part] * cores,
        in_specs=[anywhere] * 2,
        out_specs=[vmem] * cores,
        scratch_shapes=[pltpu.SemaphoreType.DMA((2 * cores,))],
        compiler_params=pltpu.CompilerParams(vmem_limit_bytes=60 * 2**20),
    )(keys, values)
    if cores == 2:
        starts = [starts[0], turn(starts[1], ka, cores, 0, 1)]

    near = [starts]
    for z in range(1, pb):
        near.append([along_ring(array, pb) for array in near[-1]])
    staged = []
    for stage in range(stages):
        here = near[stage * sources : (stage + 1) * sources]
        if sources == 1:
            staged.append(here[0])
            continue
        staged.append(
            [
                jnp.concatenate(
                    [array[:class_local] for array in arrays]
                    + [array[class_local:] for array in arrays],
                    axis=0,
                )
                for arrays in zip(*here)
            ]
        )

    def call(stage, first, last, turned, pieces, places, own_queries, state, ahead):
        held = len(places) * sources * class_local
        held += held % 2
        here = own_slots if last else slots
        state_shape = jax.ShapeDtypeStruct((here, rows, HEAD_DIM), jnp.float32)
        scratch = [pltpu.VMEM((held, block_rows, HEAD_DIM), jnp.bfloat16)] * 2
        scratch.append(pltpu.VMEM((block_rows, 2 * block_rows), jnp.float32))
        if last:
            outs = [jax.ShapeDtypeStruct((own_slots * block_rows, width), queries.dtype)]
            scratch = [pltpu.VMEM(state_shape.shape, state_shape.dtype)] * 3 + scratch
        else:
            outs = [state_shape] * 3
        return pl.pallas_call(
            functools.partial(
                attend_stage, (pb, ka, cores, places, slots, turned), first, last
            ),
            out_shape=outs,
            in_specs=[smem]
            + [vmem] * (1 + len(places) + len(state))
            + [anywhere] * len(ahead),
            out_specs=[vmem] * len(outs),
            scratch_shapes=scratch,
            compiler_params=pltpu.CompilerParams(vmem_limit_bytes=20 * 2**20),
            cost_estimate=pl.CostEstimate(
                flops=2**31, bytes_accessed=2**22, transcendentals=2**20
            ),
        )(table, own_queries, *pieces, *state, *ahead)

    own_queries = pl.pallas_call(
        functools.partial(fetch, cores),
        out_shape=jax.ShapeDtypeStruct((slots * block_rows, width), queries.dtype),
        in_specs=[anywhere],
        out_specs=vmem,
        scratch_shapes=[pltpu.SemaphoreType.DMA],
        compiler_params=pltpu.CompilerParams(vmem_limit_bytes=57 * 2**20),
    )(queries)

    state = ()
    for stage in range(stages):
        hops = range(stage * sources, (stage + 1) * sources)
        places, pieces = [], []
        for c in range(cores):
            ring = staged[stage][c]
            for y in range(rings):
                if y:
                    ring = turn(ring, ka, cores, 1, 0)
                places.append((hops, y, c))
                pieces.append(ring)
        first, last = stage == 0, stage == stages - 1
        if not last:
            ahead = [staged[stage + 1][-1]]
            state = call(stage, first, last, 0, pieces, places, own_queries, state, ahead)
            continue
        halves = [
            call(stage, first, last, c, pieces, places, own_queries, state, [])[0]
            for c in range(cores)
        ]
    if cores == 1:
        return halves[0]
    return pl.pallas_call(
        functools.partial(join, cores),
        out_shape=jax.ShapeDtypeStruct((own_slots * block_rows, cores * width), queries.dtype),
        in_specs=[anywhere] * 2,
        out_specs=hbm,
        scratch_shapes=[pltpu.SemaphoreType.DMA((2,))],
    )(halves[0], turn(halves[1], ka, cores, 0, 1))


def solution(mesh):
    in_specs = (
        P("pb", "ha"),
        P("pb", "ka", None, "ha"),
        P("pb", "ka", None, "ha"),
        P("pb"),
        P("pb", None),
    )
    out_specs = P(("pb", "ka"), "ha")
    return jax.shard_map(
        on_device, mesh=mesh, in_specs=in_specs, out_specs=out_specs, check_vma=False
    )
```

```python
import functools
import math

import jax
import jax.numpy as jnp
from jax import lax
from jax.experimental import pallas as pl
from jax.experimental.pallas import tpu as pltpu
from jax.sharding import PartitionSpec as P

HEAD_DIM = 128
MASKED = -1e30
HEADROOM = 64.0
STAGES = 4


def folded(size):
    return list(range(0, size, 2)) + list(range(1, size, 2))[::-1]


def along_ring(array, size):
    ring = folded(size)
    return lax.ppermute(array, "pb", [(ring[i], ring[(i + 1) % size]) for i in range(size)])


def ring_source(at, size, hops):
    place = jnp.where(at % 2 == 0, at // 2, size - 1 - at // 2)
    place = lax.rem(place + (size - hops), size)
    return jnp.where(place < (size + 1) // 2, 2 * place, 2 * (size - 1 - place) + 1)


def turn(array, size, cores, ring_step, core_step):
    rings = size // cores
    pairs = []
    for ring in range(rings):
        for core in range(cores):
            to = ((ring + ring_step) % rings) * cores + (core + core_step) % cores
            pairs.append((ring * cores + core, to))
    return lax.ppermute(array, "ka", pairs)


def dot(a, b, b_dim):
    return lax.dot_general(a, b, (((1,), (b_dim,)), ((), ())), preferred_element_type=jnp.float32)


def attend_stage(plan, first, last, table_ref, q_ref, *refs):
    pb, ka, cores, places, earlier, slots, turned = plan
    count = len(places)
    pieces, refs = refs[:count], refs[count:]
    if not first:
        old_refs, refs = refs[:3], refs[3:]
    if not last:
        refs = refs[1:]
    if last:
        out_ref, refs = refs[0], refs[1:]
    acc, top, total, k_pool, v_pool, bias, over = refs
    rows = acc.shape[1]
    held, block_rows, _ = pieces[0].shape
    held = held // 2
    group = rows // block_rows
    rings = ka // cores
    own_slots = slots // cores
    p_at, k_at = lax.axis_index("pb"), lax.axis_index("ka")
    ring_at, core_at = k_at // cores, lax.rem(k_at, cores)
    scale = math.log2(math.e) / math.sqrt(HEAD_DIM)

    def ids(where, class_local):
        found = []
        for hops, y, c in where:
            ring = lax.rem(ring_at + (rings - y), rings)
            core = lax.rem(core_at + (cores - c), cores)
            for z in hops:
                source = ring_source(p_at, pb, z)
                for t in range(class_local):
                    found.append((source * class_local + t) * ka + ring * cores + core)
        return found

    class_local = held // len(places[0][0])
    blocks, before = ids(places, class_local), ids(earlier, class_local)

    row_id = lax.broadcasted_iota(jnp.int32, (block_rows, block_rows), 0)
    col_id = lax.broadcasted_iota(jnp.int32, (block_rows, block_rows), 1)

    def fill(row):
        own = table_ref[row, 0]
        listed = [table_ref[row, 1 + block] for block in blocks]
        size = functools.reduce(lambda a, b: a + b, listed)
        done = jnp.int32(0)
        has_own = jnp.int32(0)
        for at, block in enumerate(blocks):
            piece, t = at // held, at % held
            is_own = block == own
            place = jnp.where(is_own, size - 1, done)

            @pl.when(listed[at] == 1)
            def _():
                k_pool[place] = pieces[piece][t]
                v_pool[place] = pieces[piece][held + t]

            done = done + jnp.where(is_own, 0, listed[at])
            has_own = has_own + jnp.where(is_own, listed[at], 0)

        known = functools.reduce(
            lambda a, b: a + b, [table_ref[row, 1 + block] for block in before], jnp.int32(0)
        )
        return size, has_own, known

    def steps(step, size, has_own):
        free = size - has_own
        odd = lax.rem(free, 2)

        def pair(u, carry):
            step((2 * u, 2 * u + 1), False)
            return carry

        def single(j, carry):
            entry = free - odd + j
            reach = jnp.where((entry == size - 1) & (has_own == 1), 0, block_rows)
            bias[...] = jnp.where(col_id <= row_id + reach, 0.0, MASKED)
            step((entry,), True)
            return carry

        lax.fori_loop(0, free // 2, pair, 0)
        lax.fori_loop(0, odd + has_own, single, 0)

    def score(s, entries):
        q_rows = jnp.concatenate(
            [
                q_ref[
                    pl.ds(pl.multiple_of(s * block_rows, block_rows), block_rows),
                    x * HEAD_DIM : (x + 1) * HEAD_DIM,
                ]
                for x in range(group)
            ],
            axis=0,
        )
        return dot(q_rows, jnp.concatenate([k_pool[e] for e in entries], axis=0), 1)

    def parts(scores, x, biased):
        found = []
        for h in range(scores.shape[1] // block_rows):
            part = scores[
                x * block_rows : (x + 1) * block_rows, h * block_rows : (h + 1) * block_rows
            ]
            found.append(part + bias[...] if biased else part)
        return found

    def raise_top(s, at, entries, biased):
        scores = score(s, entries)
        for x in range(group):
            span = slice(x * block_rows, (x + 1) * block_rows)
            top[at, span] = functools.reduce(
                jnp.maximum, parts(scores, x, biased), top[at, span]
            )

    def take(s, at, entries, biased):
        scores = score(s, entries)
        weights = []
        highest = over[...]
        for x in range(group):
            span = slice(x * block_rows, (x + 1) * block_rows)
            shift = top[at, span] * scale
            row = []
            for part in parts(scores, x, biased):
                power = part * scale - shift
                for i in range(0, block_rows, 8):
                    highest = jnp.maximum(highest, power[i : i + 8])
                row.append(jnp.exp2(power))
            total[at, span] = functools.reduce(lambda a, b: a + b, row, total[at, span])
            weights.append(jnp.concatenate([w.astype(jnp.bfloat16) for w in row], axis=1))
        over[...] = highest
        acc[at] += dot(
            jnp.concatenate(weights, axis=0),
            jnp.concatenate([v_pool[e] for e in entries], axis=0),
            0,
        )

    def settle(s, at, size, has_own):
        if first:
            top[at] = jnp.full(top.shape[1:], MASKED, top.dtype)
        else:
            top[at] = old_refs[1][s]
        steps(functools.partial(raise_top, s, at), size, has_own)
        for x in range(group):
            span = slice(x * block_rows, (x + 1) * block_rows)
            peak = jnp.max(top[at, span], axis=1, keepdims=True)
            new = jnp.broadcast_to(peak, (block_rows, HEAD_DIM))
            top[at, span] = new
            if first:
                acc[at, span] = jnp.zeros_like(new)
                total[at, span] = jnp.zeros_like(new)
            else:
                shrink = jnp.exp2((old_refs[1][s, span] - new) * scale)
                acc[at, span] = old_refs[0][s, span] * shrink
                total[at, span] = old_refs[2][s, span] * shrink

    def one_slot(at, carry):
        s = lax.rem(core_at + turned, cores) * own_slots + at if last else at
        size, has_own, known = fill(ring_at * slots + s)

        def attempt(need):
            if first:
                settle(s, at, size, has_own)
            else:

                @pl.when(need)
                def _():
                    settle(s, at, size, has_own)

                @pl.when(jnp.logical_not(need))
                def _():
                    for new, old in zip((acc, top, total), old_refs):
                        new[at] = old[s]

            over[...] = jnp.full(over.shape, MASKED, over.dtype)
            steps(functools.partial(take, s, at), size, has_own)

        def again(state):
            need, _ = state
            attempt(need)
            passed = jnp.logical_not(need) & (jnp.max(over[...]) > HEADROOM)
            return passed, passed

        if first:
            attempt(True)
        else:
            lax.while_loop(lambda state: state[1], again, ((known == 0) & (size > 0), True))
        if last:
            for x in range(group):
                span = slice(x * block_rows, (x + 1) * block_rows)
                under = 1.0 / jnp.sum(total[at, span], axis=1, keepdims=True)
                out_ref[
                    pl.ds(pl.multiple_of(at * block_rows, block_rows), block_rows),
                    x * HEAD_DIM : (x + 1) * HEAD_DIM,
                ] = (acc[at, span] * under).astype(out_ref.dtype)
        return carry

    lax.fori_loop(0, acc.shape[0], one_slot, 0)


def split(cores, keys_ref, values_ref, *refs):
    outs, sems = refs[:cores], refs[cores]
    count = keys_ref.shape[0]
    width = outs[0].shape[2]
    core = lax.rem(lax.axis_index("ka"), cores)
    copies = []
    for i, out in enumerate(outs):
        column = pl.multiple_of(lax.rem(core + i, cores) * width, HEAD_DIM)
        for j, ref in enumerate((keys_ref, values_ref)):
            copy = pltpu.make_async_copy(
                ref.at[:, 0, :, pl.ds(column, width)],
                out.at[pl.ds(j * count, count)],
                sems.at[2 * i + j],
            )
            copy.start()
            copies.append(copy)
    for copy in copies:
        copy.wait()


def fetch(cores, queries_ref, out_ref, sem):
    rows, width = out_ref.shape
    at = lax.axis_index("ka")
    copy = pltpu.make_async_copy(
        queries_ref.at[
            pl.ds(pl.multiple_of(at // cores * rows, HEAD_DIM), rows),
            pl.ds(pl.multiple_of(lax.rem(at, cores) * width, HEAD_DIM), width),
        ],
        out_ref,
        sem,
    )
    copy.start()
    copy.wait()


def join(cores, own_ref, other_ref, out_ref, sems):
    width = own_ref.shape[1]
    core = lax.rem(lax.axis_index("ka"), cores)
    copies = []
    for i, ref in enumerate((own_ref, other_ref)):
        at = lax.rem(core + (cores - i), cores) * width
        copy = pltpu.make_async_copy(
            ref, out_ref.at[:, pl.ds(pl.multiple_of(at, HEAD_DIM), width)], sems.at[i]
        )
        copy.start()
        copies.append(copy)
    for copy in copies:
        copy.wait()


def on_device(queries, keys, values, q_order, block_mask):
    pb, ka = lax.axis_size("pb"), lax.axis_size("ka")
    class_local, _, block_rows, kv_width = keys.shape
    cores = 2 if ka % 2 == 0 and kv_width == 2 * HEAD_DIM else 1
    rings = ka // cores
    head_width = kv_width // cores
    width = queries.shape[1] // cores
    rows = width // head_width * block_rows
    own_slots = queries.shape[0] // block_rows // ka
    slots = own_slots * cores

    vmem = pl.BlockSpec(memory_space=pltpu.VMEM)
    smem = pl.BlockSpec(memory_space=pltpu.SMEM)
    hbm = pl.BlockSpec(memory_space=pltpu.HBM)
    anywhere = pl.BlockSpec(memory_space=pl.ANY)
    stages = min(STAGES, pb)
    sources = pb // stages

    table = jnp.concatenate([q_order[:, None], block_mask], axis=1)
    part = jax.ShapeDtypeStruct((2 * class_local, block_rows, head_width), keys.dtype)
    starts = pl.pallas_call(
        functools.partial(split, cores),
        out_shape=[part] * cores,
        in_specs=[anywhere] * 2,
        out_specs=[vmem] * cores,
        scratch_shapes=[pltpu.SemaphoreType.DMA((2 * cores,))],
        compiler_params=pltpu.CompilerParams(vmem_limit_bytes=54 * 2**20),
    )(keys, values)
    own_queries = pl.pallas_call(
        functools.partial(fetch, cores),
        out_shape=jax.ShapeDtypeStruct((slots * block_rows, width), queries.dtype),
        in_specs=[anywhere],
        out_specs=vmem,
        scratch_shapes=[pltpu.SemaphoreType.DMA],
        compiler_params=pltpu.CompilerParams(vmem_limit_bytes=50 * 2**20),
    )(queries)
    if cores == 2:
        starts = [starts[0], turn(starts[1], ka, cores, 0, 1)]

    near = [starts]
    for z in range(1, pb):
        near.append([along_ring(array, pb) for array in near[-1]])
    staged = []
    for stage in range(stages):
        here = near[stage * sources : (stage + 1) * sources]
        if sources == 1:
            staged.append(here[0])
            continue
        staged.append(
            [
                jnp.concatenate(
                    [array[:class_local] for array in arrays]
                    + [array[class_local:] for array in arrays],
                    axis=0,
                )
                for arrays in zip(*here)
            ]
        )

    def call(first, last, turned, pieces, places, earlier, own_queries, state, ahead):
        held = len(places) * sources * class_local
        held += held % 2
        here = own_slots if last else slots
        state_shape = jax.ShapeDtypeStruct((here, rows, HEAD_DIM), jnp.float32)
        scratch = [pltpu.VMEM((held, block_rows, HEAD_DIM), jnp.bfloat16)] * 2
        scratch.append(pltpu.VMEM((block_rows, block_rows), jnp.float32))
        scratch.append(pltpu.VMEM((8, block_rows), jnp.float32))
        if last:
            outs = [jax.ShapeDtypeStruct((own_slots * block_rows, width), queries.dtype)]
            scratch = [pltpu.VMEM(state_shape.shape, state_shape.dtype)] * 3 + scratch
        else:
            outs = [state_shape] * 3
        return pl.pallas_call(
            functools.partial(
                attend_stage, (pb, ka, cores, places, earlier, slots, turned), first, last
            ),
            out_shape=outs,
            in_specs=[smem]
            + [vmem] * (1 + len(places) + len(state))
            + [anywhere] * len(ahead),
            out_specs=[vmem] * len(outs),
            scratch_shapes=scratch,
            compiler_params=pltpu.CompilerParams(vmem_limit_bytes=20 * 2**20),
            cost_estimate=pl.CostEstimate(
                flops=2**31, bytes_accessed=2**22, transcendentals=2**20
            ),
        )(table, own_queries, *pieces, *state, *ahead)

    state, earlier = (), []
    for stage in range(stages):
        hops = range(stage * sources, (stage + 1) * sources)
        places, pieces = [], []
        for c in range(cores):
            ring = staged[stage][c]
            for y in range(rings):
                if y:
                    ring = turn(ring, ka, cores, 1, 0)
                places.append((hops, y, c))
                pieces.append(ring)
        first, last = stage == 0, stage == stages - 1
        if not last:
            ahead = [staged[stage + 1][-1]]
            state = call(first, last, 0, pieces, places, earlier, own_queries, state, ahead)
            earlier = earlier + places
            continue
        halves = [
            call(first, last, c, pieces, places, earlier, own_queries, state, [])[0]
            for c in range(cores)
        ]
    if cores == 1:
        return halves[0]
    return pl.pallas_call(
        functools.partial(join, cores),
        out_shape=jax.ShapeDtypeStruct((own_slots * block_rows, cores * width), queries.dtype),
        in_specs=[vmem] * 2,
        out_specs=hbm,
        scratch_shapes=[pltpu.SemaphoreType.DMA((2,))],
    )(halves[0], turn(halves[1], ka, cores, 0, 1))


def solution(mesh):
    in_specs = (
        P("pb", "ha"),
        P("pb", "ka", None, "ha"),
        P("pb", "ka", None, "ha"),
        P("pb"),
        P("pb", None),
    )
    out_specs = P(("pb", "ka"), "ha")
    return jax.shard_map(
        on_device, mesh=mesh, in_specs=in_specs, out_specs=out_specs, check_vma=False
    )
```

```python
import functools
import math

import jax
import jax.numpy as jnp
from jax import lax
from jax.experimental import pallas as pl
from jax.experimental.pallas import tpu as pltpu
from jax.sharding import PartitionSpec as P

HEAD_DIM = 128
MASKED = -1e30
HIDDEN = -1e38
HEADROOM = 64.0
FREE, OWN, NONE = 0, 1, 2
STAGES = 4


def folded(size):
    return list(range(0, size, 2)) + list(range(1, size, 2))[::-1]


def along_ring(array, size):
    ring = folded(size)
    return lax.ppermute(array, "pb", [(ring[i], ring[(i + 1) % size]) for i in range(size)])


def ring_source(at, size, hops):
    place = jnp.where(at % 2 == 0, at // 2, size - 1 - at // 2)
    place = lax.rem(place + (size - hops), size)
    return jnp.where(place < (size + 1) // 2, 2 * place, 2 * (size - 1 - place) + 1)


def turn(array, size, cores, ring_step, core_step):
    rings = size // cores
    pairs = []
    for ring in range(rings):
        for core in range(cores):
            to = ((ring + ring_step) % rings) * cores + (core + core_step) % cores
            pairs.append((ring * cores + core, to))
    return lax.ppermute(array, "ka", pairs)


def dot(a, b, b_dim):
    return lax.dot_general(a, b, (((1,), (b_dim,)), ((), ())), preferred_element_type=jnp.float32)


def attend_stage(plan, first, last, table_ref, q_ref, *refs):
    pb, ka, cores, places, earlier, slots, turned = plan
    count = len(places)
    pieces, refs = refs[:count], refs[count:]
    if last:
        old_pieces, refs = refs[: len(earlier)], refs[len(earlier) :]
    else:
        refs = refs[1:]
    if not first:
        refs = refs[3:]
    acc, total, over, refs = *refs[:3], refs[3:]
    if last:
        out_ref, refs = refs[0], refs[1:]
    k_pool, v_pool, bias, entries, units, refs = *refs[:5], refs[5:]
    rows = acc.shape[1]
    held, block_rows, _ = pieces[0].shape
    held = held // 2
    group = rows // block_rows
    rings = ka // cores
    own_slots = slots // cores
    p_at, k_at = lax.axis_index("pb"), lax.axis_index("ka")
    ring_at, core_at = k_at // cores, lax.rem(k_at, cores)
    scale = math.log2(math.e) / math.sqrt(HEAD_DIM)
    class_local = held // len(places[0][0])

    def ids(where):
        found = []
        for hops, y, c in where:
            ring = lax.rem(ring_at + (rings - y), rings)
            core = lax.rem(core_at + (cores - c), cores)
            for z in hops:
                source = ring_source(p_at, pb, z)
                for t in range(class_local):
                    found.append((source * class_local + t) * ka + ring * cores + core)
        return found

    def pool_from(refs_in, at, k_out, v_out):
        for i, piece in enumerate(refs_in):
            k_out[at + i * held : at + (i + 1) * held] = piece[:held]
            v_out[at + i * held : at + (i + 1) * held] = piece[held:]

    if last:
        mine = lax.rem(core_at + turned, cores) * own_slots
        slot_ids = [mine + i for i in range(own_slots)]
    else:
        slot_ids = list(range(slots))

    row_id = lax.broadcasted_iota(jnp.int32, (block_rows, block_rows), 0)
    col_id = lax.broadcasted_iota(jnp.int32, (block_rows, block_rows), 1)
    bias[FREE] = jnp.zeros((block_rows, block_rows), jnp.float32)
    bias[OWN] = jnp.where(col_id <= row_id, 0.0, HIDDEN)
    bias[NONE] = jnp.full((block_rows, block_rows), HIDDEN, jnp.float32)
    pool_from(pieces, 0, k_pool, v_pool)
    if first:
        acc[...] = jnp.zeros(acc.shape, acc.dtype)
        total[...] = jnp.zeros(total.shape, total.dtype)
        over[...] = jnp.full(over.shape, MASKED, over.dtype)

    def put(place, index, kind):
        entries[place, 0] = index
        entries[place, 1] = kind

    blocks = ids(places)
    unit_count = jnp.int32(0)
    for s in slot_ids:
        row = ring_at * slots + s
        own = table_ref[row, 0]
        place = 2 * unit_count
        for index, block in enumerate(blocks):
            put(place, index, jnp.where(block == own, OWN, FREE))
            place = place + table_ref[row, 1 + block]
        put(place, 0, NONE)
        ends = lax.div(place + 1, 2)

        def mark(u, carry, s=s):
            units[u] = s
            return carry

        lax.fori_loop(unit_count, ends, mark, 0)
        unit_count = ends
    put(2 * unit_count, 0, NONE)
    put(2 * unit_count + 1, 0, NONE)
    units[unit_count] = slot_ids[0]

    def query_rows(s):
        return jnp.concatenate(
            [
                q_ref[
                    pl.ds(pl.multiple_of(s * block_rows, block_rows), block_rows),
                    x * HEAD_DIM : (x + 1) * HEAD_DIM,
                ]
                for x in range(group)
            ],
            axis=0,
        )

    def unit_weights(u, highest):
        s = units[u]
        index = [entries[2 * u + half, 0] for half in range(2)]
        kind = [entries[2 * u + half, 1] for half in range(2)]
        scores = dot(query_rows(s), jnp.concatenate([k_pool[i] for i in index], axis=0), 1)
        weights, sums = [], []
        for x in range(group):
            row = []
            for half in range(2):
                power = (
                    scores[
                        x * block_rows : (x + 1) * block_rows,
                        half * block_rows : (half + 1) * block_rows,
                    ]
                    * scale
                    + bias[kind[half]]
                )
                tops = [power[i : i + 8] for i in range(0, block_rows, 8)]
                while len(tops) > 1:
                    tops = [jnp.maximum(*tops[i : i + 2]) for i in range(0, len(tops), 2)]
                highest = jnp.maximum(highest, tops[0])
                row.append(jnp.exp2(power))
            sums.append(row[0] + row[1])
            weights.append(jnp.concatenate([w.astype(jnp.bfloat16) for w in row], axis=1))
        added = dot(
            jnp.concatenate(weights, axis=0),
            jnp.concatenate([v_pool[i] for i in index], axis=0),
            0,
        )
        return s, jnp.concatenate(sums, axis=0), added, highest

    def two_units(i, carry):
        highest = over[...]
        done = []
        for j in range(2):
            s, sums, added, highest = unit_weights(2 * i + j, highest)
            done.append((s, sums, added))
        for s, sums, added in done:
            total[s] += sums
            acc[s] += added
        over[...] = highest
        return carry

    lax.fori_loop(0, lax.div(unit_count + 1, 2), two_units, 0)
    if not last:
        return

    out_buf, top, k_all, v_all, sems = refs

    def finish(s, i):
        least = jnp.full((block_rows, 1), 1.0, jnp.float32)
        for x in range(group):
            span = slice(x * block_rows, (x + 1) * block_rows)
            under = jnp.sum(total[s, span], axis=1, keepdims=True)
            least = jnp.minimum(least, under)
            out_buf[
                i * block_rows : (i + 1) * block_rows, x * HEAD_DIM : (x + 1) * HEAD_DIM
            ] = (acc[s, span] * (1.0 / under)).astype(out_buf.dtype)
        return least

    least = [finish(s, i) for i, s in enumerate(slot_ids)]
    unsafe = (jnp.max(over[...]) > HEADROOM) | (
        jnp.min(functools.reduce(jnp.minimum, least)) < 2.0**-HEADROOM
    )

    @pl.when(unsafe)
    def _():
        pool_from(old_pieces, 0, k_all, v_all)
        pool_from(pieces, len(earlier) * held, k_all, v_all)
        blocks_all = ids(earlier) + blocks
        for i, s in enumerate(slot_ids):
            row = ring_at * slots + s
            own = table_ref[row, 0]
            place = jnp.int32(0)
            for index, block in enumerate(blocks_all):
                put(place, index, jnp.where(block == own, OWN, FREE))
                place = place + table_ref[row, 1 + block]
            acc[s] = jnp.zeros(acc.shape[1:], acc.dtype)
            total[s] = jnp.zeros(total.shape[1:], total.dtype)
            top[...] = jnp.full(top.shape, MASKED, top.dtype)

            def one_block(e, carry, s=s):
                scores = dot(query_rows(s), k_all[entries[e, 0]], 1)
                weights, shrinks = [], []
                for x in range(group):
                    span = slice(x * block_rows, (x + 1) * block_rows)
                    power = scores[span] * scale + bias[entries[e, 1]]
                    new = jnp.maximum(top[span], jnp.max(power, axis=1, keepdims=True))
                    shrink = jnp.exp2(top[span] - new)
                    top[span] = new
                    weight = jnp.exp2(power - new)
                    total[s, span] = total[s, span] * shrink + weight
                    weights.append(weight.astype(jnp.bfloat16))
                    shrinks.append(shrink)
                added = dot(jnp.concatenate(weights, axis=0), v_all[entries[e, 0]], 0)
                acc[s] = acc[s] * jnp.concatenate(shrinks, axis=0) + added
                return carry

            lax.fori_loop(0, place, one_block, 0)
            finish(s, i)

    if turned == 0 and cores > 1:
        width = out_buf.shape[1]
        copy = pltpu.make_async_copy(
            out_buf, out_ref.at[:, pl.ds(pl.multiple_of(core_at * width, HEAD_DIM), width)], sems
        )
        copy.start()
        copy.wait()
    else:
        out_ref[...] = out_buf[...]


def split(cores, keys_ref, values_ref, *refs):
    outs, sems = refs[:cores], refs[cores]
    count = keys_ref.shape[0]
    width = outs[0].shape[2]
    core = lax.rem(lax.axis_index("ka"), cores)
    copies = []
    for i, out in enumerate(outs):
        column = pl.multiple_of(lax.rem(core + i, cores) * width, HEAD_DIM)
        for j, ref in enumerate((keys_ref, values_ref)):
            copy = pltpu.make_async_copy(
                ref.at[:, 0, :, pl.ds(column, width)],
                out.at[pl.ds(j * count, count)],
                sems.at[2 * i + j],
            )
            copy.start()
            copies.append(copy)
    for copy in copies:
        copy.wait()


def fetch(cores, queries_ref, out_ref, sem):
    rows, width = out_ref.shape
    at = lax.axis_index("ka")
    copy = pltpu.make_async_copy(
        queries_ref.at[
            pl.ds(pl.multiple_of(at // cores * rows, HEAD_DIM), rows),
            pl.ds(pl.multiple_of(lax.rem(at, cores) * width, HEAD_DIM), width),
        ],
        out_ref,
        sem,
    )
    copy.start()
    copy.wait()


def join(cores, other_ref, half_ref, out_ref, sem):
    width = other_ref.shape[1]
    at = lax.rem(lax.axis_index("ka") + 1, cores) * width
    copy = pltpu.make_async_copy(
        other_ref, out_ref.at[:, pl.ds(pl.multiple_of(at, HEAD_DIM), width)], sem
    )
    copy.start()
    copy.wait()


def on_device(queries, keys, values, q_order, block_mask):
    pb, ka = lax.axis_size("pb"), lax.axis_size("ka")
    class_local, _, block_rows, kv_width = keys.shape
    cores = 2 if ka % 2 == 0 and kv_width == 2 * HEAD_DIM else 1
    rings = ka // cores
    head_width = kv_width // cores
    width = queries.shape[1] // cores
    rows = width // head_width * block_rows
    own_slots = queries.shape[0] // block_rows // ka
    slots = own_slots * cores

    vmem = pl.BlockSpec(memory_space=pltpu.VMEM)
    smem = pl.BlockSpec(memory_space=pltpu.SMEM)
    hbm = pl.BlockSpec(memory_space=pltpu.HBM)
    anywhere = pl.BlockSpec(memory_space=pl.ANY)
    stages = min(STAGES, pb)
    sources = pb // stages

    table = jnp.concatenate([q_order[:, None], block_mask], axis=1)
    part = jax.ShapeDtypeStruct((2 * class_local, block_rows, head_width), keys.dtype)
    starts = pl.pallas_call(
        functools.partial(split, cores),
        out_shape=[part] * cores,
        in_specs=[anywhere] * 2,
        out_specs=[vmem] * cores,
        scratch_shapes=[pltpu.SemaphoreType.DMA((2 * cores,))],
        compiler_params=pltpu.CompilerParams(vmem_limit_bytes=54 * 2**20),
    )(keys, values)
    own_queries = pl.pallas_call(
        functools.partial(fetch, cores),
        out_shape=jax.ShapeDtypeStruct((slots * block_rows, width), queries.dtype),
        in_specs=[anywhere],
        out_specs=vmem,
        scratch_shapes=[pltpu.SemaphoreType.DMA],
        compiler_params=pltpu.CompilerParams(vmem_limit_bytes=50 * 2**20),
    )(queries)
    if cores == 2:
        starts = [starts[0], turn(starts[1], ka, cores, 0, 1)]

    near = [starts]
    for z in range(1, pb):
        near.append([along_ring(array, pb) for array in near[-1]])
    staged = []
    for stage in range(stages):
        here = near[stage * sources : (stage + 1) * sources]
        if sources == 1:
            staged.append(here[0])
            continue
        staged.append(
            [
                jnp.concatenate(
                    [array[:class_local] for array in arrays]
                    + [array[class_local:] for array in arrays],
                    axis=0,
                )
                for arrays in zip(*here)
            ]
        )

    def call(first, last, turned, pieces, places, earlier, own_queries, state, extra):
        held = len(places) * sources * class_local
        everything = held + len(earlier) * sources * class_local
        sums = jax.ShapeDtypeStruct((slots, rows, HEAD_DIM), jnp.float32)
        outs = [sums, sums, jax.ShapeDtypeStruct((8, block_rows), jnp.float32)]
        out_specs = [vmem] * 3
        here = own_slots if last else slots
        scratch = [pltpu.VMEM((held, block_rows, HEAD_DIM), jnp.bfloat16)] * 2
        scratch += [
            pltpu.VMEM((3, block_rows, block_rows), jnp.float32),
            pltpu.SMEM((max(here * (held + 1) + 2, everything + 1), 2), jnp.int32),
            pltpu.SMEM((here * (held // 2 + 1) + 1,), jnp.int32),
        ]
        if last:
            whole = turned == 0 and cores > 1
            half = (own_slots * block_rows, width)
            outs.append(
                jax.ShapeDtypeStruct((half[0], cores * width if whole else width), queries.dtype)
            )
            out_specs.append(hbm if whole else vmem)
            scratch += [
                pltpu.VMEM(half, queries.dtype),
                pltpu.VMEM((rows, HEAD_DIM), jnp.float32),
                pltpu.VMEM((everything, block_rows, HEAD_DIM), jnp.bfloat16),
                pltpu.VMEM((everything, block_rows, HEAD_DIM), jnp.bfloat16),
                pltpu.SemaphoreType.DMA,
            ]
        state_at = 2 + len(places) + len(extra)
        return pl.pallas_call(
            functools.partial(
                attend_stage, (pb, ka, cores, places, earlier, slots, turned), first, last
            ),
            out_shape=outs,
            in_specs=[smem]
            + [vmem] * (1 + len(places))
            + [vmem if last else anywhere] * len(extra)
            + [vmem] * len(state),
            out_specs=out_specs,
            input_output_aliases={state_at + i: i for i in range(len(state))},
            scratch_shapes=scratch,
            compiler_params=pltpu.CompilerParams(vmem_limit_bytes=24 * 2**20),
            cost_estimate=pl.CostEstimate(
                flops=2**31, bytes_accessed=2**22, transcendentals=2**20
            ),
        )(table, own_queries, *pieces, *extra, *state)

    state, earlier, before = [], [], []
    for stage in range(stages):
        hops = range(stage * sources, (stage + 1) * sources)
        places, pieces = [], []
        for c in range(cores):
            ring = staged[stage][c]
            for y in range(rings):
                if y:
                    ring = turn(ring, ka, cores, 1, 0)
                places.append((hops, y, c))
                pieces.append(ring)
        first, last = stage == 0, stage == stages - 1
        if not last:
            ahead = [staged[stage + 1][-1]]
            state = call(first, last, 0, pieces, places, earlier, own_queries, state, ahead)
            earlier, before = earlier + places, before + pieces
    halves = []
    for c in reversed(range(cores)):
        *state, half = call(False, True, c, pieces, places, earlier, own_queries, state, before)
        halves.append(half)
    if cores == 1:
        return halves[0]
    return pl.pallas_call(
        functools.partial(join, cores),
        out_shape=jax.ShapeDtypeStruct((own_slots * block_rows, cores * width), queries.dtype),
        in_specs=[vmem, anywhere],
        out_specs=anywhere,
        input_output_aliases={1: 0},
        scratch_shapes=[pltpu.SemaphoreType.DMA],
    )(turn(halves[0], ka, cores, 0, 1), halves[1])


def solution(mesh):
    in_specs = (
        P("pb", "ha"),
        P("pb", "ka", None, "ha"),
        P("pb", "ka", None, "ha"),
        P("pb"),
        P("pb", None),
    )
    out_specs = P(("pb", "ka"), "ha")
    return jax.shard_map(
        on_device, mesh=mesh, in_specs=in_specs, out_specs=out_specs, check_vma=False
    )
```

```python
import functools
import math

import jax
import jax.numpy as jnp
from jax import lax
from jax.experimental import pallas as pl
from jax.experimental.pallas import tpu as pltpu
from jax.sharding import PartitionSpec as P

HEAD_DIM = 128
MASKED = -1e30
HIDDEN = -1e38
HEADROOM = 64.0
FREE, OWN, NONE = 0, 1, 2
STAGES = 4


def folded(size):
    return list(range(0, size, 2)) + list(range(1, size, 2))[::-1]


def along_ring(array, size):
    ring = folded(size)
    return lax.ppermute(array, "pb", [(ring[i], ring[(i + 1) % size]) for i in range(size)])


def ring_source(at, size, hops):
    place = jnp.where(at % 2 == 0, at // 2, size - 1 - at // 2)
    place = lax.rem(place + (size - hops), size)
    return jnp.where(place < (size + 1) // 2, 2 * place, 2 * (size - 1 - place) + 1)


def turn(array, size, cores, ring_step, core_step):
    rings = size // cores
    pairs = []
    for ring in range(rings):
        for core in range(cores):
            to = ((ring + ring_step) % rings) * cores + (core + core_step) % cores
            pairs.append((ring * cores + core, to))
    return lax.ppermute(array, "ka", pairs)


def dot(a, b, b_dim):
    return lax.dot_general(a, b, (((1,), (b_dim,)), ((), ())), preferred_element_type=jnp.float32)


def attend_stage(plan, first, last, table_ref, q_ref, *refs):
    pb, ka, cores, places, earlier, slots, turned = plan
    count = len(places)
    pieces, refs = refs[:count], refs[count:]
    if last:
        old_pieces, refs = refs[: len(earlier)], refs[len(earlier) :]
    else:
        refs = refs[1:]
    if not first:
        refs = refs[3:]
    acc, total, over, refs = *refs[:3], refs[3:]
    if last:
        out_ref, refs = refs[0], refs[1:]
    k_pool, v_pool, bias, entries, units, refs = *refs[:5], refs[5:]
    rows = acc.shape[1]
    held, block_rows, _ = pieces[0].shape
    held = held // 2
    group = rows // block_rows
    rings = ka // cores
    own_slots = slots // cores
    p_at, k_at = lax.axis_index("pb"), lax.axis_index("ka")
    ring_at, core_at = k_at // cores, lax.rem(k_at, cores)
    scale = math.log2(math.e) / math.sqrt(HEAD_DIM)
    class_local = held // len(places[0][0])

    def ids(where):
        found = []
        for hops, y, c in where:
            ring = lax.rem(ring_at + (rings - y), rings)
            core = lax.rem(core_at + (cores - c), cores)
            for z in hops:
                source = ring_source(p_at, pb, z)
                for t in range(class_local):
                    found.append((source * class_local + t) * ka + ring * cores + core)
        return found

    def pool_from(refs_in, at, k_out, v_out):
        for i, piece in enumerate(refs_in):
            k_out[at + i * held : at + (i + 1) * held] = piece[:held]
            v_out[at + i * held : at + (i + 1) * held] = piece[held:]

    if last:
        mine = lax.rem(core_at + turned, cores) * own_slots
        slot_ids = [mine + i for i in range(own_slots)]
    else:
        slot_ids = list(range(slots))

    row_id = lax.broadcasted_iota(jnp.int32, (block_rows, block_rows), 0)
    col_id = lax.broadcasted_iota(jnp.int32, (block_rows, block_rows), 1)
    bias[FREE] = jnp.zeros((block_rows, block_rows), jnp.float32)
    bias[OWN] = jnp.where(col_id <= row_id, 0.0, HIDDEN)
    bias[NONE] = jnp.full((block_rows, block_rows), HIDDEN, jnp.float32)
    pool_from(pieces, 0, k_pool, v_pool)
    if first:
        acc[...] = jnp.zeros(acc.shape, acc.dtype)
        total[...] = jnp.zeros(total.shape, total.dtype)
        over[...] = jnp.full(over.shape, MASKED, over.dtype)

    def put(place, index, kind):
        entries[place, 0] = index
        entries[place, 1] = kind

    blocks = ids(places)
    unit_count = jnp.int32(0)
    for s in slot_ids:
        row = ring_at * slots + s
        own = table_ref[row, 0]
        place = 2 * unit_count
        for index, block in enumerate(blocks):
            put(place, index, jnp.where(block == own, OWN, FREE))
            place = place + table_ref[row, 1 + block]
        put(place, 0, NONE)
        ends = lax.div(place + 1, 2)

        def mark(u, carry, s=s):
            units[u] = s
            return carry

        lax.fori_loop(unit_count, ends, mark, 0)
        unit_count = ends
    put(2 * unit_count, 0, NONE)
    put(2 * unit_count + 1, 0, NONE)
    units[unit_count] = slot_ids[0]

    def query_rows(s):
        return jnp.concatenate(
            [
                q_ref[
                    pl.ds(pl.multiple_of(s * block_rows, block_rows), block_rows),
                    x * HEAD_DIM : (x + 1) * HEAD_DIM,
                ]
                for x in range(group)
            ],
            axis=0,
        )

    def unit_weights(u, highest):
        s = units[u]
        index = [entries[2 * u + half, 0] for half in range(2)]
        kind = [entries[2 * u + half, 1] for half in range(2)]
        scores = dot(query_rows(s), jnp.concatenate([k_pool[i] for i in index], axis=0), 1)
        weights, sums = [], []
        for x in range(group):
            row = []
            for half in range(2):
                power = (
                    scores[
                        x * block_rows : (x + 1) * block_rows,
                        half * block_rows : (half + 1) * block_rows,
                    ]
                    * scale
                    + bias[kind[half]]
                )
                tops = [power[i : i + 8] for i in range(0, block_rows, 8)]
                while len(tops) > 1:
                    tops = [jnp.maximum(*tops[i : i + 2]) for i in range(0, len(tops), 2)]
                highest = jnp.maximum(highest, tops[0])
                row.append(jnp.exp2(power))
            sums.append(row[0] + row[1])
            weights.append(jnp.concatenate([w.astype(jnp.bfloat16) for w in row], axis=1))
        added = dot(
            jnp.concatenate(weights, axis=0),
            jnp.concatenate([v_pool[i] for i in index], axis=0),
            0,
        )
        return s, jnp.concatenate(sums, axis=0), added, highest

    def two_units(i, carry):
        highest = over[...]
        done = []
        for j in range(2):
            s, sums, added, highest = unit_weights(2 * i + j, highest)
            done.append((s, sums, added))
        for s, sums, added in done:
            total[s] += sums
            acc[s] += added
        over[...] = highest
        return carry

    lax.fori_loop(0, lax.div(unit_count + 1, 2), two_units, 0)
    if not last:
        return

    out_buf, top, k_all, v_all, sems = refs

    def finish(s, i):
        least = jnp.full((block_rows, 1), 1.0, jnp.float32)
        for x in range(group):
            span = slice(x * block_rows, (x + 1) * block_rows)
            under = jnp.sum(total[s, span], axis=1, keepdims=True)
            least = jnp.minimum(least, under)
            out_buf[
                i * block_rows : (i + 1) * block_rows, x * HEAD_DIM : (x + 1) * HEAD_DIM
            ] = (acc[s, span] * (1.0 / under)).astype(out_buf.dtype)
        return least

    least = [finish(s, i) for i, s in enumerate(slot_ids)]
    unsafe = (jnp.max(over[...]) > HEADROOM) | (
        jnp.min(functools.reduce(jnp.minimum, least)) < 2.0**-HEADROOM
    )

    @pl.when(unsafe)
    def _():
        pool_from(old_pieces, 0, k_all, v_all)
        pool_from(pieces, len(earlier) * held, k_all, v_all)
        blocks_all = ids(earlier) + blocks
        for i, s in enumerate(slot_ids):
            row = ring_at * slots + s
            own = table_ref[row, 0]
            place = jnp.int32(0)
            for index, block in enumerate(blocks_all):
                put(place, index, jnp.where(block == own, OWN, FREE))
                place = place + table_ref[row, 1 + block]
            acc[s] = jnp.zeros(acc.shape[1:], acc.dtype)
            total[s] = jnp.zeros(total.shape[1:], total.dtype)
            top[...] = jnp.full(top.shape, MASKED, top.dtype)

            def one_block(e, carry, s=s):
                scores = dot(query_rows(s), k_all[entries[e, 0]], 1)
                weights, shrinks = [], []
                for x in range(group):
                    span = slice(x * block_rows, (x + 1) * block_rows)
                    power = scores[span] * scale + bias[entries[e, 1]]
                    new = jnp.maximum(top[span], jnp.max(power, axis=1, keepdims=True))
                    shrink = jnp.exp2(top[span] - new)
                    top[span] = new
                    weight = jnp.exp2(power - new)
                    total[s, span] = total[s, span] * shrink + weight
                    weights.append(weight.astype(jnp.bfloat16))
                    shrinks.append(shrink)
                added = dot(jnp.concatenate(weights, axis=0), v_all[entries[e, 0]], 0)
                acc[s] = acc[s] * jnp.concatenate(shrinks, axis=0) + added
                return carry

            lax.fori_loop(0, place, one_block, 0)
            finish(s, i)

    if turned == 0 and cores > 1:
        width = out_buf.shape[1]
        copy = pltpu.make_async_copy(
            out_buf, out_ref.at[:, pl.ds(pl.multiple_of(core_at * width, HEAD_DIM), width)], sems
        )
        copy.start()
        copy.wait()
    else:
        out_ref[...] = out_buf[...]


def split(cores, keys_ref, values_ref, *refs):
    outs, sems = refs[:cores], refs[cores]
    count = keys_ref.shape[0]
    width = outs[0].shape[2]
    core = lax.rem(lax.axis_index("ka"), cores)
    copies = []
    for i, out in enumerate(outs):
        column = pl.multiple_of(lax.rem(core + i, cores) * width, HEAD_DIM)
        for j, ref in enumerate((keys_ref, values_ref)):
            copy = pltpu.make_async_copy(
                ref.at[:, 0, :, pl.ds(column, width)],
                out.at[pl.ds(j * count, count)],
                sems.at[2 * i + j],
            )
            copy.start()
            copies.append(copy)
    for copy in copies:
        copy.wait()


def fetch(cores, queries_ref, out_ref, sem):
    rows, width = out_ref.shape
    at = lax.axis_index("ka")
    copy = pltpu.make_async_copy(
        queries_ref.at[
            pl.ds(pl.multiple_of(at // cores * rows, HEAD_DIM), rows),
            pl.ds(pl.multiple_of(lax.rem(at, cores) * width, HEAD_DIM), width),
        ],
        out_ref,
        sem,
    )
    copy.start()
    copy.wait()


def on_device(queries, keys, values, q_order, block_mask):
    pb, ka = lax.axis_size("pb"), lax.axis_size("ka")
    class_local, _, block_rows, kv_width = keys.shape
    cores = 2 if ka % 2 == 0 and kv_width == 2 * HEAD_DIM else 1
    rings = ka // cores
    head_width = kv_width // cores
    width = queries.shape[1] // cores
    rows = width // head_width * block_rows
    own_slots = queries.shape[0] // block_rows // ka
    slots = own_slots * cores

    vmem = pl.BlockSpec(memory_space=pltpu.VMEM)
    smem = pl.BlockSpec(memory_space=pltpu.SMEM)
    hbm = pl.BlockSpec(memory_space=pltpu.HBM)
    anywhere = pl.BlockSpec(memory_space=pl.ANY)
    stages = min(STAGES, pb)
    sources = pb // stages

    table = jnp.concatenate([q_order[:, None], block_mask], axis=1)
    part = jax.ShapeDtypeStruct((2 * class_local, block_rows, head_width), keys.dtype)
    starts = pl.pallas_call(
        functools.partial(split, cores),
        out_shape=[part] * cores,
        in_specs=[anywhere] * 2,
        out_specs=[vmem] * cores,
        scratch_shapes=[pltpu.SemaphoreType.DMA((2 * cores,))],
        compiler_params=pltpu.CompilerParams(vmem_limit_bytes=54 * 2**20),
    )(keys, values)
    own_queries = pl.pallas_call(
        functools.partial(fetch, cores),
        out_shape=jax.ShapeDtypeStruct((slots * block_rows, width), queries.dtype),
        in_specs=[anywhere],
        out_specs=vmem,
        scratch_shapes=[pltpu.SemaphoreType.DMA],
        compiler_params=pltpu.CompilerParams(vmem_limit_bytes=50 * 2**20),
    )(queries)
    if cores == 2:
        starts = [starts[0], turn(starts[1], ka, cores, 0, 1)]

    near = [starts]
    for z in range(1, pb):
        near.append([along_ring(array, pb) for array in near[-1]])
    staged = []
    for stage in range(stages):
        here = near[stage * sources : (stage + 1) * sources]
        if sources == 1:
            staged.append(here[0])
            continue
        staged.append(
            [
                jnp.concatenate(
                    [array[:class_local] for array in arrays]
                    + [array[class_local:] for array in arrays],
                    axis=0,
                )
                for arrays in zip(*here)
            ]
        )

    def call(first, last, turned, pieces, places, earlier, own_queries, state, extra):
        held = len(places) * sources * class_local
        everything = held + len(earlier) * sources * class_local
        sums = jax.ShapeDtypeStruct((slots, rows, HEAD_DIM), jnp.float32)
        outs = [sums, sums, jax.ShapeDtypeStruct((8, block_rows), jnp.float32)]
        out_specs = [vmem] * 3
        here = own_slots if last else slots
        scratch = [pltpu.VMEM((held, block_rows, HEAD_DIM), jnp.bfloat16)] * 2
        scratch += [
            pltpu.VMEM((3, block_rows, block_rows), jnp.float32),
            pltpu.SMEM((max(here * (held + 1) + 2, everything + 1), 2), jnp.int32),
            pltpu.SMEM((here * (held // 2 + 1) + 1,), jnp.int32),
        ]
        if last:
            whole = turned == 0 and cores > 1
            half = (own_slots * block_rows, width)
            outs.append(
                jax.ShapeDtypeStruct((half[0], cores * width if whole else width), queries.dtype)
            )
            out_specs.append(hbm if whole else vmem)
            scratch += [
                pltpu.VMEM(half, queries.dtype),
                pltpu.VMEM((rows, HEAD_DIM), jnp.float32),
                pltpu.VMEM((everything, block_rows, HEAD_DIM), jnp.bfloat16),
                pltpu.VMEM((everything, block_rows, HEAD_DIM), jnp.bfloat16),
                pltpu.SemaphoreType.DMA,
            ]
        state_at = 2 + len(places) + len(extra)
        return pl.pallas_call(
            functools.partial(
                attend_stage, (pb, ka, cores, places, earlier, slots, turned), first, last
            ),
            out_shape=outs,
            in_specs=[smem]
            + [vmem] * (1 + len(places))
            + [vmem if last else anywhere] * len(extra)
            + [vmem] * len(state),
            out_specs=out_specs,
            input_output_aliases={state_at + i: i for i in range(len(state))},
            scratch_shapes=scratch,
            compiler_params=pltpu.CompilerParams(vmem_limit_bytes=16 * 2**20),
            cost_estimate=pl.CostEstimate(
                flops=2**31, bytes_accessed=2**22, transcendentals=2**20
            ),
        )(table, own_queries, *pieces, *extra, *state)

    state, earlier, before = [], [], []
    for stage in range(stages):
        hops = range(stage * sources, (stage + 1) * sources)
        places, pieces = [], []
        for c in range(cores):
            ring = staged[stage][c]
            for y in range(rings):
                if y:
                    ring = turn(ring, ka, cores, 1, 0)
                places.append((hops, y, c))
                pieces.append(ring)
        first, last = stage == 0, stage == stages - 1
        if not last:
            ahead = [staged[min(stage // 2 + 2, stages - 1)][0 if stage == 1 else -1]]
            state = call(first, last, 0, pieces, places, earlier, own_queries, state, ahead)
            earlier, before = earlier + places, before + pieces
    halves = []
    for c in reversed(range(cores)):
        *state, half = call(False, True, c, pieces, places, earlier, own_queries, state, before)
        halves.append(half)
    if cores == 1:
        return halves[0]
    core_at = lax.rem(lax.axis_index("ka"), cores)
    other = turn(halves[0], ka, cores, 0, 1)
    return lax.dynamic_update_slice(halves[1], other, (0, (1 - core_at) * width))


def solution(mesh):
    in_specs = (
        P("pb", "ha"),
        P("pb", "ka", None, "ha"),
        P("pb", "ka", None, "ha"),
        P("pb"),
        P("pb", None),
    )
    out_specs = P(("pb", "ka"), "ha")
    return jax.shard_map(
        on_device, mesh=mesh, in_specs=in_specs, out_specs=out_specs, check_vma=False
    )
```

```python
import functools
import math

import jax
import jax.numpy as jnp
from jax import lax
from jax.experimental import pallas as pl
from jax.experimental.pallas import tpu as pltpu
from jax.sharding import PartitionSpec as P

HEAD_DIM = 128
MASKED = -1e30
HIDDEN = -1e38
HEADROOM = 64.0
PARTS = 8
FREE, OWN, NONE = 0, 1, 2
STAGES = 4


def folded(size):
    return list(range(0, size, 2)) + list(range(1, size, 2))[::-1]


def along_ring(array, size):
    ring = folded(size)
    return lax.ppermute(array, "pb", [(ring[i], ring[(i + 1) % size]) for i in range(size)])


def ring_source(at, size, hops):
    place = jnp.where(at % 2 == 0, at // 2, size - 1 - at // 2)
    place = lax.rem(place + (size - hops), size)
    return jnp.where(place < (size + 1) // 2, 2 * place, 2 * (size - 1 - place) + 1)


def turn(array, size, cores, ring_step, core_step):
    rings = size // cores
    pairs = []
    for ring in range(rings):
        for core in range(cores):
            to = ((ring + ring_step) % rings) * cores + (core + core_step) % cores
            pairs.append((ring * cores + core, to))
    return lax.ppermute(array, "ka", pairs)


def dot(a, b, b_dim):
    return lax.dot_general(a, b, (((1,), (b_dim,)), ((), ())), preferred_element_type=jnp.float32)


def copy_rows(source, target, sems):
    step = source.shape[0] // PARTS
    copies = [
        pltpu.make_async_copy(
            source.at[pl.ds(i * step, step)], target.at[pl.ds(i * step, step)], sems.at[i]
        )
        for i in range(PARTS)
    ]
    for copy in copies:
        copy.start()
    for copy in copies:
        copy.wait()


def attend_stage(plan, first, last, table_ref, q_ref, *refs):
    pb, ka, cores, places, earlier, slots, turned = plan
    count = len(places)
    pieces, refs = refs[:count], refs[count:]
    if last:
        old_pieces, refs = refs[: len(earlier)], refs[len(earlier) :]
    else:
        refs = refs[1:]
    if not first:
        refs = refs[3:]
    acc, total, over, refs = *refs[:3], refs[3:]
    if last:
        out_ref, refs = refs[0], refs[1:]
    k_pool, v_pool, bias, entries, units, refs = *refs[:5], refs[5:]
    rows = acc.shape[1]
    held, block_rows, _ = pieces[0].shape
    held = held // 2
    group = rows // block_rows
    rings = ka // cores
    own_slots = slots // cores
    p_at, k_at = lax.axis_index("pb"), lax.axis_index("ka")
    ring_at, core_at = k_at // cores, lax.rem(k_at, cores)
    scale = math.log2(math.e) / math.sqrt(HEAD_DIM)
    class_local = held // len(places[0][0]) // cores

    def ids(where):
        found = []
        for hops, y in where:
            ring = lax.rem(ring_at + (rings - y), rings)
            for z in hops:
                source = ring_source(p_at, pb, z)
                for c in range(cores):
                    core = lax.rem(core_at + (cores - c), cores)
                    for t in range(class_local):
                        found.append((source * class_local + t) * ka + ring * cores + core)
        return found

    def pool_from(refs_in, at, k_out, v_out):
        for piece in refs_in:
            for i in range(0, 2 * held, 2 * class_local):
                k_out[at : at + class_local] = piece[i : i + class_local]
                v_out[at : at + class_local] = piece[i + class_local : i + 2 * class_local]
                at += class_local

    if last:
        mine = lax.rem(core_at + turned, cores) * own_slots
        slot_ids = [mine + i for i in range(own_slots)]
    else:
        slot_ids = list(range(slots))

    row_id = lax.broadcasted_iota(jnp.int32, (block_rows, block_rows), 0)
    col_id = lax.broadcasted_iota(jnp.int32, (block_rows, block_rows), 1)
    bias[FREE] = jnp.zeros((block_rows, block_rows), jnp.float32)
    bias[OWN] = jnp.where(col_id <= row_id, 0.0, HIDDEN)
    bias[NONE] = jnp.full((block_rows, block_rows), HIDDEN, jnp.float32)
    pool_from(pieces, 0, k_pool, v_pool)
    if first:
        acc[...] = jnp.zeros(acc.shape, acc.dtype)
        total[...] = jnp.zeros(total.shape, total.dtype)
        over[...] = jnp.full(over.shape, MASKED, over.dtype)

    def put(place, index, kind):
        entries[place, 0] = index
        entries[place, 1] = kind

    blocks = ids(places)
    unit_count = jnp.int32(0)
    for s in slot_ids:
        row = ring_at * slots + s
        own = table_ref[row, 0]
        place = 2 * unit_count
        for index, block in enumerate(blocks):
            put(place, index, jnp.where(block == own, OWN, FREE))
            place = place + table_ref[row, 1 + block]
        put(place, 0, NONE)
        ends = lax.div(place + 1, 2)

        def mark(u, carry, s=s):
            units[u] = s
            return carry

        lax.fori_loop(unit_count, ends, mark, 0)
        unit_count = ends
    put(2 * unit_count, 0, NONE)
    put(2 * unit_count + 1, 0, NONE)
    units[unit_count] = slot_ids[0]

    def query_rows(s):
        return jnp.concatenate(
            [
                q_ref[
                    pl.ds(pl.multiple_of(s * block_rows, block_rows), block_rows),
                    x * HEAD_DIM : (x + 1) * HEAD_DIM,
                ]
                for x in range(group)
            ],
            axis=0,
        )

    def unit_weights(u, highest):
        s = units[u]
        index = [entries[2 * u + half, 0] for half in range(2)]
        kind = [entries[2 * u + half, 1] for half in range(2)]
        scores = dot(query_rows(s), jnp.concatenate([k_pool[i] for i in index], axis=0), 1)
        weights, sums = [], []
        for x in range(group):
            row = []
            for half in range(2):
                power = (
                    scores[
                        x * block_rows : (x + 1) * block_rows,
                        half * block_rows : (half + 1) * block_rows,
                    ]
                    * scale
                    + bias[kind[half]]
                )
                tops = [power[i : i + 8] for i in range(0, block_rows, 8)]
                while len(tops) > 1:
                    tops = [jnp.maximum(*tops[i : i + 2]) for i in range(0, len(tops), 2)]
                highest = jnp.maximum(highest, tops[0])
                row.append(jnp.exp2(power))
            sums.append(row[0] + row[1])
            weights.append(jnp.concatenate([w.astype(jnp.bfloat16) for w in row], axis=1))
        added = dot(
            jnp.concatenate(weights, axis=0),
            jnp.concatenate([v_pool[i] for i in index], axis=0),
            0,
        )
        return s, jnp.concatenate(sums, axis=0), added, highest

    def two_units(i, carry):
        highest = over[...]
        done = []
        for j in range(2):
            s, sums, added, highest = unit_weights(2 * i + j, highest)
            done.append((s, sums, added))
        for s, sums, added in done:
            total[s] += sums
            acc[s] += added
        over[...] = highest
        return carry

    lax.fori_loop(0, lax.div(unit_count + 1, 2), two_units, 0)
    if not last:
        return

    out_buf, top, k_all, v_all, sems = refs

    ones = jnp.ones((HEAD_DIM, HEAD_DIM), jnp.bfloat16)

    def finish(s, i):
        sums = total[s]
        high = sums.astype(jnp.bfloat16)
        low = (sums - high.astype(jnp.float32)).astype(jnp.bfloat16)
        under = dot(high, ones, 0) + dot(low, ones, 0)
        result = (acc[s] / under).astype(out_buf.dtype)
        for x in range(group):
            span = slice(x * block_rows, (x + 1) * block_rows)
            out_buf[
                i * block_rows : (i + 1) * block_rows, x * HEAD_DIM : (x + 1) * HEAD_DIM
            ] = result[span]
        tops = [under[i : i + 8] for i in range(0, rows, 8)]
        while len(tops) > 1:
            tops = [functools.reduce(jnp.minimum, tops[i : i + 2]) for i in range(0, len(tops), 2)]
        return tops[0]

    least = [finish(s, i) for i, s in enumerate(slot_ids)]
    unsafe = (jnp.max(over[...]) > HEADROOM) | (
        jnp.min(functools.reduce(jnp.minimum, least)) < 2.0**-HEADROOM
    )

    @pl.when(unsafe)
    def _():
        pool_from(old_pieces, 0, k_all, v_all)
        pool_from(pieces, len(earlier) * held, k_all, v_all)
        blocks_all = ids(earlier) + blocks
        for i, s in enumerate(slot_ids):
            row = ring_at * slots + s
            own = table_ref[row, 0]
            place = jnp.int32(0)
            for index, block in enumerate(blocks_all):
                put(place, index, jnp.where(block == own, OWN, FREE))
                place = place + table_ref[row, 1 + block]
            acc[s] = jnp.zeros(acc.shape[1:], acc.dtype)
            total[s] = jnp.zeros(total.shape[1:], total.dtype)
            top[...] = jnp.full(top.shape, MASKED, top.dtype)

            def one_block(e, carry, s=s):
                scores = dot(query_rows(s), k_all[entries[e, 0]], 1)
                weights, shrinks = [], []
                for x in range(group):
                    span = slice(x * block_rows, (x + 1) * block_rows)
                    power = scores[span] * scale + bias[entries[e, 1]]
                    new = jnp.maximum(top[span], jnp.max(power, axis=1, keepdims=True))
                    shrink = jnp.exp2(top[span] - new)
                    top[span] = new
                    weight = jnp.exp2(power - new)
                    total[s, span] = total[s, span] * shrink + weight
                    weights.append(weight.astype(jnp.bfloat16))
                    shrinks.append(shrink)
                added = dot(jnp.concatenate(weights, axis=0), v_all[entries[e, 0]], 0)
                acc[s] = acc[s] * jnp.concatenate(shrinks, axis=0) + added
                return carry

            lax.fori_loop(0, place, one_block, 0)
            finish(s, i)

    if turned == 0 and cores > 1:
        width = out_buf.shape[1]
        copy_rows(
            out_buf, out_ref.at[:, pl.ds(pl.multiple_of(core_at * width, HEAD_DIM), width)], sems
        )
    else:
        out_ref[...] = out_buf[...]


def split(cores, keys_ref, values_ref, *refs):
    outs, sems = refs[:cores], refs[cores]
    count = keys_ref.shape[0]
    width = outs[0].shape[2]
    core = lax.rem(lax.axis_index("ka"), cores)
    copies = []
    for i in reversed(range(cores)):
        column = pl.multiple_of(lax.rem(core + i, cores) * width, HEAD_DIM)
        for j, ref in enumerate((keys_ref, values_ref)):
            for t in range(count):
                copy = pltpu.make_async_copy(
                    ref.at[t, 0, :, pl.ds(column, width)],
                    outs[i].at[j * count + t],
                    sems.at[(2 * i + j) * count + t],
                )
                copy.start()
                copies.append(copy)
    for copy in copies:
        copy.wait()


def merge(other_ref, queries_ref, own_ref, both_ref, sem):
    half = other_ref.shape[0]
    copy = pltpu.make_async_copy(other_ref, both_ref.at[pl.ds(half, half)], sem)
    copy.start()
    copy.wait()


def fetch(cores, queries_ref, out_ref, sems):
    rows, width = out_ref.shape
    at = lax.axis_index("ka")
    copy_rows(
        queries_ref.at[
            pl.ds(pl.multiple_of(at // cores * rows, HEAD_DIM), rows),
            pl.ds(pl.multiple_of(lax.rem(at, cores) * width, HEAD_DIM), width),
        ],
        out_ref,
        sems,
    )


def join(cores, other_ref, half_ref, out_ref, sems):
    width = other_ref.shape[1]
    at = lax.rem(lax.axis_index("ka") + 1, cores) * width
    copy_rows(
        other_ref, out_ref.at[:, pl.ds(pl.multiple_of(at, HEAD_DIM), width)], sems
    )


def on_device(queries, keys, values, q_order, block_mask):
    pb, ka = lax.axis_size("pb"), lax.axis_size("ka")
    class_local, _, block_rows, kv_width = keys.shape
    cores = 2 if ka % 2 == 0 and kv_width == 2 * HEAD_DIM else 1
    rings = ka // cores
    head_width = kv_width // cores
    width = queries.shape[1] // cores
    rows = width // head_width * block_rows
    own_slots = queries.shape[0] // block_rows // ka
    slots = own_slots * cores

    vmem = pl.BlockSpec(memory_space=pltpu.VMEM)
    smem = pl.BlockSpec(memory_space=pltpu.SMEM)
    hbm = pl.BlockSpec(memory_space=pltpu.HBM)
    anywhere = pl.BlockSpec(memory_space=pl.ANY)
    stages = min(STAGES, pb)
    sources = pb // stages

    table = jnp.concatenate([q_order[:, None], block_mask], axis=1)
    held = 2 * class_local
    starts = pl.pallas_call(
        functools.partial(split, cores),
        out_shape=[
            jax.ShapeDtypeStruct(((cores if i == 0 else 1) * held, block_rows, head_width), keys.dtype)
            for i in range(cores)
        ],
        in_specs=[anywhere] * 2,
        out_specs=[vmem] * cores,
        scratch_shapes=[pltpu.SemaphoreType.DMA((cores * held,))],
        compiler_params=pltpu.CompilerParams(vmem_limit_bytes=54 * 2**20),
    )(keys, values)
    own_queries = pl.pallas_call(
        functools.partial(fetch, cores),
        out_shape=jax.ShapeDtypeStruct((slots * block_rows, width), queries.dtype),
        in_specs=[anywhere],
        out_specs=vmem,
        scratch_shapes=[pltpu.SemaphoreType.DMA((PARTS,))],
        compiler_params=pltpu.CompilerParams(vmem_limit_bytes=50 * 2**20),
    )(queries)
    start = starts[0]
    if cores == 2:
        start = pl.pallas_call(
            merge,
            out_shape=jax.ShapeDtypeStruct(start.shape, start.dtype),
            in_specs=[anywhere] * 3,
            out_specs=anywhere,
            input_output_aliases={2: 0},
            scratch_shapes=[pltpu.SemaphoreType.DMA],
        )(turn(starts[1], ka, cores, 0, 1), own_queries, start)

    beside = turn(start, ka, cores, 1, 0) if rings > 1 else start
    near = [start]
    for z in range(1, pb):
        near.append(along_ring(near[-1], pb))
        if z == 1:
            near[1], beside = lax.optimization_barrier((near[1], beside))
    staged = []
    for stage in range(stages):
        here = near[stage * sources : (stage + 1) * sources]
        staged.append(here[0] if sources == 1 else jnp.concatenate(here, axis=0))

    def call(first, last, turned, pieces, places, earlier, own_queries, state, extra):
        held = len(places) * sources * cores * class_local
        everything = held + len(earlier) * sources * cores * class_local
        sums = jax.ShapeDtypeStruct((slots, rows, HEAD_DIM), jnp.float32)
        outs = [sums, sums, jax.ShapeDtypeStruct((8, block_rows), jnp.float32)]
        out_specs = [vmem] * 3
        here = own_slots if last else slots
        scratch = [pltpu.VMEM((held, block_rows, HEAD_DIM), jnp.bfloat16)] * 2
        scratch += [
            pltpu.VMEM((3, block_rows, block_rows), jnp.float32),
            pltpu.SMEM((max(here * (held + 1) + 2, everything + 1), 2), jnp.int32),
            pltpu.SMEM((here * (held // 2 + 1) + 1,), jnp.int32),
        ]
        if last:
            whole = turned == 0 and cores > 1
            half = (own_slots * block_rows, width)
            outs.append(
                jax.ShapeDtypeStruct((half[0], cores * width if whole else width), queries.dtype)
            )
            out_specs.append(hbm if whole else vmem)
            scratch += [
                pltpu.VMEM(half, queries.dtype),
                pltpu.VMEM((rows, HEAD_DIM), jnp.float32),
                pltpu.VMEM((everything, block_rows, HEAD_DIM), jnp.bfloat16),
                pltpu.VMEM((everything, block_rows, HEAD_DIM), jnp.bfloat16),
                pltpu.SemaphoreType.DMA((PARTS,)),
            ]
        state_at = 2 + len(places) + len(extra)
        return pl.pallas_call(
            functools.partial(
                attend_stage, (pb, ka, cores, places, earlier, slots, turned), first, last
            ),
            out_shape=outs,
            in_specs=[smem]
            + [vmem] * (1 + len(places))
            + [vmem if last else anywhere] * len(extra)
            + [vmem] * len(state),
            out_specs=out_specs,
            input_output_aliases={state_at + i: i for i in range(len(state))},
            scratch_shapes=scratch,
            compiler_params=pltpu.CompilerParams(vmem_limit_bytes=16 * 2**20),
            cost_estimate=pl.CostEstimate(
                flops=2**31, bytes_accessed=2**22, transcendentals=2**20
            ),
        )(table, own_queries, *pieces, *extra, *state)

    state, earlier, before = [], [], []
    for stage in range(stages):
        hops = range(stage * sources, (stage + 1) * sources)
        places, pieces = [], []
        ring = staged[stage]
        for y in range(rings):
            if y:
                ring = beside if y == 1 and stage == 0 and sources == 1 else turn(ring, ka, cores, 1, 0)
            places.append((hops, y))
            pieces.append(ring)
        first, last = stage == 0, stage == stages - 1
        if not last:
            ahead = [staged[stage + 1]]
            state = call(first, last, 0, pieces, places, earlier, own_queries, state, ahead)
            earlier, before = earlier + places, before + pieces
    halves = []
    for c in reversed(range(cores)):
        *state, half = call(False, True, c, pieces, places, earlier, own_queries, state, before)
        halves.append(half)
    if cores == 1:
        return halves[0]
    return pl.pallas_call(
        functools.partial(join, cores),
        out_shape=jax.ShapeDtypeStruct((own_slots * block_rows, cores * width), queries.dtype),
        in_specs=[vmem, anywhere],
        out_specs=anywhere,
        input_output_aliases={1: 0},
        scratch_shapes=[pltpu.SemaphoreType.DMA((PARTS,))],
    )(turn(halves[0], ka, cores, 0, 1), halves[1])


def solution(mesh):
    in_specs = (
        P("pb", "ha"),
        P("pb", "ka", None, "ha"),
        P("pb", "ka", None, "ha"),
        P("pb"),
        P("pb", None),
    )
    out_specs = P(("pb", "ka"), "ha")
    return jax.shard_map(
        on_device, mesh=mesh, in_specs=in_specs, out_specs=out_specs, check_vma=False
    )
```

```python
import functools
import math

import jax
import jax.numpy as jnp
from jax import lax
from jax.experimental import pallas as pl
from jax.experimental.pallas import tpu as pltpu
from jax.sharding import PartitionSpec as P

HEAD_DIM = 128
MASKED = -1e30
HIDDEN = -1e38
HEADROOM = 64.0
PARTS = 8
LIMIT = 10
STAGES = 4


def folded(size):
    return list(range(0, size, 2)) + list(range(1, size, 2))[::-1]


def along_ring(array, size, step):
    ring = folded(size)
    return lax.ppermute(array, "pb", [(ring[i], ring[(i + step) % size]) for i in range(size)])


def ring_source(at, size, hops):
    place = jnp.where(at % 2 == 0, at // 2, size - 1 - at // 2)
    place = lax.rem(place + (size - hops), size)
    return jnp.where(place < (size + 1) // 2, 2 * place, 2 * (size - 1 - place) + 1)


def turn(array, size, cores, ring_step, core_step):
    rings = size // cores
    pairs = []
    for ring in range(rings):
        for core in range(cores):
            to = ((ring + ring_step) % rings) * cores + (core + core_step) % cores
            pairs.append((ring * cores + core, to))
    return lax.ppermute(array, "ka", pairs)


def dot(a, b, b_dim):
    return lax.dot_general(a, b, (((1,), (b_dim,)), ((), ())), preferred_element_type=jnp.float32)


def copy_rows(source, target, sems):
    step = source.shape[0] // PARTS
    copies = [
        pltpu.make_async_copy(
            source.at[pl.ds(i * step, step)], target.at[pl.ds(i * step, step)], sems.at[i]
        )
        for i in range(PARTS)
    ]
    for copy in copies:
        copy.start()
    return copies


def attend_stage(plan, first, last, ahead, table_ref, q_ref, *refs):
    pb, ka, cores, places, earlier, slots, turned = plan
    count = len(places)
    pieces, refs = refs[:count], refs[count:]
    old_pieces, refs = refs[:ahead], refs[ahead:]
    if not first:
        refs = refs[1:]
    acc, refs = refs[0], refs[1:]
    if last:
        out_ref, refs = refs[0], refs[1:]
    k_pool, v_pool, entries, units, refs = *refs[:4], refs[4:]
    rows = acc.shape[1]
    held, block_rows, _ = pieces[0].shape
    held = held // 2
    group = rows // block_rows
    rings = ka // cores
    own_slots = slots // cores
    p_at, k_at = lax.axis_index("pb"), lax.axis_index("ka")
    ring_at, core_at = k_at // cores, lax.rem(k_at, cores)
    scale = math.log2(math.e) / math.sqrt(HEAD_DIM)
    class_local = held // len(places[0][0])
    nothing = count * held

    def ids(where):
        found = []
        for hops, y, c in where:
            ring = lax.rem(ring_at + (rings - y), rings)
            core = lax.rem(core_at + (cores - c), cores)
            for z in hops:
                source = ring_source(p_at, pb, z)
                for t in range(class_local):
                    found.append((source * class_local + t) * ka + ring * cores + core)
        return found

    def pool_from(refs_in, at, k_out, v_out):
        for i, piece in enumerate(refs_in):
            span = slice(at + i * held, at + (i + 1) * held)
            k_out[span] = piece[:held]
            v_out[span, :, :HEAD_DIM] = piece[held:]
            v_out[span, :, HEAD_DIM:] = jnp.ones(piece[held:].shape, v_out.dtype)

    if last:
        mine = lax.rem(core_at + turned, cores) * own_slots
        slot_ids = [mine + i for i in range(own_slots)]
    else:
        slot_ids = list(range(slots))

    row_id = lax.broadcasted_iota(jnp.int32, (block_rows, block_rows), 0)
    col_id = lax.broadcasted_iota(jnp.int32, (block_rows, block_rows), 1)
    pool_from(pieces, 0, k_pool, v_pool)
    k_pool[nothing] = jnp.zeros(k_pool.shape[1:], k_pool.dtype)
    v_pool[nothing] = jnp.zeros(v_pool.shape[1:], v_pool.dtype)
    if first:
        acc[...] = jnp.zeros(acc.shape, acc.dtype)

    blocks = ids(places)
    unit_count = jnp.int32(0)
    for s in slot_ids:
        row = ring_at * slots + s
        own = table_ref[row, 0]
        place = 2 * unit_count
        for index, block in enumerate(blocks):
            entries[place] = jnp.where(block == own, index + nothing + 1, index)
            place = place + table_ref[row, 1 + block]
        entries[place] = nothing
        ends = lax.div(place + 1, 2)

        def mark(u, carry, s=s):
            units[u] = s
            return carry

        lax.fori_loop(unit_count, ends, mark, 0)
        unit_count = ends
    entries[2 * unit_count] = nothing
    entries[2 * unit_count + 1] = nothing
    units[unit_count] = slot_ids[0]

    def query_rows(s):
        return jnp.concatenate(
            [
                q_ref[
                    pl.ds(pl.multiple_of(s * block_rows, block_rows), block_rows),
                    x * HEAD_DIM : (x + 1) * HEAD_DIM,
                ]
                for x in range(group)
            ],
            axis=0,
        )

    def unit_sums(s, index, owns):
        scores = dot(query_rows(s), jnp.concatenate([k_pool[i] for i in index], axis=0), 1)
        power = scores * scale
        if owns is not None:
            reach = jnp.concatenate(
                [
                    jnp.where(col_id <= row_id + jnp.where(own, 0, block_rows), 0.0, HIDDEN)
                    for own in owns
                ],
                axis=1,
            )
            power = power + jnp.concatenate([reach] * group, axis=0)
        weights = jnp.exp2(power).astype(jnp.bfloat16)
        return dot(weights, jnp.concatenate([v_pool[i] for i in index], axis=0), 0)

    def two_units(i, carry):
        raw = [entries[4 * i + j] for j in range(4)]
        owns = [entry > nothing for entry in raw]
        index = [
            jnp.where(own, entry - (nothing + 1), entry) for own, entry in zip(owns, raw)
        ]
        which = [units[2 * i], units[2 * i + 1]]
        some = functools.reduce(jnp.logical_or, owns)

        def take(masked):
            added = [
                unit_sums(
                    which[j],
                    index[2 * j : 2 * j + 2],
                    owns[2 * j : 2 * j + 2] if masked else None,
                )
                for j in range(2)
            ]
            for j in range(2):
                acc[which[j]] += added[j]

        pl.when(some)(functools.partial(take, True))
        pl.when(jnp.logical_not(some))(functools.partial(take, False))
        return carry

    lax.fori_loop(0, lax.div(unit_count + 1, 2), two_units, 0)
    if not last:
        return

    top, k_all, v_all = refs

    def finish(s, i):
        under = acc[s, :, HEAD_DIM:]
        result = (acc[s, :, :HEAD_DIM] / under).astype(out_ref.dtype)
        for x in range(group):
            out_ref[
                i * block_rows : (i + 1) * block_rows, x * HEAD_DIM : (x + 1) * HEAD_DIM
            ] = result[x * block_rows : (x + 1) * block_rows]
        low = high = [under[j : j + 8] for j in range(0, rows, 8)]
        while len(low) > 1:
            low = [functools.reduce(jnp.minimum, low[j : j + 2]) for j in range(0, len(low), 2)]
            high = [functools.reduce(jnp.maximum, high[j : j + 2]) for j in range(0, len(high), 2)]
        return low[0], high[0]

    low, high = zip(*[finish(s, i) for i, s in enumerate(slot_ids)])
    low, high = functools.reduce(jnp.minimum, low), functools.reduce(jnp.maximum, high)
    safe = (low > 2.0**-HEADROOM) & (high < 2.0**HEADROOM)

    @pl.when(jnp.min(jnp.where(safe, 1.0, 0.0)) < 0.5)
    def _():
        pool_from(old_pieces, 0, k_all, v_all)
        pool_from(pieces, len(earlier) * held, k_all, v_all)
        blocks_all = ids(earlier) + blocks
        for i, s in enumerate(slot_ids):
            row = ring_at * slots + s
            own = table_ref[row, 0]
            place = jnp.int32(0)
            for index, block in enumerate(blocks_all):
                entries[place] = jnp.where(block == own, index + len(blocks_all), index)
                place = place + table_ref[row, 1 + block]
            acc[s] = jnp.zeros(acc.shape[1:], acc.dtype)
            top[...] = jnp.full(top.shape, MASKED, top.dtype)

            def one_block(e, carry, s=s):
                is_own = entries[e] >= len(blocks_all)
                index = jnp.where(is_own, entries[e] - len(blocks_all), entries[e])
                reach = jnp.where(
                    col_id <= row_id + jnp.where(is_own, 0, block_rows), 0.0, HIDDEN
                )
                scores = dot(query_rows(s), k_all[index], 1)
                weights, shrinks = [], []
                for x in range(group):
                    span = slice(x * block_rows, (x + 1) * block_rows)
                    power = scores[span] * scale + reach
                    new = jnp.maximum(top[span], jnp.max(power, axis=1, keepdims=True))
                    shrink = jnp.exp2(top[span] - new)
                    top[span] = new
                    weights.append(jnp.exp2(power - new).astype(jnp.bfloat16))
                    shrinks.append(jnp.concatenate([shrink, shrink], axis=1))
                added = dot(jnp.concatenate(weights, axis=0), v_all[index], 0)
                acc[s] = acc[s] * jnp.concatenate(shrinks, axis=0) + added
                return carry

            lax.fori_loop(0, place, one_block, 0)
            finish(s, i)


def split(cores, keys_ref, values_ref, *refs):
    outs, sems = refs[:cores], refs[cores]
    count = keys_ref.shape[0]
    width = outs[0].shape[2]
    core = lax.rem(lax.axis_index("ka"), cores)
    copies = []
    for i, out in enumerate(outs):
        column = pl.multiple_of(lax.rem(core + i, cores) * width, HEAD_DIM)
        for j, ref in enumerate((keys_ref, values_ref)):
            copy = pltpu.make_async_copy(
                ref.at[:, 0, :, pl.ds(column, width)],
                out.at[pl.ds(j * count, count)],
                sems.at[2 * i + j],
            )
            copy.start()
            copies.append(copy)
    for copy in copies:
        copy.wait()


def fetch(cores, queries_ref, out_ref, sems):
    rows, width = out_ref.shape
    at = lax.axis_index("ka")
    copies = copy_rows(
        queries_ref.at[
            pl.ds(pl.multiple_of(at // cores * rows, HEAD_DIM), rows),
            pl.ds(pl.multiple_of(lax.rem(at, cores) * width, HEAD_DIM), width),
        ],
        out_ref,
        sems,
    )
    for copy in copies:
        copy.wait()


def join(cores, own_ref, other_ref, out_ref, sems):
    width = own_ref.shape[1]
    core = lax.rem(lax.axis_index("ka"), cores)
    copies = []
    for i, ref in enumerate((own_ref, other_ref)):
        at = pl.multiple_of(lax.rem(core + (cores - i), cores) * width, HEAD_DIM)
        copies += copy_rows(ref, out_ref.at[:, pl.ds(at, width)], sems.at[i])
    for copy in copies:
        copy.wait()


def on_device(queries, keys, values, q_order, block_mask):
    pb, ka = lax.axis_size("pb"), lax.axis_size("ka")
    class_local, _, block_rows, kv_width = keys.shape
    cores = 2 if ka % 2 == 0 and kv_width == 2 * HEAD_DIM else 1
    rings = ka // cores
    head_width = kv_width // cores
    width = queries.shape[1] // cores
    rows = width // head_width * block_rows
    own_slots = queries.shape[0] // block_rows // ka
    slots = own_slots * cores

    vmem = pl.BlockSpec(memory_space=pltpu.VMEM)
    smem = pl.BlockSpec(memory_space=pltpu.SMEM)
    hbm = pl.BlockSpec(memory_space=pltpu.HBM)
    anywhere = pl.BlockSpec(memory_space=pl.ANY)
    stages = min(STAGES, pb)
    sources = pb // stages

    table = jnp.concatenate([q_order[:, None], block_mask], axis=1)
    part = jax.ShapeDtypeStruct((2 * class_local, block_rows, head_width), keys.dtype)
    starts = pl.pallas_call(
        functools.partial(split, cores),
        out_shape=[part] * cores,
        in_specs=[anywhere] * 2,
        out_specs=[vmem] * cores,
        scratch_shapes=[pltpu.SemaphoreType.DMA((2 * cores,))],
        compiler_params=pltpu.CompilerParams(vmem_limit_bytes=54 * 2**20),
    )(keys, values)
    own_queries = pl.pallas_call(
        functools.partial(fetch, cores),
        out_shape=jax.ShapeDtypeStruct((slots * block_rows, width), queries.dtype),
        in_specs=[anywhere],
        out_specs=vmem,
        scratch_shapes=[pltpu.SemaphoreType.DMA((PARTS,))],
        compiler_params=pltpu.CompilerParams(vmem_limit_bytes=50 * 2**20),
    )(queries)
    if cores == 2:
        starts = [starts[0], turn(starts[1], ka, cores, 0, 1)]

    near = {0: starts}
    order = [0]
    for hop in range(1, pb // 2 + 1):
        for z, step in ((hop, 1), (pb - hop, -1)):
            if z not in near:
                near[z] = [along_ring(array, pb, step) for array in near[(z - step) % pb]]
                order.append(z)
    staged = []
    for stage in range(stages):
        here = [near[z] for z in order[stage * sources : (stage + 1) * sources]]
        if sources == 1:
            staged.append(here[0])
            continue
        staged.append(
            [
                jnp.concatenate(
                    [array[:class_local] for array in arrays]
                    + [array[class_local:] for array in arrays],
                    axis=0,
                )
                for arrays in zip(*here)
            ]
        )

    def call(first, last, turned, pieces, places, earlier, own_queries, state, extra):
        held = len(places) * sources * class_local
        everything = held + len(earlier) * sources * class_local
        here = own_slots if last else slots
        outs = [jax.ShapeDtypeStruct((slots, rows, 2 * HEAD_DIM), jnp.float32)]
        scratch = [
            pltpu.VMEM((held + 1, block_rows, HEAD_DIM), jnp.bfloat16),
            pltpu.VMEM((held + 1, block_rows, 2 * HEAD_DIM), jnp.bfloat16),
            pltpu.SMEM((max(here * (held + 1) + 2, everything + 1),), jnp.int32),
            pltpu.SMEM((here * (held // 2 + 1) + 1,), jnp.int32),
        ]
        if last:
            outs.append(jax.ShapeDtypeStruct((own_slots * block_rows, width), queries.dtype))
            scratch += [
                pltpu.VMEM((rows, HEAD_DIM), jnp.float32),
                pltpu.VMEM((everything, block_rows, HEAD_DIM), jnp.bfloat16),
                pltpu.VMEM((everything, block_rows, 2 * HEAD_DIM), jnp.bfloat16),
            ]
        pooled = held + (everything if last else 0)
        room = LIMIT * 2**20 + pooled * block_rows * HEAD_DIM * 6
        state_at = 2 + len(places) + len(extra)
        return pl.pallas_call(
            functools.partial(
                attend_stage,
                (pb, ka, cores, places, earlier, slots, turned),
                first,
                last,
                len(extra),
            ),
            out_shape=outs,
            in_specs=[smem]
            + [vmem] * (1 + len(places))
            + [vmem if last else anywhere] * len(extra)
            + [vmem] * len(state),
            out_specs=[vmem] * len(outs),
            input_output_aliases={state_at + i: i for i in range(len(state))},
            scratch_shapes=scratch,
            compiler_params=pltpu.CompilerParams(vmem_limit_bytes=room),
            cost_estimate=pl.CostEstimate(
                flops=2**31, bytes_accessed=2**22, transcendentals=2**20
            ),
        )(table, own_queries, *pieces, *extra, *state)

    placed = []
    for stage in range(stages):
        hops = order[stage * sources : (stage + 1) * sources]
        places, pieces = [], []
        for c in range(cores):
            ring = staged[stage][c]
            for y in range(rings):
                if y:
                    ring = turn(ring, ka, cores, 1, 0)
                places.append((hops, y, c))
                pieces.append(ring)
        placed.append((places, pieces))
    state, earlier, before = [], [], []
    for stage in range(stages - 1):
        places, pieces = placed[stage]
        ahead = [staged[stage + 1][-1]]
        state = call(stage == 0, False, 0, pieces, places, earlier, own_queries, state, ahead)
        earlier, before = earlier + places, before + pieces
    places, pieces = placed[-1]
    halves = []
    for c in reversed(range(cores)):
        *state, half = call(False, True, c, pieces, places, earlier, own_queries, state, before)
        halves.append(half)
    if cores == 1:
        return halves[0]
    return pl.pallas_call(
        functools.partial(join, cores),
        out_shape=jax.ShapeDtypeStruct((own_slots * block_rows, cores * width), queries.dtype),
        in_specs=[vmem] * 2,
        out_specs=anywhere,
        scratch_shapes=[pltpu.SemaphoreType.DMA((cores, PARTS))],
    )(halves[1], turn(halves[0], ka, cores, 0, 1))


def solution(mesh):
    in_specs = (
        P("pb", "ha"),
        P("pb", "ka", None, "ha"),
        P("pb", "ka", None, "ha"),
        P("pb"),
        P("pb", None),
    )
    out_specs = P(("pb", "ka"), "ha")
    return jax.shard_map(
        on_device, mesh=mesh, in_specs=in_specs, out_specs=out_specs, check_vma=False
    )
```

```python
import functools
import math

import jax
import jax.numpy as jnp
from jax import lax
from jax.experimental import pallas as pl
from jax.experimental.pallas import tpu as pltpu
from jax.sharding import PartitionSpec as P

HEAD_DIM = 128
MASKED = -1e30
HIDDEN = -1e38
HEADROOM = 64.0
PARTS = 8
LIMIT = 10
SMALL = 4
STAGES = 4


def folded(size):
    return list(range(0, size, 2)) + list(range(1, size, 2))[::-1]


def along_ring(array, size):
    ring = folded(size)
    return lax.ppermute(array, "pb", [(ring[i], ring[(i + 1) % size]) for i in range(size)])


def ring_source(at, size, hops):
    place = jnp.where(at % 2 == 0, at // 2, size - 1 - at // 2)
    place = lax.rem(place + (size - hops), size)
    return jnp.where(place < (size + 1) // 2, 2 * place, 2 * (size - 1 - place) + 1)


def turn(array, size, cores, ring_step, core_step):
    rings = size // cores
    pairs = []
    for ring in range(rings):
        for core in range(cores):
            to = ((ring + ring_step) % rings) * cores + (core + core_step) % cores
            pairs.append((ring * cores + core, to))
    return lax.ppermute(array, "ka", pairs)


def dot(a, b, b_dim):
    return lax.dot_general(a, b, (((1,), (b_dim,)), ((), ())), preferred_element_type=jnp.float32)


def copy_rows(source, target, sems):
    step = source.shape[0] // PARTS
    copies = [
        pltpu.make_async_copy(
            source.at[pl.ds(i * step, step)], target.at[pl.ds(i * step, step)], sems.at[i]
        )
        for i in range(PARTS)
    ]
    for copy in copies:
        copy.start()
    return copies


def attend_stage(plan, first, last, ahead, table_ref, q_ref, *refs):
    pb, ka, cores, places, earlier, slots, turned = plan
    count = len(places)
    pieces, refs = refs[:count], refs[count:]
    old_pieces, refs = refs[:ahead], refs[ahead:]
    if not first:
        refs = refs[1:]
    acc, refs = refs[0], refs[1:]
    if last:
        out_ref, refs = refs[0], refs[1:]
    k_pool, v_pool, entries, units, refs = *refs[:4], refs[4:]
    rows = acc.shape[1]
    held, block_rows, _ = pieces[0].shape
    held = held // 2
    group = rows // block_rows
    rings = ka // cores
    own_slots = slots // cores
    p_at, k_at = lax.axis_index("pb"), lax.axis_index("ka")
    ring_at, core_at = k_at // cores, lax.rem(k_at, cores)
    scale = math.log2(math.e) / math.sqrt(HEAD_DIM)
    class_local = held // len(places[0][0]) // cores
    nothing = count * held

    def ids(where):
        found = []
        for hops, y in where:
            ring = lax.rem(ring_at + (rings - y), rings)
            for z in hops:
                source = ring_source(p_at, pb, z)
                for c in range(cores):
                    core = lax.rem(core_at + (cores - c), cores)
                    for t in range(class_local):
                        found.append((source * class_local + t) * ka + ring * cores + core)
        return found

    def pool_from(refs_in, at, k_out, v_out):
        for piece in refs_in:
            for i in range(0, 2 * held, 2 * class_local):
                span = slice(at, at + class_local)
                k_out[span] = piece[i : i + class_local]
                value = piece[i + class_local : i + 2 * class_local]
                v_out[span, :, :HEAD_DIM] = value
                v_out[span, :, HEAD_DIM:] = jnp.ones(value.shape, v_out.dtype)
                at += class_local

    if last:
        mine = lax.rem(core_at + turned, cores) * own_slots
        slot_ids = [mine + i for i in range(own_slots)]
    else:
        slot_ids = list(range(slots))

    row_id = lax.broadcasted_iota(jnp.int32, (block_rows, block_rows), 0)
    col_id = lax.broadcasted_iota(jnp.int32, (block_rows, block_rows), 1)
    pool_from(pieces, 0, k_pool, v_pool)
    k_pool[nothing] = jnp.zeros(k_pool.shape[1:], k_pool.dtype)
    v_pool[nothing] = jnp.zeros(v_pool.shape[1:], v_pool.dtype)
    if first:
        acc[...] = jnp.zeros(acc.shape, acc.dtype)

    blocks = ids(places)
    unit_count = jnp.int32(0)
    for s in slot_ids:
        row = ring_at * slots + s
        own = table_ref[row, 0]
        place = 2 * unit_count
        for index, block in enumerate(blocks):
            entries[place] = jnp.where(block == own, index + nothing + 1, index)
            place = place + table_ref[row, 1 + block]
        entries[place] = nothing
        ends = lax.div(place + 1, 2)

        def mark(u, carry, s=s):
            units[u] = s
            return carry

        lax.fori_loop(unit_count, ends, mark, 0)
        unit_count = ends
    entries[2 * unit_count] = nothing
    entries[2 * unit_count + 1] = nothing
    units[unit_count] = slot_ids[0]

    def query_rows(s):
        return jnp.concatenate(
            [
                q_ref[
                    pl.ds(pl.multiple_of(s * block_rows, block_rows), block_rows),
                    x * HEAD_DIM : (x + 1) * HEAD_DIM,
                ]
                for x in range(group)
            ],
            axis=0,
        )

    def unit_sums(s, index, owns):
        scores = dot(query_rows(s), jnp.concatenate([k_pool[i] for i in index], axis=0), 1)
        power = scores * scale
        if owns is not None:
            reach = jnp.concatenate(
                [
                    jnp.where(col_id <= row_id + jnp.where(own, 0, block_rows), 0.0, HIDDEN)
                    for own in owns
                ],
                axis=1,
            )
            power = power + jnp.concatenate([reach] * group, axis=0)
        weights = jnp.exp2(power).astype(jnp.bfloat16)
        return dot(weights, jnp.concatenate([v_pool[i] for i in index], axis=0), 0)

    def two_units(i, carry):
        raw = [entries[4 * i + j] for j in range(4)]
        owns = [entry > nothing for entry in raw]
        index = [
            jnp.where(own, entry - (nothing + 1), entry) for own, entry in zip(owns, raw)
        ]
        which = [units[2 * i], units[2 * i + 1]]
        some = functools.reduce(jnp.logical_or, owns)

        def take(masked):
            added = [
                unit_sums(
                    which[j],
                    index[2 * j : 2 * j + 2],
                    owns[2 * j : 2 * j + 2] if masked else None,
                )
                for j in range(2)
            ]
            for j in range(2):
                acc[which[j]] += added[j]

        pl.when(some)(functools.partial(take, True))
        pl.when(jnp.logical_not(some))(functools.partial(take, False))
        return carry

    lax.fori_loop(0, lax.div(unit_count + 1, 2), two_units, 0)
    if not last:
        return

    top, k_all, v_all = refs

    def finish(s, i):
        under = acc[s, :, HEAD_DIM:]
        result = (acc[s, :, :HEAD_DIM] / under).astype(out_ref.dtype)
        for x in range(group):
            out_ref[
                i * block_rows : (i + 1) * block_rows, x * HEAD_DIM : (x + 1) * HEAD_DIM
            ] = result[x * block_rows : (x + 1) * block_rows]
        low = high = [under[j : j + 8] for j in range(0, rows, 8)]
        while len(low) > 1:
            low = [functools.reduce(jnp.minimum, low[j : j + 2]) for j in range(0, len(low), 2)]
            high = [functools.reduce(jnp.maximum, high[j : j + 2]) for j in range(0, len(high), 2)]
        return low[0], high[0]

    low, high = zip(*[finish(s, i) for i, s in enumerate(slot_ids)])
    low, high = functools.reduce(jnp.minimum, low), functools.reduce(jnp.maximum, high)
    safe = (low > 2.0**-HEADROOM) & (high < 2.0**HEADROOM)

    @pl.when(jnp.min(jnp.where(safe, 1.0, 0.0)) < 0.5)
    def _():
        pool_from(old_pieces, 0, k_all, v_all)
        pool_from(pieces, len(earlier) * held, k_all, v_all)
        blocks_all = ids(earlier) + blocks
        for i, s in enumerate(slot_ids):
            row = ring_at * slots + s
            own = table_ref[row, 0]
            place = jnp.int32(0)
            for index, block in enumerate(blocks_all):
                entries[place] = jnp.where(block == own, index + len(blocks_all), index)
                place = place + table_ref[row, 1 + block]
            acc[s] = jnp.zeros(acc.shape[1:], acc.dtype)
            top[...] = jnp.full(top.shape, MASKED, top.dtype)

            def one_block(e, carry, s=s):
                is_own = entries[e] >= len(blocks_all)
                index = jnp.where(is_own, entries[e] - len(blocks_all), entries[e])
                reach = jnp.where(
                    col_id <= row_id + jnp.where(is_own, 0, block_rows), 0.0, HIDDEN
                )
                scores = dot(query_rows(s), k_all[index], 1)
                weights, shrinks = [], []
                for x in range(group):
                    span = slice(x * block_rows, (x + 1) * block_rows)
                    power = scores[span] * scale + reach
                    new = jnp.maximum(top[span], jnp.max(power, axis=1, keepdims=True))
                    shrink = jnp.exp2(top[span] - new)
                    top[span] = new
                    weights.append(jnp.exp2(power - new).astype(jnp.bfloat16))
                    shrinks.append(jnp.concatenate([shrink, shrink], axis=1))
                added = dot(jnp.concatenate(weights, axis=0), v_all[index], 0)
                acc[s] = acc[s] * jnp.concatenate(shrinks, axis=0) + added
                return carry

            lax.fori_loop(0, place, one_block, 0)
            finish(s, i)


def split(cores, keys_ref, values_ref, *refs):
    outs, sems = refs[:cores], refs[cores]
    count = keys_ref.shape[0]
    width = outs[0].shape[2]
    core = lax.rem(lax.axis_index("ka"), cores)
    copies = []
    for i, out in enumerate(outs):
        column = pl.multiple_of(lax.rem(core + i, cores) * width, HEAD_DIM)
        for j, ref in enumerate((keys_ref, values_ref)):
            copy = pltpu.make_async_copy(
                ref.at[:, 0, :, pl.ds(column, width)],
                out.at[pl.ds(j * count, count)],
                sems.at[2 * i + j],
            )
            copy.start()
            copies.append(copy)
    for copy in copies:
        copy.wait()


def merge(own_ref, other_ref, queries_ref, both_ref):
    half = own_ref.shape[0]
    both_ref[:half] = own_ref[...]
    both_ref[half:] = other_ref[...]


def fetch(cores, queries_ref, out_ref, sems):
    rows, width = out_ref.shape
    at = lax.axis_index("ka")
    copies = copy_rows(
        queries_ref.at[
            pl.ds(pl.multiple_of(at // cores * rows, HEAD_DIM), rows),
            pl.ds(pl.multiple_of(lax.rem(at, cores) * width, HEAD_DIM), width),
        ],
        out_ref,
        sems,
    )
    for copy in copies:
        copy.wait()


def join(cores, own_ref, other_ref, out_ref, sems):
    width = own_ref.shape[1]
    core = lax.rem(lax.axis_index("ka"), cores)
    copies = []
    for i, ref in enumerate((own_ref, other_ref)):
        at = pl.multiple_of(lax.rem(core + (cores - i), cores) * width, HEAD_DIM)
        copies += copy_rows(ref, out_ref.at[:, pl.ds(at, width)], sems.at[i])
    for copy in copies:
        copy.wait()


def on_device(queries, keys, values, q_order, block_mask):
    pb, ka = lax.axis_size("pb"), lax.axis_size("ka")
    class_local, _, block_rows, kv_width = keys.shape
    cores = 2 if ka % 2 == 0 and kv_width == 2 * HEAD_DIM else 1
    rings = ka // cores
    head_width = kv_width // cores
    width = queries.shape[1] // cores
    rows = width // head_width * block_rows
    own_slots = queries.shape[0] // block_rows // ka
    slots = own_slots * cores

    vmem = pl.BlockSpec(memory_space=pltpu.VMEM)
    smem = pl.BlockSpec(memory_space=pltpu.SMEM)
    hbm = pl.BlockSpec(memory_space=pltpu.HBM)
    anywhere = pl.BlockSpec(memory_space=pl.ANY)
    stages = min(STAGES, pb)
    sources = pb // stages

    table = jnp.concatenate([q_order[:, None], block_mask], axis=1)
    part = jax.ShapeDtypeStruct((2 * class_local, block_rows, head_width), keys.dtype)
    starts = pl.pallas_call(
        functools.partial(split, cores),
        out_shape=[part] * cores,
        in_specs=[anywhere] * 2,
        out_specs=[vmem] * cores,
        scratch_shapes=[pltpu.SemaphoreType.DMA((2 * cores,))],
        compiler_params=pltpu.CompilerParams(vmem_limit_bytes=54 * 2**20),
    )(keys, values)
    own_queries = pl.pallas_call(
        functools.partial(fetch, cores),
        out_shape=jax.ShapeDtypeStruct((slots * block_rows, width), queries.dtype),
        in_specs=[anywhere],
        out_specs=vmem,
        scratch_shapes=[pltpu.SemaphoreType.DMA((PARTS,))],
        compiler_params=pltpu.CompilerParams(vmem_limit_bytes=50 * 2**20),
    )(queries)
    if cores == 2:
        starts = [starts[0], turn(starts[1], ka, cores, 0, 1)]

    held = cores * 2 * class_local
    start = starts[0]
    if cores == 2:
        start = pl.pallas_call(
            merge,
            out_shape=jax.ShapeDtypeStruct((held, block_rows, head_width), keys.dtype),
            in_specs=[vmem] * 2 + [anywhere],
            out_specs=vmem,
            compiler_params=pltpu.CompilerParams(vmem_limit_bytes=SMALL * 2**20),
        )(start, starts[1], own_queries)

    def call(first, last, turned, pieces, places, earlier, own_queries, state, extra):
        held = len(places) * sources * cores * class_local
        everything = held + len(earlier) * sources * cores * class_local
        here = own_slots if last else slots
        outs = [jax.ShapeDtypeStruct((slots, rows, 2 * HEAD_DIM), jnp.float32)]
        scratch = [
            pltpu.VMEM((held + 1, block_rows, HEAD_DIM), jnp.bfloat16),
            pltpu.VMEM((held + 1, block_rows, 2 * HEAD_DIM), jnp.bfloat16),
            pltpu.SMEM((max(here * (held + 1) + 2, everything + 1),), jnp.int32),
            pltpu.SMEM((here * (held // 2 + 1) + 1,), jnp.int32),
        ]
        if last:
            outs.append(jax.ShapeDtypeStruct((own_slots * block_rows, width), queries.dtype))
            scratch += [
                pltpu.VMEM((rows, HEAD_DIM), jnp.float32),
                pltpu.VMEM((everything, block_rows, HEAD_DIM), jnp.bfloat16),
                pltpu.VMEM((everything, block_rows, 2 * HEAD_DIM), jnp.bfloat16),
            ]
        pooled = held + (everything if last else 0)
        room = LIMIT * 2**20 + pooled * block_rows * HEAD_DIM * 6
        state_at = 2 + len(places) + len(extra)
        return pl.pallas_call(
            functools.partial(
                attend_stage,
                (pb, ka, cores, places, earlier, slots, turned),
                first,
                last,
                len(extra),
            ),
            out_shape=outs,
            in_specs=[smem]
            + [vmem] * (1 + len(places))
            + [vmem if last else anywhere] * len(extra)
            + [vmem] * len(state),
            out_specs=[vmem] * len(outs),
            input_output_aliases={state_at + i: i for i in range(len(state))},
            scratch_shapes=scratch,
            compiler_params=pltpu.CompilerParams(vmem_limit_bytes=room),
            cost_estimate=pl.CostEstimate(
                flops=2**31, bytes_accessed=2**22, transcendentals=2**20
            ),
        )(table, own_queries, *pieces, *extra, *state)

    def along(array, count):
        found = []
        for _ in range(count):
            array = along_ring(array, pb)
            found.append(array)
        return found

    def stacked(arrays):
        return arrays[0] if len(arrays) == 1 else jnp.concatenate(arrays, axis=0)

    def beside(array):
        found = [array]
        for _ in range(rings - 1):
            found.append(turn(found[-1], ka, cores, 1, 0))
        return found

    hops = [range(stage * sources, (stage + 1) * sources) for stage in range(stages)]
    placed = [[(hops[stage], y) for y in range(rings)] for stage in range(stages)]
    state, earlier, before = [], [], []
    arrived = [start] + along(start, sources - 1)
    ready = None
    for stage in range(stages):
        if ready is not None:
            arrived, ready, state = lax.optimization_barrier((arrived, ready, state))
        pieces = beside(stacked(arrived))
        if stage < stages - 1:
            arrived = along(arrived[-1], sources)
        if ready is not None:
            state = call(
                stage == 1, False, 0, ready, placed[stage - 1], earlier, own_queries, state,
                [pieces[0]],
            )
            earlier, before = earlier + placed[stage - 1], before + ready
        ready = pieces
    places, pieces = placed[-1], ready
    halves = []
    for c in reversed(range(cores)):
        *state, half = call(False, True, c, pieces, places, earlier, own_queries, state, before)
        halves.append(half)
    if cores == 1:
        return halves[0]
    return pl.pallas_call(
        functools.partial(join, cores),
        out_shape=jax.ShapeDtypeStruct((own_slots * block_rows, cores * width), queries.dtype),
        in_specs=[vmem] * 2,
        out_specs=anywhere,
        scratch_shapes=[pltpu.SemaphoreType.DMA((cores, PARTS))],
        compiler_params=pltpu.CompilerParams(vmem_limit_bytes=SMALL * 2**20),
    )(halves[1], turn(halves[0], ka, cores, 0, 1))


def solution(mesh):
    in_specs = (
        P("pb", "ha"),
        P("pb", "ka", None, "ha"),
        P("pb", "ka", None, "ha"),
        P("pb"),
        P("pb", None),
    )
    out_specs = P(("pb", "ka"), "ha")
    return jax.shard_map(
        on_device, mesh=mesh, in_specs=in_specs, out_specs=out_specs, check_vma=False
    )
```

```python
import functools
import math

import jax
import jax.numpy as jnp
from jax import lax
from jax.experimental import pallas as pl
from jax.experimental.pallas import tpu as pltpu
from jax.sharding import PartitionSpec as P

HEAD_DIM = 128
MASKED = -1e30
HIDDEN = -1e38
HEADROOM = 64.0
PARTS = 8
LIMIT = 10
SMALL = 4
STAGES = 4


def folded(size):
    return list(range(0, size, 2)) + list(range(1, size, 2))[::-1]


def along_ring(array, size):
    ring = folded(size)
    return lax.ppermute(array, "pb", [(ring[i], ring[(i + 1) % size]) for i in range(size)])


def ring_source(at, size, hops):
    place = jnp.where(at % 2 == 0, at // 2, size - 1 - at // 2)
    place = lax.rem(place + (size - hops), size)
    return jnp.where(place < (size + 1) // 2, 2 * place, 2 * (size - 1 - place) + 1)


def turn(array, size, cores, ring_step, core_step):
    rings = size // cores
    pairs = []
    for ring in range(rings):
        for core in range(cores):
            to = ((ring + ring_step) % rings) * cores + (core + core_step) % cores
            pairs.append((ring * cores + core, to))
    return lax.ppermute(array, "ka", pairs)


def dot(a, b, b_dim):
    return lax.dot_general(a, b, (((1,), (b_dim,)), ((), ())), preferred_element_type=jnp.float32)


def copy_rows(source, target, sems):
    step = source.shape[0] // PARTS
    copies = [
        pltpu.make_async_copy(
            source.at[pl.ds(i * step, step)], target.at[pl.ds(i * step, step)], sems.at[i]
        )
        for i in range(PARTS)
    ]
    for copy in copies:
        copy.start()
    return copies


def attend_stage(plan, first, last, ahead, table_ref, q_ref, *refs):
    pb, ka, cores, places, earlier, slots, turned = plan
    count = len(places)
    pieces, refs = refs[:count], refs[count:]
    old_pieces, refs = refs[:ahead], refs[ahead:]
    if not first:
        refs = refs[1:]
    acc, refs = refs[0], refs[1:]
    if last:
        out_ref, refs = refs[0], refs[1:]
    k_pool, v_pool, held_weights, entries, units, refs = *refs[:5], refs[5:]
    rows = acc.shape[1]
    held, block_rows, _ = pieces[0].shape
    held = held // 2
    group = rows // block_rows
    rings = ka // cores
    own_slots = slots // cores
    p_at, k_at = lax.axis_index("pb"), lax.axis_index("ka")
    ring_at, core_at = k_at // cores, lax.rem(k_at, cores)
    scale = math.log2(math.e) / math.sqrt(HEAD_DIM)
    class_local = held // len(places[0][0]) // cores
    nothing = count * held

    def ids(where):
        found = []
        for hops, y in where:
            ring = lax.rem(ring_at + (rings - y), rings)
            for z in hops:
                source = ring_source(p_at, pb, z)
                for c in range(cores):
                    core = lax.rem(core_at + (cores - c), cores)
                    for t in range(class_local):
                        found.append((source * class_local + t) * ka + ring * cores + core)
        return found

    def pool_from(refs_in, at, k_out, v_out):
        for piece in refs_in:
            for i in range(0, 2 * held, 2 * class_local):
                span = slice(at, at + class_local)
                k_out[span] = piece[i : i + class_local]
                value = piece[i + class_local : i + 2 * class_local]
                v_out[span, :, :HEAD_DIM] = value
                v_out[span, :, HEAD_DIM:] = jnp.ones(value.shape, v_out.dtype)
                at += class_local

    if last:
        mine = lax.rem(core_at + turned, cores) * own_slots
        slot_ids = [mine + i for i in range(own_slots)]
    else:
        slot_ids = list(range(slots))

    row_id = lax.broadcasted_iota(jnp.int32, (block_rows, block_rows), 0)
    col_id = lax.broadcasted_iota(jnp.int32, (block_rows, block_rows), 1)
    pool_from(pieces, 0, k_pool, v_pool)
    k_pool[nothing] = jnp.zeros(k_pool.shape[1:], k_pool.dtype)
    v_pool[nothing] = jnp.zeros(v_pool.shape[1:], v_pool.dtype)

    blocks = ids(places)
    unit_count = jnp.int32(0)
    for s in slot_ids:
        row = ring_at * slots + s
        own = table_ref[row, 0]
        place = 2 * unit_count
        for index, block in enumerate(blocks):
            entries[place] = jnp.where(block == own, index + nothing + 1, index)
            place = place + table_ref[row, 1 + block]
        entries[place] = nothing
        ends = lax.div(place + 1, 2)
        if first:

            @pl.when(ends == unit_count)
            def _(s=s):
                acc[s] = jnp.zeros(acc.shape[1:], acc.dtype)


        def mark(u, carry, s=s):
            units[u] = s
            return carry

        lax.fori_loop(unit_count, ends, mark, 0)
        unit_count = ends
    def query_rows(s):
        return jnp.concatenate(
            [
                q_ref[
                    pl.ds(pl.multiple_of(s * block_rows, block_rows), block_rows),
                    x * HEAD_DIM : (x + 1) * HEAD_DIM,
                ]
                for x in range(group)
            ],
            axis=0,
        )

    def pair_of(u):
        raw = [entries[2 * u], entries[2 * u + 1]]
        owns = [entry > nothing for entry in raw]
        return owns, [jnp.where(o, e - (nothing + 1), e) for o, e in zip(owns, raw)]

    def weigh(u):
        owns, index = pair_of(u)
        keys = jnp.concatenate([k_pool[i] for i in index], axis=0)
        reach = jnp.concatenate(
            [
                jnp.where(col_id <= row_id + jnp.where(own, 0, block_rows), 0.0, HIDDEN)
                for own in owns
            ],
            axis=1,
        )
        power = dot(query_rows(units[u]), keys, 1) * scale
        power = power + jnp.concatenate([reach] * group, axis=0)
        held_weights[...] = jnp.exp2(power).astype(held_weights.dtype)

    def add(u):
        _, index = pair_of(u)
        s = units[u]
        values = jnp.concatenate([v_pool[i] for i in index], axis=0)
        added = dot(held_weights[...], values, 0)
        old = acc[s]
        if first:
            fresh = (u == 0) | (units[jnp.maximum(u - 1, 0)] != s)
            old = jnp.where(fresh, 0.0, old)
        acc[s] = old + added

    @pl.when(unit_count > 0)
    def _():
        weigh(0)

        def both(u, carry):
            add(u)
            weigh(u + 1)
            return carry

        lax.fori_loop(0, unit_count - 1, both, 0)
        add(unit_count - 1)

    if not last:
        return

    top, k_all, v_all = refs

    def finish(s, i):
        under = acc[s, :, HEAD_DIM:]
        result = (acc[s, :, :HEAD_DIM] / under).astype(out_ref.dtype)
        for x in range(group):
            out_ref[
                i * block_rows : (i + 1) * block_rows, x * HEAD_DIM : (x + 1) * HEAD_DIM
            ] = result[x * block_rows : (x + 1) * block_rows]
        low = high = [under[j : j + 8] for j in range(0, rows, 8)]
        while len(low) > 1:
            low = [functools.reduce(jnp.minimum, low[j : j + 2]) for j in range(0, len(low), 2)]
            high = [functools.reduce(jnp.maximum, high[j : j + 2]) for j in range(0, len(high), 2)]
        return low[0], high[0]

    low, high = zip(*[finish(s, i) for i, s in enumerate(slot_ids)])
    low, high = functools.reduce(jnp.minimum, low), functools.reduce(jnp.maximum, high)
    safe = (low > 2.0**-HEADROOM) & (high < 2.0**HEADROOM)

    @pl.when(jnp.min(jnp.where(safe, 1.0, 0.0)) < 0.5)
    def _():
        pool_from(old_pieces, 0, k_all, v_all)
        pool_from(pieces, len(earlier) * held, k_all, v_all)
        blocks_all = ids(earlier) + blocks
        for i, s in enumerate(slot_ids):
            row = ring_at * slots + s
            own = table_ref[row, 0]
            place = jnp.int32(0)
            for index, block in enumerate(blocks_all):
                entries[place] = jnp.where(block == own, index + len(blocks_all), index)
                place = place + table_ref[row, 1 + block]
            acc[s] = jnp.zeros(acc.shape[1:], acc.dtype)
            top[...] = jnp.full(top.shape, MASKED, top.dtype)

            def one_block(e, carry, s=s):
                is_own = entries[e] >= len(blocks_all)
                index = jnp.where(is_own, entries[e] - len(blocks_all), entries[e])
                reach = jnp.where(
                    col_id <= row_id + jnp.where(is_own, 0, block_rows), 0.0, HIDDEN
                )
                scores = dot(query_rows(s), k_all[index], 1)
                weights, shrinks = [], []
                for x in range(group):
                    span = slice(x * block_rows, (x + 1) * block_rows)
                    power = scores[span] * scale + reach
                    new = jnp.maximum(top[span], jnp.max(power, axis=1, keepdims=True))
                    shrink = jnp.exp2(top[span] - new)
                    top[span] = new
                    weights.append(jnp.exp2(power - new).astype(jnp.bfloat16))
                    shrinks.append(jnp.concatenate([shrink, shrink], axis=1))
                added = dot(jnp.concatenate(weights, axis=0), v_all[index], 0)
                acc[s] = acc[s] * jnp.concatenate(shrinks, axis=0) + added
                return carry

            lax.fori_loop(0, place, one_block, 0)
            finish(s, i)


def split(cores, keys_ref, values_ref, *refs):
    outs, sems = refs[:cores], refs[cores]
    count = keys_ref.shape[0]
    width = outs[0].shape[2]
    core = lax.rem(lax.axis_index("ka"), cores)
    copies = []
    for i, out in enumerate(outs):
        column = pl.multiple_of(lax.rem(core + i, cores) * width, HEAD_DIM)
        for j, ref in enumerate((keys_ref, values_ref)):
            copy = pltpu.make_async_copy(
                ref.at[:, 0, :, pl.ds(column, width)],
                out.at[pl.ds(j * count, count)],
                sems.at[2 * i + j],
            )
            copy.start()
            copies.append(copy)
    for copy in copies:
        copy.wait()


def merge(own_ref, other_ref, queries_ref, both_ref):
    half = own_ref.shape[0]
    both_ref[:half] = own_ref[...]
    both_ref[half:] = other_ref[...]


def fetch(cores, queries_ref, out_ref, sems):
    rows, width = out_ref.shape
    at = lax.axis_index("ka")
    copies = copy_rows(
        queries_ref.at[
            pl.ds(pl.multiple_of(at // cores * rows, HEAD_DIM), rows),
            pl.ds(pl.multiple_of(lax.rem(at, cores) * width, HEAD_DIM), width),
        ],
        out_ref,
        sems,
    )
    for copy in copies:
        copy.wait()


def join(cores, own_ref, other_ref, out_ref, sems):
    width = own_ref.shape[1]
    core = lax.rem(lax.axis_index("ka"), cores)
    copies = []
    for i, ref in enumerate((own_ref, other_ref)):
        at = pl.multiple_of(lax.rem(core + (cores - i), cores) * width, HEAD_DIM)
        copies += copy_rows(ref, out_ref.at[:, pl.ds(at, width)], sems.at[i])
    for copy in copies:
        copy.wait()


def on_device(queries, keys, values, q_order, block_mask):
    pb, ka = lax.axis_size("pb"), lax.axis_size("ka")
    class_local, _, block_rows, kv_width = keys.shape
    cores = 2 if ka % 2 == 0 and kv_width == 2 * HEAD_DIM else 1
    rings = ka // cores
    head_width = kv_width // cores
    width = queries.shape[1] // cores
    rows = width // head_width * block_rows
    own_slots = queries.shape[0] // block_rows // ka
    slots = own_slots * cores

    vmem = pl.BlockSpec(memory_space=pltpu.VMEM)
    smem = pl.BlockSpec(memory_space=pltpu.SMEM)
    hbm = pl.BlockSpec(memory_space=pltpu.HBM)
    anywhere = pl.BlockSpec(memory_space=pl.ANY)
    stages = min(STAGES, pb)
    sources = pb // stages

    table = jnp.concatenate([q_order[:, None], block_mask], axis=1)
    part = jax.ShapeDtypeStruct((2 * class_local, block_rows, head_width), keys.dtype)
    starts = pl.pallas_call(
        functools.partial(split, cores),
        out_shape=[part] * cores,
        in_specs=[anywhere] * 2,
        out_specs=[vmem] * cores,
        scratch_shapes=[pltpu.SemaphoreType.DMA((2 * cores,))],
        compiler_params=pltpu.CompilerParams(vmem_limit_bytes=54 * 2**20),
    )(keys, values)
    own_queries = pl.pallas_call(
        functools.partial(fetch, cores),
        out_shape=jax.ShapeDtypeStruct((slots * block_rows, width), queries.dtype),
        in_specs=[anywhere],
        out_specs=vmem,
        scratch_shapes=[pltpu.SemaphoreType.DMA((PARTS,))],
        compiler_params=pltpu.CompilerParams(vmem_limit_bytes=50 * 2**20),
    )(queries)
    if cores == 2:
        starts = [starts[0], turn(starts[1], ka, cores, 0, 1)]

    held = cores * 2 * class_local
    start = starts[0]
    if cores == 2:
        start = pl.pallas_call(
            merge,
            out_shape=jax.ShapeDtypeStruct((held, block_rows, head_width), keys.dtype),
            in_specs=[vmem] * 2 + [anywhere],
            out_specs=vmem,
            compiler_params=pltpu.CompilerParams(vmem_limit_bytes=SMALL * 2**20),
        )(start, starts[1], own_queries)

    def call(first, last, turned, pieces, places, earlier, own_queries, state, extra):
        held = len(places) * sources * cores * class_local
        everything = held + len(earlier) * sources * cores * class_local
        here = own_slots if last else slots
        outs = [jax.ShapeDtypeStruct((slots, rows, 2 * HEAD_DIM), jnp.float32)]
        scratch = [
            pltpu.VMEM((held + 1, block_rows, HEAD_DIM), jnp.bfloat16),
            pltpu.VMEM((held + 1, block_rows, 2 * HEAD_DIM), jnp.bfloat16),
            pltpu.VMEM((rows, 2 * block_rows), jnp.bfloat16),
            pltpu.SMEM((max(here * (held + 1) + 1, everything + 1),), jnp.int32),
            pltpu.SMEM((here * (held // 2 + 1),), jnp.int32),
        ]
        if last:
            outs.append(jax.ShapeDtypeStruct((own_slots * block_rows, width), queries.dtype))
            scratch += [
                pltpu.VMEM((rows, HEAD_DIM), jnp.float32),
                pltpu.VMEM((everything, block_rows, HEAD_DIM), jnp.bfloat16),
                pltpu.VMEM((everything, block_rows, 2 * HEAD_DIM), jnp.bfloat16),
            ]
        pooled = held + (everything if last else 0)
        room = LIMIT * 2**20 + pooled * block_rows * HEAD_DIM * 6
        state_at = 2 + len(places) + len(extra)
        return pl.pallas_call(
            functools.partial(
                attend_stage,
                (pb, ka, cores, places, earlier, slots, turned),
                first,
                last,
                len(extra),
            ),
            out_shape=outs,
            in_specs=[smem]
            + [vmem] * (1 + len(places))
            + [vmem if last else anywhere] * len(extra)
            + [vmem] * len(state),
            out_specs=[vmem] * len(outs),
            input_output_aliases={state_at + i: i for i in range(len(state))},
            scratch_shapes=scratch,
            compiler_params=pltpu.CompilerParams(vmem_limit_bytes=room),
            cost_estimate=pl.CostEstimate(
                flops=2**31, bytes_accessed=2**22, transcendentals=2**20
            ),
        )(table, own_queries, *pieces, *extra, *state)

    def along(array, count):
        found = []
        for _ in range(count):
            array = along_ring(array, pb)
            found.append(array)
        return found

    def stacked(arrays):
        return arrays[0] if len(arrays) == 1 else jnp.concatenate(arrays, axis=0)

    def beside(array):
        found = [array]
        for _ in range(rings - 1):
            found.append(turn(found[-1], ka, cores, 1, 0))
        return found

    hops = [range(stage * sources, (stage + 1) * sources) for stage in range(stages)]
    placed = [[(hops[stage], y) for y in range(rings)] for stage in range(stages)]
    state, earlier, before = [], [], []
    arrived = [start] + along(start, sources - 1)
    ready = None
    for stage in range(stages):
        if ready is not None:
            arrived, ready, state = lax.optimization_barrier((arrived, ready, state))
        pieces = beside(stacked(arrived))
        if stage < stages - 1:
            arrived = along(arrived[-1], sources)
        if ready is not None:
            state = call(
                stage == 1, False, 0, ready, placed[stage - 1], earlier, own_queries, state,
                [pieces[0]],
            )
            earlier, before = earlier + placed[stage - 1], before + ready
        ready = pieces
    places, pieces = placed[-1], ready
    halves = []
    for c in reversed(range(cores)):
        *state, half = call(False, True, c, pieces, places, earlier, own_queries, state, before)
        halves.append(half)
    if cores == 1:
        return halves[0]
    return pl.pallas_call(
        functools.partial(join, cores),
        out_shape=jax.ShapeDtypeStruct((own_slots * block_rows, cores * width), queries.dtype),
        in_specs=[vmem] * 2,
        out_specs=anywhere,
        scratch_shapes=[pltpu.SemaphoreType.DMA((cores, PARTS))],
        compiler_params=pltpu.CompilerParams(vmem_limit_bytes=SMALL * 2**20),
    )(halves[1], turn(halves[0], ka, cores, 0, 1))


def solution(mesh):
    in_specs = (
        P("pb", "ha"),
        P("pb", "ka", None, "ha"),
        P("pb", "ka", None, "ha"),
        P("pb"),
        P("pb", None),
    )
    out_specs = P(("pb", "ka"), "ha")
    return jax.shard_map(
        on_device, mesh=mesh, in_specs=in_specs, out_specs=out_specs, check_vma=False
    )
```

```python
import functools
import math

import jax
import jax.numpy as jnp
from jax import lax
from jax.experimental import pallas as pl
from jax.experimental.pallas import tpu as pltpu
from jax.sharding import PartitionSpec as P

HEAD_DIM = 128
MASKED = -1e30
HIDDEN = -1e38
HEADROOM = 64.0
PARTS = 8
LIMIT = 10
SMALL = 4
STAGES = 4


def folded(size):
    return list(range(0, size, 2)) + list(range(1, size, 2))[::-1]


def along_ring(array, size):
    ring = folded(size)
    return lax.ppermute(array, "pb", [(ring[i], ring[(i + 1) % size]) for i in range(size)])


def ring_source(at, size, hops):
    place = jnp.where(at % 2 == 0, at // 2, size - 1 - at // 2)
    place = lax.rem(place + (size - hops), size)
    return jnp.where(place < (size + 1) // 2, 2 * place, 2 * (size - 1 - place) + 1)


def turn(array, size, cores, ring_step, core_step):
    rings = size // cores
    pairs = []
    for ring in range(rings):
        for core in range(cores):
            to = ((ring + ring_step) % rings) * cores + (core + core_step) % cores
            pairs.append((ring * cores + core, to))
    return lax.ppermute(array, "ka", pairs)


def dot(a, b, b_dim):
    return lax.dot_general(a, b, (((1,), (b_dim,)), ((), ())), preferred_element_type=jnp.float32)


def copy_rows(source, target, sems):
    step = source.shape[0] // PARTS
    copies = [
        pltpu.make_async_copy(
            source.at[pl.ds(i * step, step)], target.at[pl.ds(i * step, step)], sems.at[i]
        )
        for i in range(PARTS)
    ]
    for copy in copies:
        copy.start()
    return copies


def attend_stage(plan, first, last, ahead, table_ref, q_ref, *refs):
    pb, ka, cores, class_local, places, earlier, slots, turned = plan
    count = len(places)
    pieces, refs = refs[:count], refs[count:]
    old_pieces, refs = refs[:ahead], refs[ahead:]
    if not first:
        refs = refs[1:]
    acc, refs = refs[0], refs[1:]
    if last:
        out_ref, refs = refs[0], refs[1:]
    k_pool, v_pool, held_weights, entries, units, refs = *refs[:5], refs[5:]
    rows = acc.shape[1]
    block_rows = q_ref.shape[0] // slots
    group = rows // block_rows
    rings = ka // cores
    own_slots = slots // cores
    p_at, k_at = lax.axis_index("pb"), lax.axis_index("ka")
    ring_at, core_at = k_at // cores, lax.rem(k_at, cores)
    scale = math.log2(math.e) / math.sqrt(HEAD_DIM)

    def ids(where):
        found = []
        for hops, y, offsets in where:
            ring = lax.rem(ring_at + (rings - y), rings)
            for z in hops:
                source = ring_source(p_at, pb, z)
                for c in offsets:
                    core = lax.rem(core_at + (cores - c), cores)
                    for t in range(class_local):
                        found.append((source * class_local + t) * ka + ring * cores + core)
        return found

    def pool_from(refs_in, at, k_out, v_out):
        for piece in refs_in:
            for i in range(0, piece.shape[0], 2 * class_local):
                span = slice(at, at + class_local)
                k_out[span] = piece[i : i + class_local]
                value = piece[i + class_local : i + 2 * class_local]
                v_out[span, :, :HEAD_DIM] = value
                v_out[span, :, HEAD_DIM:] = jnp.ones(value.shape, v_out.dtype)
                at += class_local

    nothing = sum(piece.shape[0] for piece in pieces) // 2

    if last:
        mine = lax.rem(core_at + turned, cores) * own_slots
        slot_ids = [mine + i for i in range(own_slots)]
    else:
        slot_ids = list(range(slots))

    row_id = lax.broadcasted_iota(jnp.int32, (block_rows, block_rows), 0)
    col_id = lax.broadcasted_iota(jnp.int32, (block_rows, block_rows), 1)
    pool_from(pieces, 0, k_pool, v_pool)
    k_pool[nothing] = jnp.zeros(k_pool.shape[1:], k_pool.dtype)
    v_pool[nothing] = jnp.zeros(v_pool.shape[1:], v_pool.dtype)

    blocks = ids(places)
    unit_count = jnp.int32(0)
    for s in slot_ids:
        row = ring_at * slots + s
        own = table_ref[row, 0]
        place = 2 * unit_count
        for index, block in enumerate(blocks):
            entries[place] = jnp.where(block == own, index + nothing + 1, index)
            place = place + table_ref[row, 1 + block]
        entries[place] = nothing
        ends = lax.div(place + 1, 2)
        if first:

            @pl.when(ends == unit_count)
            def _(s=s):
                acc[s] = jnp.zeros(acc.shape[1:], acc.dtype)


        def mark(u, carry, s=s):
            units[u] = s
            return carry

        lax.fori_loop(unit_count, ends, mark, 0)
        unit_count = ends
    def query_rows(s):
        return jnp.concatenate(
            [
                q_ref[
                    pl.ds(pl.multiple_of(s * block_rows, block_rows), block_rows),
                    x * HEAD_DIM : (x + 1) * HEAD_DIM,
                ]
                for x in range(group)
            ],
            axis=0,
        )

    def pair_of(u):
        raw = [entries[2 * u], entries[2 * u + 1]]
        owns = [entry > nothing for entry in raw]
        return owns, [jnp.where(o, e - (nothing + 1), e) for o, e in zip(owns, raw)]

    def weigh(u):
        owns, index = pair_of(u)
        keys = jnp.concatenate([k_pool[i] for i in index], axis=0)
        reach = jnp.concatenate(
            [
                jnp.where(col_id <= row_id + jnp.where(own, 0, block_rows), 0.0, HIDDEN)
                for own in owns
            ],
            axis=1,
        )
        power = dot(query_rows(units[u]), keys, 1) * scale
        power = power + jnp.concatenate([reach] * group, axis=0)
        held_weights[...] = jnp.exp2(power).astype(held_weights.dtype)

    def add(u):
        _, index = pair_of(u)
        s = units[u]
        values = jnp.concatenate([v_pool[i] for i in index], axis=0)
        added = dot(held_weights[...], values, 0)
        old = acc[s]
        if first:
            fresh = (u == 0) | (units[jnp.maximum(u - 1, 0)] != s)
            old = jnp.where(fresh, 0.0, old)
        acc[s] = old + added

    @pl.when(unit_count > 0)
    def _():
        weigh(0)

        def both(u, carry):
            add(u)
            weigh(u + 1)
            return carry

        lax.fori_loop(0, unit_count - 1, both, 0)
        add(unit_count - 1)

    if not last:
        return

    top, k_all, v_all = refs

    def finish(s, i):
        under = acc[s, :, HEAD_DIM:]
        result = (acc[s, :, :HEAD_DIM] / under).astype(out_ref.dtype)
        for x in range(group):
            out_ref[
                i * block_rows : (i + 1) * block_rows, x * HEAD_DIM : (x + 1) * HEAD_DIM
            ] = result[x * block_rows : (x + 1) * block_rows]
        low = high = [under[j : j + 8] for j in range(0, rows, 8)]
        while len(low) > 1:
            low = [functools.reduce(jnp.minimum, low[j : j + 2]) for j in range(0, len(low), 2)]
            high = [functools.reduce(jnp.maximum, high[j : j + 2]) for j in range(0, len(high), 2)]
        return low[0], high[0]

    low, high = zip(*[finish(s, i) for i, s in enumerate(slot_ids)])
    low, high = functools.reduce(jnp.minimum, low), functools.reduce(jnp.maximum, high)
    safe = (low > 2.0**-HEADROOM) & (high < 2.0**HEADROOM)

    @pl.when(jnp.min(jnp.where(safe, 1.0, 0.0)) < 0.5)
    def _():
        pool_from(old_pieces, 0, k_all, v_all)
        pool_from(pieces, sum(p.shape[0] for p in old_pieces) // 2, k_all, v_all)
        blocks_all = ids(earlier) + blocks
        for i, s in enumerate(slot_ids):
            row = ring_at * slots + s
            own = table_ref[row, 0]
            place = jnp.int32(0)
            for index, block in enumerate(blocks_all):
                entries[place] = jnp.where(block == own, index + len(blocks_all), index)
                place = place + table_ref[row, 1 + block]
            acc[s] = jnp.zeros(acc.shape[1:], acc.dtype)
            top[...] = jnp.full(top.shape, MASKED, top.dtype)

            def one_block(e, carry, s=s):
                is_own = entries[e] >= len(blocks_all)
                index = jnp.where(is_own, entries[e] - len(blocks_all), entries[e])
                reach = jnp.where(
                    col_id <= row_id + jnp.where(is_own, 0, block_rows), 0.0, HIDDEN
                )
                scores = dot(query_rows(s), k_all[index], 1)
                weights, shrinks = [], []
                for x in range(group):
                    span = slice(x * block_rows, (x + 1) * block_rows)
                    power = scores[span] * scale + reach
                    new = jnp.maximum(top[span], jnp.max(power, axis=1, keepdims=True))
                    shrink = jnp.exp2(top[span] - new)
                    top[span] = new
                    weights.append(jnp.exp2(power - new).astype(jnp.bfloat16))
                    shrinks.append(jnp.concatenate([shrink, shrink], axis=1))
                added = dot(jnp.concatenate(weights, axis=0), v_all[index], 0)
                acc[s] = acc[s] * jnp.concatenate(shrinks, axis=0) + added
                return carry

            lax.fori_loop(0, place, one_block, 0)
            finish(s, i)


def cut(cores, *refs):
    ins, out_ref = refs[:-1], refs[-1]
    count = ins[0].shape[0]
    width = out_ref.shape[2]
    core = lax.rem(lax.axis_index("ka"), cores)
    for c in range(cores):

        @pl.when(core == c)
        def _():
            for i, ref in enumerate(ins):
                out_ref[i * count : (i + 1) * count] = ref[
                    :, 0, :, c * width : (c + 1) * width
                ]


def fetch(cores, queries_ref, out_ref, sems):
    rows, width = out_ref.shape
    at = lax.axis_index("ka")
    copies = copy_rows(
        queries_ref.at[
            pl.ds(pl.multiple_of(at // cores * rows, HEAD_DIM), rows),
            pl.ds(pl.multiple_of(lax.rem(at, cores) * width, HEAD_DIM), width),
        ],
        out_ref,
        sems,
    )
    for copy in copies:
        copy.wait()


def join(cores, own_ref, other_ref, out_ref, sems):
    width = own_ref.shape[1]
    core = lax.rem(lax.axis_index("ka"), cores)
    copies = []
    for i, ref in enumerate((own_ref, other_ref)):
        at = pl.multiple_of(lax.rem(core + (cores - i), cores) * width, HEAD_DIM)
        copies += copy_rows(ref, out_ref.at[:, pl.ds(at, width)], sems.at[i])
    for copy in copies:
        copy.wait()


def on_device(queries, keys, values, q_order, block_mask):
    pb, ka = lax.axis_size("pb"), lax.axis_size("ka")
    class_local, _, block_rows, kv_width = keys.shape
    cores = 2 if ka % 2 == 0 and kv_width == 2 * HEAD_DIM else 1
    rings = ka // cores
    head_width = kv_width // cores
    width = queries.shape[1] // cores
    rows = width // head_width * block_rows
    own_slots = queries.shape[0] // block_rows // ka
    slots = own_slots * cores

    vmem = pl.BlockSpec(memory_space=pltpu.VMEM)
    smem = pl.BlockSpec(memory_space=pltpu.SMEM)

    anywhere = pl.BlockSpec(memory_space=pl.ANY)
    stages = min(STAGES, pb)
    sources = pb // stages

    table = jnp.concatenate([q_order[:, None], block_mask], axis=1)
    own_queries = pl.pallas_call(
        functools.partial(fetch, cores),
        out_shape=jax.ShapeDtypeStruct((slots * block_rows, width), queries.dtype),
        in_specs=[anywhere],
        out_specs=vmem,
        scratch_shapes=[pltpu.SemaphoreType.DMA((PARTS,))],
        compiler_params=pltpu.CompilerParams(vmem_limit_bytes=50 * 2**20),
    )(queries)
    raw = [keys, values]
    for c in range(1, cores):
        raw += [turn(keys, ka, cores, 0, c), turn(values, ka, cores, 0, c)]
    start = pl.pallas_call(
        functools.partial(cut, cores),
        out_shape=jax.ShapeDtypeStruct(
            (2 * cores * class_local, block_rows, head_width), keys.dtype
        ),
        in_specs=[vmem] * len(raw),
        out_specs=vmem,
        compiler_params=pltpu.CompilerParams(vmem_limit_bytes=SMALL * 2**20),
    )(*raw)

    def blocks_of(where):
        return sum(len(hops) * len(offsets) * class_local for hops, _, offsets in where)

    def call(first, last, turned, pieces, places, earlier, own_queries, state, extra):
        held = blocks_of(places)
        everything = held + blocks_of(earlier)
        here = own_slots if last else slots
        outs = [jax.ShapeDtypeStruct((slots, rows, 2 * HEAD_DIM), jnp.float32)]
        scratch = [
            pltpu.VMEM((held + 1, block_rows, HEAD_DIM), jnp.bfloat16),
            pltpu.VMEM((held + 1, block_rows, 2 * HEAD_DIM), jnp.bfloat16),
            pltpu.VMEM((rows, 2 * block_rows), jnp.bfloat16),
            pltpu.SMEM((max(here * (held + 1) + 1, everything + 1),), jnp.int32),
            pltpu.SMEM((here * (held // 2 + 1),), jnp.int32),
        ]
        if last:
            outs.append(jax.ShapeDtypeStruct((own_slots * block_rows, width), queries.dtype))
            scratch += [
                pltpu.VMEM((rows, HEAD_DIM), jnp.float32),
                pltpu.VMEM((everything, block_rows, HEAD_DIM), jnp.bfloat16),
                pltpu.VMEM((everything, block_rows, 2 * HEAD_DIM), jnp.bfloat16),
            ]
        pooled = held + (everything if last else 0)
        room = LIMIT * 2**20 + pooled * block_rows * HEAD_DIM * 6
        state_at = 2 + len(places) + len(extra)
        return pl.pallas_call(
            functools.partial(
                attend_stage,
                (pb, ka, cores, class_local, places, earlier, slots, turned),
                first,
                last,
                len(extra),
            ),
            out_shape=outs,
            in_specs=[smem]
            + [vmem] * (1 + len(places))
            + [vmem] * (len(extra) + len(state)),
            out_specs=[vmem] * len(outs),
            input_output_aliases={state_at + i: i for i in range(len(state))},
            scratch_shapes=scratch,
            compiler_params=pltpu.CompilerParams(vmem_limit_bytes=room),
            cost_estimate=pl.CostEstimate(
                flops=2**31, bytes_accessed=2**22, transcendentals=2**20
            ),
        )(table, own_queries, *pieces, *extra, *state)

    def along(array, count):
        found = []
        for _ in range(count):
            array = along_ring(array, pb)
            found.append(array)
        return found

    def stacked(arrays):
        return arrays[0] if len(arrays) == 1 else jnp.concatenate(arrays, axis=0)

    def beside(array):
        found = []
        for _ in range(rings - 1):
            array = turn(array, ka, cores, 1, 0)
            found.append(array)
        return found

    every = list(range(cores))
    state, earlier, before = [], [], []
    arrived = [start] + along(start, sources - 1)
    others, places = [], []
    for stage in range(stages):
        hops = range(stage * sources, (stage + 1) * sources)
        if stage:
            arrived, others, state = lax.optimization_barrier((arrived, others, state))
        near = stacked(arrived)
        pieces, places = [near] + others, [(hops, 0, every)] + places
        if stage < stages - 1:
            arrived = along(arrived[-1], sources)
            others = beside(near)
            coming = [(hops, y, every) for y in range(1, rings)]
        elif rings == cores == 2 and sources == 1:
            half = near.shape[0] // 2
            others = [turn(near[:half], ka, cores, 1, 0), along_ring(others[0][half:], pb)]
            coming = [(hops, 1, [0]), (hops, 1, [1])]
        else:
            others = beside(near)
            coming = [(hops, y, every) for y in range(1, rings)]
        state = call(stage == 0, False, 0, pieces, places, earlier, own_queries, state, [])
        earlier, before = earlier + places, before + pieces
        places = coming
    pieces = others
    halves = []
    for c in reversed(range(cores)):
        *state, half = call(False, True, c, pieces, places, earlier, own_queries, state, before)
        halves.append(half)
    if cores == 1:
        return halves[0]
    return pl.pallas_call(
        functools.partial(join, cores),
        out_shape=jax.ShapeDtypeStruct((own_slots * block_rows, cores * width), queries.dtype),
        in_specs=[vmem] * 2,
        out_specs=anywhere,
        scratch_shapes=[pltpu.SemaphoreType.DMA((cores, PARTS))],
        compiler_params=pltpu.CompilerParams(vmem_limit_bytes=SMALL * 2**20),
    )(halves[1], turn(halves[0], ka, cores, 0, 1))


def solution(mesh):
    in_specs = (
        P("pb", "ha"),
        P("pb", "ka", None, "ha"),
        P("pb", "ka", None, "ha"),
        P("pb"),
        P("pb", None),
    )
    out_specs = P(("pb", "ka"), "ha")
    return jax.shard_map(
        on_device, mesh=mesh, in_specs=in_specs, out_specs=out_specs, check_vma=False
    )
```

```python
import functools
import math

import jax
import jax.numpy as jnp
from jax import lax
from jax.experimental import pallas as pl
from jax.experimental.pallas import tpu as pltpu
from jax.sharding import PartitionSpec as P

HEAD_DIM = 128
MASKED = -1e30
HIDDEN = -1e38
HEADROOM = 64.0
PARTS = 8
LIMIT = 10
SMALL = 4
STAGES = 4


def folded(size):
    return list(range(0, size, 2)) + list(range(1, size, 2))[::-1]


def along_ring(array, size, step=1):
    ring = folded(size)
    return lax.ppermute(array, "pb", [(ring[i], ring[(i + step) % size]) for i in range(size)])


def ring_source(at, size, hops):
    place = jnp.where(at % 2 == 0, at // 2, size - 1 - at // 2)
    place = lax.rem(place + (size - hops), size)
    return jnp.where(place < (size + 1) // 2, 2 * place, 2 * (size - 1 - place) + 1)


def turn(array, size, cores, ring_step, core_step):
    rings = size // cores
    pairs = []
    for ring in range(rings):
        for core in range(cores):
            to = ((ring + ring_step) % rings) * cores + (core + core_step) % cores
            pairs.append((ring * cores + core, to))
    return lax.ppermute(array, "ka", pairs)


def dot(a, b, b_dim):
    return lax.dot_general(a, b, (((1,), (b_dim,)), ((), ())), preferred_element_type=jnp.float32)


def copy_rows(source, target, sems):
    step = source.shape[0] // PARTS
    copies = [
        pltpu.make_async_copy(
            source.at[pl.ds(i * step, step)], target.at[pl.ds(i * step, step)], sems.at[i]
        )
        for i in range(PARTS)
    ]
    for copy in copies:
        copy.start()
    return copies


def attend_stage(plan, first, last, ahead, table_ref, q_ref, *refs):
    pb, ka, cores, class_local, places, earlier, slots, turned = plan
    count = len(places)
    pieces, refs = refs[:count], refs[count:]
    old_pieces, refs = refs[:ahead], refs[ahead:]
    if not first:
        refs = refs[1:]
    acc, refs = refs[0], refs[1:]
    if last:
        out_ref, refs = refs[0], refs[1:]
    k_pool, v_pool, held_weights, entries, units, refs = *refs[:5], refs[5:]
    rows = acc.shape[1]
    block_rows = q_ref.shape[0] // slots
    group = rows // block_rows
    rings = ka // cores
    own_slots = slots // cores
    p_at, k_at = lax.axis_index("pb"), lax.axis_index("ka")
    ring_at, core_at = k_at // cores, lax.rem(k_at, cores)
    scale = math.log2(math.e) / math.sqrt(HEAD_DIM)

    def ids(where):
        found = []
        for hops, y, offsets in where:
            ring = lax.rem(ring_at + (rings - y), rings)
            for z in hops:
                source = ring_source(p_at, pb, z)
                for c in offsets:
                    core = lax.rem(core_at + (cores - c), cores)
                    for t in range(class_local):
                        found.append((source * class_local + t) * ka + ring * cores + core)
        return found

    def pool_from(refs_in, at, k_out, v_out):
        for piece in refs_in:
            for i in range(0, piece.shape[0], 2 * class_local):
                span = slice(at, at + class_local)
                k_out[span] = piece[i : i + class_local]
                value = piece[i + class_local : i + 2 * class_local]
                v_out[span, :, :HEAD_DIM] = value
                v_out[span, :, HEAD_DIM:] = jnp.ones(value.shape, v_out.dtype)
                at += class_local

    nothing = sum(piece.shape[0] for piece in pieces) // 2

    if last:
        mine = lax.rem(core_at + turned, cores) * own_slots
        slot_ids = [mine + i for i in range(own_slots)]
    else:
        slot_ids = list(range(slots))

    row_id = lax.broadcasted_iota(jnp.int32, (block_rows, block_rows), 0)
    col_id = lax.broadcasted_iota(jnp.int32, (block_rows, block_rows), 1)
    pool_from(pieces, 0, k_pool, v_pool)
    k_pool[nothing] = jnp.zeros(k_pool.shape[1:], k_pool.dtype)
    v_pool[nothing] = jnp.zeros(v_pool.shape[1:], v_pool.dtype)

    blocks = ids(places)
    unit_count = jnp.int32(0)
    for s in slot_ids:
        row = ring_at * slots + s
        own = table_ref[row, 0]
        place = 2 * unit_count
        for index, block in enumerate(blocks):
            entries[place] = jnp.where(block == own, index + nothing + 1, index)
            place = place + table_ref[row, 1 + block]
        entries[place] = nothing
        ends = lax.div(place + 1, 2)
        if first:

            @pl.when(ends == unit_count)
            def _(s=s):
                acc[s] = jnp.zeros(acc.shape[1:], acc.dtype)


        def mark(u, carry, s=s):
            units[u] = s
            return carry

        lax.fori_loop(unit_count, ends, mark, 0)
        unit_count = ends
    def query_rows(s):
        return jnp.concatenate(
            [
                q_ref[
                    pl.ds(pl.multiple_of(s * block_rows, block_rows), block_rows),
                    x * HEAD_DIM : (x + 1) * HEAD_DIM,
                ]
                for x in range(group)
            ],
            axis=0,
        )

    def pair_of(u):
        raw = [entries[2 * u], entries[2 * u + 1]]
        owns = [entry > nothing for entry in raw]
        return owns, [jnp.where(o, e - (nothing + 1), e) for o, e in zip(owns, raw)]

    def weigh(u):
        owns, index = pair_of(u)
        keys = jnp.concatenate([k_pool[i] for i in index], axis=0)
        reach = jnp.concatenate(
            [
                jnp.where(col_id <= row_id + jnp.where(own, 0, block_rows), 0.0, HIDDEN)
                for own in owns
            ],
            axis=1,
        )
        power = dot(query_rows(units[u]), keys, 1) * scale
        power = power + jnp.concatenate([reach] * group, axis=0)
        held_weights[...] = jnp.exp2(power).astype(held_weights.dtype)

    def add(u):
        _, index = pair_of(u)
        s = units[u]
        values = jnp.concatenate([v_pool[i] for i in index], axis=0)
        added = dot(held_weights[...], values, 0)
        old = acc[s]
        if first:
            fresh = (u == 0) | (units[jnp.maximum(u - 1, 0)] != s)
            old = jnp.where(fresh, 0.0, old)
        acc[s] = old + added

    @pl.when(unit_count > 0)
    def _():
        weigh(0)

        def both(u, carry):
            add(u)
            weigh(u + 1)
            return carry

        lax.fori_loop(0, unit_count - 1, both, 0)
        add(unit_count - 1)

    if not last:
        return

    top, k_all, v_all = refs

    def finish(s, i):
        under = acc[s, :, HEAD_DIM:]
        result = (acc[s, :, :HEAD_DIM] / under).astype(out_ref.dtype)
        for x in range(group):
            out_ref[
                i * block_rows : (i + 1) * block_rows, x * HEAD_DIM : (x + 1) * HEAD_DIM
            ] = result[x * block_rows : (x + 1) * block_rows]
        low = high = [under[j : j + 8] for j in range(0, rows, 8)]
        while len(low) > 1:
            low = [functools.reduce(jnp.minimum, low[j : j + 2]) for j in range(0, len(low), 2)]
            high = [functools.reduce(jnp.maximum, high[j : j + 2]) for j in range(0, len(high), 2)]
        return low[0], high[0]

    low, high = zip(*[finish(s, i) for i, s in enumerate(slot_ids)])
    low, high = functools.reduce(jnp.minimum, low), functools.reduce(jnp.maximum, high)
    safe = (low > 2.0**-HEADROOM) & (high < 2.0**HEADROOM)

    @pl.when(jnp.min(jnp.where(safe, 1.0, 0.0)) < 0.5)
    def _():
        pool_from(old_pieces, 0, k_all, v_all)
        pool_from(pieces, sum(p.shape[0] for p in old_pieces) // 2, k_all, v_all)
        blocks_all = ids(earlier) + blocks
        for i, s in enumerate(slot_ids):
            row = ring_at * slots + s
            own = table_ref[row, 0]
            place = jnp.int32(0)
            for index, block in enumerate(blocks_all):
                entries[place] = jnp.where(block == own, index + len(blocks_all), index)
                place = place + table_ref[row, 1 + block]
            acc[s] = jnp.zeros(acc.shape[1:], acc.dtype)
            top[...] = jnp.full(top.shape, MASKED, top.dtype)

            def one_block(e, carry, s=s):
                is_own = entries[e] >= len(blocks_all)
                index = jnp.where(is_own, entries[e] - len(blocks_all), entries[e])
                reach = jnp.where(
                    col_id <= row_id + jnp.where(is_own, 0, block_rows), 0.0, HIDDEN
                )
                scores = dot(query_rows(s), k_all[index], 1)
                weights, shrinks = [], []
                for x in range(group):
                    span = slice(x * block_rows, (x + 1) * block_rows)
                    power = scores[span] * scale + reach
                    new = jnp.maximum(top[span], jnp.max(power, axis=1, keepdims=True))
                    shrink = jnp.exp2(top[span] - new)
                    top[span] = new
                    weights.append(jnp.exp2(power - new).astype(jnp.bfloat16))
                    shrinks.append(jnp.concatenate([shrink, shrink], axis=1))
                added = dot(jnp.concatenate(weights, axis=0), v_all[index], 0)
                acc[s] = acc[s] * jnp.concatenate(shrinks, axis=0) + added
                return carry

            lax.fori_loop(0, place, one_block, 0)
            finish(s, i)


def cut(cores, *refs):
    ins, out_ref = refs[:-1], refs[-1]
    count = ins[0].shape[0]
    width = out_ref.shape[2]
    core = lax.rem(lax.axis_index("ka"), cores)
    for c in range(cores):

        @pl.when(core == c)
        def _():
            for i, ref in enumerate(ins):
                out_ref[i * count : (i + 1) * count] = ref[
                    :, 0, :, c * width : (c + 1) * width
                ]


def fetch(cores, queries_ref, out_ref, sems):
    rows, width = out_ref.shape
    at = lax.axis_index("ka")
    copies = copy_rows(
        queries_ref.at[
            pl.ds(pl.multiple_of(at // cores * rows, HEAD_DIM), rows),
            pl.ds(pl.multiple_of(lax.rem(at, cores) * width, HEAD_DIM), width),
        ],
        out_ref,
        sems,
    )
    for copy in copies:
        copy.wait()


def join(cores, own_ref, other_ref, out_ref, sems):
    width = own_ref.shape[1]
    core = lax.rem(lax.axis_index("ka"), cores)
    copies = []
    for i, ref in enumerate((own_ref, other_ref)):
        at = pl.multiple_of(lax.rem(core + (cores - i), cores) * width, HEAD_DIM)
        copies += copy_rows(ref, out_ref.at[:, pl.ds(at, width)], sems.at[i])
    for copy in copies:
        copy.wait()


def on_device(queries, keys, values, q_order, block_mask):
    pb, ka = lax.axis_size("pb"), lax.axis_size("ka")
    class_local, _, block_rows, kv_width = keys.shape
    cores = 2 if ka % 2 == 0 and kv_width == 2 * HEAD_DIM else 1
    rings = ka // cores
    head_width = kv_width // cores
    width = queries.shape[1] // cores
    rows = width // head_width * block_rows
    own_slots = queries.shape[0] // block_rows // ka
    slots = own_slots * cores

    vmem = pl.BlockSpec(memory_space=pltpu.VMEM)
    smem = pl.BlockSpec(memory_space=pltpu.SMEM)

    anywhere = pl.BlockSpec(memory_space=pl.ANY)
    stages = min(STAGES, pb)
    sources = pb // stages

    table = jnp.concatenate([q_order[:, None], block_mask], axis=1)
    own_queries = pl.pallas_call(
        functools.partial(fetch, cores),
        out_shape=jax.ShapeDtypeStruct((slots * block_rows, width), queries.dtype),
        in_specs=[anywhere],
        out_specs=vmem,
        scratch_shapes=[pltpu.SemaphoreType.DMA((PARTS,))],
        compiler_params=pltpu.CompilerParams(vmem_limit_bytes=50 * 2**20),
    )(queries)
    raw = [keys, values]
    for c in range(1, cores):
        raw += [turn(keys, ka, cores, 0, c), turn(values, ka, cores, 0, c)]
    start = pl.pallas_call(
        functools.partial(cut, cores),
        out_shape=jax.ShapeDtypeStruct(
            (2 * cores * class_local, block_rows, head_width), keys.dtype
        ),
        in_specs=[vmem] * len(raw),
        out_specs=vmem,
        compiler_params=pltpu.CompilerParams(vmem_limit_bytes=SMALL * 2**20),
    )(*raw)

    def blocks_of(where):
        return sum(len(hops) * len(offsets) * class_local for hops, _, offsets in where)

    def call(first, last, turned, pieces, places, earlier, own_queries, state, extra):
        held = blocks_of(places)
        everything = held + blocks_of(earlier)
        here = own_slots if last else slots
        outs = [jax.ShapeDtypeStruct((slots, rows, 2 * HEAD_DIM), jnp.float32)]
        scratch = [
            pltpu.VMEM((held + 1, block_rows, HEAD_DIM), jnp.bfloat16),
            pltpu.VMEM((held + 1, block_rows, 2 * HEAD_DIM), jnp.bfloat16),
            pltpu.VMEM((rows, 2 * block_rows), jnp.bfloat16),
            pltpu.SMEM((max(here * (held + 1) + 1, everything + 1),), jnp.int32),
            pltpu.SMEM((here * (held // 2 + 1),), jnp.int32),
        ]
        if last:
            outs.append(jax.ShapeDtypeStruct((own_slots * block_rows, width), queries.dtype))
            scratch += [
                pltpu.VMEM((rows, HEAD_DIM), jnp.float32),
                pltpu.VMEM((everything, block_rows, HEAD_DIM), jnp.bfloat16),
                pltpu.VMEM((everything, block_rows, 2 * HEAD_DIM), jnp.bfloat16),
            ]
        pooled = held + (everything if last else 0)
        room = LIMIT * 2**20 + pooled * block_rows * HEAD_DIM * 6
        state_at = 2 + len(places) + len(extra)
        return pl.pallas_call(
            functools.partial(
                attend_stage,
                (pb, ka, cores, class_local, places, earlier, slots, turned),
                first,
                last,
                len(extra),
            ),
            out_shape=outs,
            in_specs=[smem]
            + [vmem] * (1 + len(places))
            + [vmem] * (len(extra) + len(state)),
            out_specs=[vmem] * len(outs),
            input_output_aliases={state_at + i: i for i in range(len(state))},
            scratch_shapes=scratch,
            compiler_params=pltpu.CompilerParams(vmem_limit_bytes=room),
            cost_estimate=pl.CostEstimate(
                flops=2**31, bytes_accessed=2**22, transcendentals=2**20
            ),
        )(table, own_queries, *pieces, *extra, *state)

    def along(array, count):
        found = []
        for _ in range(count):
            array = along_ring(array, pb)
            found.append(array)
        return found

    def stacked(arrays):
        return arrays[0] if len(arrays) == 1 else jnp.concatenate(arrays, axis=0)

    def beside(array):
        found = []
        for _ in range(rings - 1):
            array = turn(array, ka, cores, 1, 0)
            found.append(array)
        return found

    every = list(range(cores))
    state, earlier, before = [], [], []

    def work(state, pieces, places):
        state = call(not earlier, False, 0, pieces, places, earlier, own_queries, state, [])
        earlier.extend(places)
        before.extend(pieces)
        return state

    if rings == cores == 2 and pb == STAGES:
        tie = lax.optimization_barrier
        half = start.shape[0] // 2
        on, back, others = along_ring(start, pb), along_ring(start, pb, -1), beside(start)[0]
        state = work(state, [start], [([0], 0, every)])
        on, others, state = tie((on, others, state))
        two, on_others = along_ring(on, pb), beside(on)[0]
        state = work(state, [on, others], [([1], 0, every), ([0], 1, every)])
        back, state = tie((back, state))
        back_others = beside(back)[0]
        on_others, back, state = tie((on_others, back, state))
        two_high = along_ring(on_others[half:], pb)
        state = work(state, [back, on_others], [([pb - 1], 0, every), ([1], 1, every)])
        two, state = tie((two, state))
        two_low = turn(two[:half], ka, cores, 1, 0)
        state = work(state, [two, back_others], [([2], 0, every), ([pb - 1], 1, every)])
        pieces, places = [two_low, two_high], [([2], 1, [0]), ([2], 1, [1])]
    else:
        arrived = [start] + along(start, sources - 1)
        others, places = [], []
        for stage in range(stages):
            hops = range(stage * sources, (stage + 1) * sources)
            if stage:
                arrived, others, state = lax.optimization_barrier((arrived, others, state))
            near = stacked(arrived)
            pieces, places = [near] + others, [(hops, 0, every)] + places
            if stage < stages - 1:
                arrived = along(arrived[-1], sources)
            others = beside(near)
            state = work(state, pieces, places)
            places = [(hops, y, every) for y in range(1, rings)]
        pieces = others
    halves = []
    for c in reversed(range(cores)):
        *state, half = call(False, True, c, pieces, places, earlier, own_queries, state, before)
        halves.append(half)
    if cores == 1:
        return halves[0]
    return pl.pallas_call(
        functools.partial(join, cores),
        out_shape=jax.ShapeDtypeStruct((own_slots * block_rows, cores * width), queries.dtype),
        in_specs=[vmem] * 2,
        out_specs=anywhere,
        scratch_shapes=[pltpu.SemaphoreType.DMA((cores, PARTS))],
        compiler_params=pltpu.CompilerParams(vmem_limit_bytes=SMALL * 2**20),
    )(halves[1], turn(halves[0], ka, cores, 0, 1))


def solution(mesh):
    in_specs = (
        P("pb", "ha"),
        P("pb", "ka", None, "ha"),
        P("pb", "ka", None, "ha"),
        P("pb"),
        P("pb", None),
    )
    out_specs = P(("pb", "ka"), "ha")
    return jax.shard_map(
        on_device, mesh=mesh, in_specs=in_specs, out_specs=out_specs, check_vma=False
    )
```

```python
import functools
import math

import jax
import jax.numpy as jnp
from jax import lax
from jax.experimental import pallas as pl
from jax.experimental.pallas import tpu as pltpu
from jax.sharding import PartitionSpec as P

HEAD_DIM = 128
MASKED = -1e30
HIDDEN = -1e38
HEADROOM = 64.0
PARTS = 8
LIMIT = 10
SMALL = 4
STAGES = 4


def folded(size):
    return list(range(0, size, 2)) + list(range(1, size, 2))[::-1]


def along_ring(array, size, step=1):
    ring = folded(size)
    return lax.ppermute(array, "pb", [(ring[i], ring[(i + step) % size]) for i in range(size)])


def ring_source(at, size, hops):
    place = jnp.where(at % 2 == 0, at // 2, size - 1 - at // 2)
    place = lax.rem(place + (size - hops), size)
    return jnp.where(place < (size + 1) // 2, 2 * place, 2 * (size - 1 - place) + 1)


def turn(array, size, cores, ring_step, core_step):
    rings = size // cores
    pairs = []
    for ring in range(rings):
        for core in range(cores):
            to = ((ring + ring_step) % rings) * cores + (core + core_step) % cores
            pairs.append((ring * cores + core, to))
    return lax.ppermute(array, "ka", pairs)


def dot(a, b, b_dim):
    return lax.dot_general(a, b, (((1,), (b_dim,)), ((), ())), preferred_element_type=jnp.float32)


def copy_rows(source, target, sems):
    step = source.shape[0] // PARTS
    copies = [
        pltpu.make_async_copy(
            source.at[pl.ds(i * step, step)], target.at[pl.ds(i * step, step)], sems.at[i]
        )
        for i in range(PARTS)
    ]
    for copy in copies:
        copy.start()
    return copies


def attend_stage(plan, first, last, ahead, table_ref, q_ref, *refs):
    pb, ka, cores, class_local, places, earlier, slots, turned = plan
    count = len(places)
    pieces, refs = refs[:count], refs[count:]
    old_pieces, refs = refs[:ahead], refs[ahead:]
    if not first:
        refs = refs[1:]
    acc, refs = refs[0], refs[1:]
    if last:
        out_ref, refs = refs[0], refs[1:]
    k_pool, v_pool, held_weights, entries, units, refs = *refs[:5], refs[5:]
    rows = acc.shape[1]
    block_rows = q_ref.shape[0] // slots
    group = rows // block_rows
    rings = ka // cores
    own_slots = slots // cores
    p_at, k_at = lax.axis_index("pb"), lax.axis_index("ka")
    ring_at, core_at = k_at // cores, lax.rem(k_at, cores)
    scale = math.log2(math.e) / math.sqrt(HEAD_DIM)

    def ids(where):
        found = []
        for hops, y, offsets in where:
            ring = lax.rem(ring_at + (rings - y), rings)
            for z in hops:
                source = ring_source(p_at, pb, z)
                for c in offsets:
                    core = lax.rem(core_at + (cores - c), cores)
                    for t in range(class_local):
                        found.append((source * class_local + t) * ka + ring * cores + core)
        return found

    def pool_from(refs_in, at, k_out, v_out):
        for piece in refs_in:
            for i in range(0, piece.shape[0], 2 * class_local):
                span = slice(at, at + class_local)
                k_out[span] = piece[i : i + class_local]
                value = piece[i + class_local : i + 2 * class_local]
                v_out[span, :, :HEAD_DIM] = value
                v_out[span, :, HEAD_DIM:] = jnp.ones(value.shape, v_out.dtype)
                at += class_local

    nothing = sum(piece.shape[0] for piece in pieces) // 2

    if last:
        mine = lax.rem(core_at + turned, cores) * own_slots
        slot_ids = [mine + i for i in range(own_slots)]
    else:
        slot_ids = list(range(slots))

    row_id = lax.broadcasted_iota(jnp.int32, (block_rows, block_rows), 0)
    col_id = lax.broadcasted_iota(jnp.int32, (block_rows, block_rows), 1)
    pool_from(pieces, 0, k_pool, v_pool)
    k_pool[nothing] = jnp.zeros(k_pool.shape[1:], k_pool.dtype)
    v_pool[nothing] = jnp.zeros(v_pool.shape[1:], v_pool.dtype)

    blocks = ids(places)
    unit_count = jnp.int32(0)
    for s in slot_ids:
        row = ring_at * slots + s
        own = table_ref[row, 0]
        place = 2 * unit_count
        for index, block in enumerate(blocks):
            entries[place] = jnp.where(block == own, index + nothing + 1, index)
            place = place + table_ref[row, 1 + block]
        entries[place] = nothing
        ends = lax.div(place + 1, 2)
        if first:

            @pl.when(ends == unit_count)
            def _(s=s):
                acc[s] = jnp.zeros(acc.shape[1:], acc.dtype)


        def mark(u, carry, s=s):
            units[u] = s
            return carry

        lax.fori_loop(unit_count, ends, mark, 0)
        unit_count = ends
    def query_rows(s):
        return jnp.concatenate(
            [
                q_ref[
                    pl.ds(pl.multiple_of(s * block_rows, block_rows), block_rows),
                    x * HEAD_DIM : (x + 1) * HEAD_DIM,
                ]
                for x in range(group)
            ],
            axis=0,
        )

    def pair_of(u):
        raw = [entries[2 * u], entries[2 * u + 1]]
        owns = [entry > nothing for entry in raw]
        return owns, [jnp.where(o, e - (nothing + 1), e) for o, e in zip(owns, raw)]

    def weigh(u):
        owns, index = pair_of(u)
        keys = jnp.concatenate([k_pool[i] for i in index], axis=0)
        reach = jnp.concatenate(
            [
                jnp.where(col_id <= row_id + jnp.where(own, 0, block_rows), 0.0, HIDDEN)
                for own in owns
            ],
            axis=1,
        )
        power = dot(query_rows(units[u]), keys, 1) * scale
        power = power + jnp.concatenate([reach] * group, axis=0)
        held_weights[...] = jnp.exp2(power).astype(held_weights.dtype)

    def add(u):
        _, index = pair_of(u)
        s = units[u]
        values = jnp.concatenate([v_pool[i] for i in index], axis=0)
        added = dot(held_weights[...], values, 0)
        old = acc[s]
        if first:
            fresh = (u == 0) | (units[jnp.maximum(u - 1, 0)] != s)
            old = jnp.where(fresh, 0.0, old)
        acc[s] = old + added

    @pl.when(unit_count > 0)
    def _():
        weigh(0)

        def both(u, carry):
            add(u)
            weigh(u + 1)
            return carry

        lax.fori_loop(0, unit_count - 1, both, 0)
        add(unit_count - 1)

    if not last:
        return

    top, k_all, v_all = refs

    def finish(s, i):
        under = acc[s, :, HEAD_DIM:]
        result = (acc[s, :, :HEAD_DIM] / under).astype(out_ref.dtype)
        for x in range(group):
            out_ref[
                i * block_rows : (i + 1) * block_rows, x * HEAD_DIM : (x + 1) * HEAD_DIM
            ] = result[x * block_rows : (x + 1) * block_rows]
        low = high = [under[j : j + 8] for j in range(0, rows, 8)]
        while len(low) > 1:
            low = [functools.reduce(jnp.minimum, low[j : j + 2]) for j in range(0, len(low), 2)]
            high = [functools.reduce(jnp.maximum, high[j : j + 2]) for j in range(0, len(high), 2)]
        return low[0], high[0]

    low, high = zip(*[finish(s, i) for i, s in enumerate(slot_ids)])
    low, high = functools.reduce(jnp.minimum, low), functools.reduce(jnp.maximum, high)
    safe = (low > 2.0**-HEADROOM) & (high < 2.0**HEADROOM)

    @pl.when(jnp.min(jnp.where(safe, 1.0, 0.0)) < 0.5)
    def _():
        pool_from(old_pieces, 0, k_all, v_all)
        pool_from(pieces, sum(p.shape[0] for p in old_pieces) // 2, k_all, v_all)
        blocks_all = ids(earlier) + blocks
        for i, s in enumerate(slot_ids):
            row = ring_at * slots + s
            own = table_ref[row, 0]
            place = jnp.int32(0)
            for index, block in enumerate(blocks_all):
                entries[place] = jnp.where(block == own, index + len(blocks_all), index)
                place = place + table_ref[row, 1 + block]
            acc[s] = jnp.zeros(acc.shape[1:], acc.dtype)
            top[...] = jnp.full(top.shape, MASKED, top.dtype)

            def one_block(e, carry, s=s):
                is_own = entries[e] >= len(blocks_all)
                index = jnp.where(is_own, entries[e] - len(blocks_all), entries[e])
                reach = jnp.where(
                    col_id <= row_id + jnp.where(is_own, 0, block_rows), 0.0, HIDDEN
                )
                scores = dot(query_rows(s), k_all[index], 1)
                weights, shrinks = [], []
                for x in range(group):
                    span = slice(x * block_rows, (x + 1) * block_rows)
                    power = scores[span] * scale + reach
                    new = jnp.maximum(top[span], jnp.max(power, axis=1, keepdims=True))
                    shrink = jnp.exp2(top[span] - new)
                    top[span] = new
                    weights.append(jnp.exp2(power - new).astype(jnp.bfloat16))
                    shrinks.append(jnp.concatenate([shrink, shrink], axis=1))
                added = dot(jnp.concatenate(weights, axis=0), v_all[index], 0)
                acc[s] = acc[s] * jnp.concatenate(shrinks, axis=0) + added
                return carry

            lax.fori_loop(0, place, one_block, 0)
            finish(s, i)


def cut(cores, *refs):
    ins, out_ref = refs[:-1], refs[-1]
    count = ins[0].shape[0]
    width = out_ref.shape[2]
    core = lax.rem(lax.axis_index("ka"), cores)
    for c in range(cores):

        @pl.when(core == c)
        def _():
            for i, ref in enumerate(ins):
                out_ref[i * count : (i + 1) * count] = ref[
                    :, 0, :, c * width : (c + 1) * width
                ]


def fetch(cores, queries_ref, out_ref, sems):
    rows, width = out_ref.shape
    at = lax.axis_index("ka")
    copies = copy_rows(
        queries_ref.at[
            pl.ds(pl.multiple_of(at // cores * rows, HEAD_DIM), rows),
            pl.ds(pl.multiple_of(lax.rem(at, cores) * width, HEAD_DIM), width),
        ],
        out_ref,
        sems,
    )
    for copy in copies:
        copy.wait()


def join(cores, own_ref, other_ref, out_ref, sems):
    width = own_ref.shape[1]
    core = lax.rem(lax.axis_index("ka"), cores)
    copies = []
    for i, ref in enumerate((own_ref, other_ref)):
        at = pl.multiple_of(lax.rem(core + (cores - i), cores) * width, HEAD_DIM)
        copies += copy_rows(ref, out_ref.at[:, pl.ds(at, width)], sems.at[i])
    for copy in copies:
        copy.wait()


def on_device(queries, keys, values, q_order, block_mask):
    pb, ka = lax.axis_size("pb"), lax.axis_size("ka")
    class_local, _, block_rows, kv_width = keys.shape
    cores = 2 if ka % 2 == 0 and kv_width == 2 * HEAD_DIM else 1
    rings = ka // cores
    head_width = kv_width // cores
    width = queries.shape[1] // cores
    rows = width // head_width * block_rows
    own_slots = queries.shape[0] // block_rows // ka
    slots = own_slots * cores

    vmem = pl.BlockSpec(memory_space=pltpu.VMEM)
    smem = pl.BlockSpec(memory_space=pltpu.SMEM)

    anywhere = pl.BlockSpec(memory_space=pl.ANY)
    stages = min(STAGES, pb)
    sources = pb // stages

    own_queries = pl.pallas_call(
        functools.partial(fetch, cores),
        out_shape=jax.ShapeDtypeStruct((slots * block_rows, width), queries.dtype),
        in_specs=[anywhere],
        out_specs=vmem,
        scratch_shapes=[pltpu.SemaphoreType.DMA((PARTS,))],
        compiler_params=pltpu.CompilerParams(vmem_limit_bytes=50 * 2**20),
    )(queries)
    raw = [keys, values]
    for c in range(1, cores):
        raw += [turn(keys, ka, cores, 0, c), turn(values, ka, cores, 0, c)]
    start = pl.pallas_call(
        functools.partial(cut, cores),
        out_shape=jax.ShapeDtypeStruct(
            (2 * cores * class_local, block_rows, head_width), keys.dtype
        ),
        in_specs=[vmem] * len(raw),
        out_specs=vmem,
        compiler_params=pltpu.CompilerParams(vmem_limit_bytes=SMALL * 2**20),
    )(*raw)

    start, q_order = lax.optimization_barrier((start, q_order))
    table = jnp.concatenate([q_order[:, None], block_mask], axis=1)
    def blocks_of(where):
        return sum(len(hops) * len(offsets) * class_local for hops, _, offsets in where)

    def call(first, last, turned, pieces, places, earlier, own_queries, state, extra):
        held = blocks_of(places)
        everything = held + blocks_of(earlier)
        here = own_slots if last else slots
        outs = [jax.ShapeDtypeStruct((slots, rows, 2 * HEAD_DIM), jnp.float32)]
        scratch = [
            pltpu.VMEM((held + 1, block_rows, HEAD_DIM), jnp.bfloat16),
            pltpu.VMEM((held + 1, block_rows, 2 * HEAD_DIM), jnp.bfloat16),
            pltpu.VMEM((rows, 2 * block_rows), jnp.bfloat16),
            pltpu.SMEM((max(here * (held + 1) + 1, everything + 1),), jnp.int32),
            pltpu.SMEM((here * (held // 2 + 1),), jnp.int32),
        ]
        if last:
            outs.append(jax.ShapeDtypeStruct((own_slots * block_rows, width), queries.dtype))
            scratch += [
                pltpu.VMEM((rows, HEAD_DIM), jnp.float32),
                pltpu.VMEM((everything, block_rows, HEAD_DIM), jnp.bfloat16),
                pltpu.VMEM((everything, block_rows, 2 * HEAD_DIM), jnp.bfloat16),
            ]
        pooled = held + (everything if last else 0)
        room = LIMIT * 2**20 + pooled * block_rows * HEAD_DIM * 6
        state_at = 2 + len(places) + len(extra)
        return pl.pallas_call(
            functools.partial(
                attend_stage,
                (pb, ka, cores, class_local, places, earlier, slots, turned),
                first,
                last,
                len(extra),
            ),
            out_shape=outs,
            in_specs=[smem]
            + [vmem] * (1 + len(places))
            + [vmem] * (len(extra) + len(state)),
            out_specs=[vmem] * len(outs),
            input_output_aliases={state_at + i: i for i in range(len(state))},
            scratch_shapes=scratch,
            compiler_params=pltpu.CompilerParams(vmem_limit_bytes=room),
            cost_estimate=pl.CostEstimate(
                flops=2**31, bytes_accessed=2**22, transcendentals=2**20
            ),
        )(table, own_queries, *pieces, *extra, *state)

    def along(array, count):
        found = []
        for _ in range(count):
            array = along_ring(array, pb)
            found.append(array)
        return found

    def stacked(arrays):
        return arrays[0] if len(arrays) == 1 else jnp.concatenate(arrays, axis=0)

    def beside(array):
        found = []
        for _ in range(rings - 1):
            array = turn(array, ka, cores, 1, 0)
            found.append(array)
        return found

    every = list(range(cores))
    state, earlier, before = [], [], []

    def work(state, pieces, places):
        state = call(not earlier, False, 0, pieces, places, earlier, own_queries, state, [])
        earlier.extend(places)
        before.extend(pieces)
        return state

    if rings == cores == 2 and pb == STAGES:
        tie = lax.optimization_barrier
        half = start.shape[0] // 2
        on, back, others = along_ring(start, pb), along_ring(start, pb, -1), beside(start)[0]
        state = work(state, [start], [([0], 0, every)])
        on, others, state = tie((on, others, state))
        on_others, two = beside(on)[0], along_ring(on, pb)
        state = work(state, [on, others], [([1], 0, every), ([0], 1, every)])
        back, state = tie((back, state))
        back_others = beside(back)[0]
        on_others, back, state = tie((on_others, back, state))
        two_high = along_ring(on_others[half:], pb)
        state = work(state, [back, on_others], [([pb - 1], 0, every), ([1], 1, every)])
        two, state = tie((two, state))
        two_low = turn(two[:half], ka, cores, 1, 0)
        state = work(state, [two], [([2], 0, every)])
        pieces = [back_others, two_low, two_high]
        places = [([pb - 1], 1, every), ([2], 1, [0]), ([2], 1, [1])]
    else:
        arrived = [start] + along(start, sources - 1)
        others, places = [], []
        for stage in range(stages):
            hops = range(stage * sources, (stage + 1) * sources)
            if stage:
                arrived, others, state = lax.optimization_barrier((arrived, others, state))
            near = stacked(arrived)
            pieces, places = [near] + others, [(hops, 0, every)] + places
            if stage < stages - 1:
                arrived = along(arrived[-1], sources)
            others = beside(near)
            state = work(state, pieces, places)
            places = [(hops, y, every) for y in range(1, rings)]
        pieces = others
    halves = []
    for c in reversed(range(cores)):
        *state, half = call(False, True, c, pieces, places, earlier, own_queries, state, before)
        halves.append(half)
    if cores == 1:
        return halves[0]
    return pl.pallas_call(
        functools.partial(join, cores),
        out_shape=jax.ShapeDtypeStruct((own_slots * block_rows, cores * width), queries.dtype),
        in_specs=[vmem] * 2,
        out_specs=anywhere,
        scratch_shapes=[pltpu.SemaphoreType.DMA((cores, PARTS))],
        compiler_params=pltpu.CompilerParams(vmem_limit_bytes=SMALL * 2**20),
    )(halves[1], turn(halves[0], ka, cores, 0, 1))


def solution(mesh):
    in_specs = (
        P("pb", "ha"),
        P("pb", "ka", None, "ha"),
        P("pb", "ka", None, "ha"),
        P("pb"),
        P("pb", None),
    )
    out_specs = P(("pb", "ka"), "ha")
    return jax.shard_map(
        on_device, mesh=mesh, in_specs=in_specs, out_specs=out_specs, check_vma=False
    )
```

```python
import functools
import math

import jax
import jax.numpy as jnp
from jax import lax
from jax.experimental import pallas as pl
from jax.experimental.pallas import tpu as pltpu
from jax.sharding import PartitionSpec as P

HEAD_DIM = 128
MASKED = -1e30
HIDDEN = -1e38
HEADROOM = 64.0
PARTS = 8
LIMIT = 10
SMALL = 4
STAGES = 4


def folded(size):
    return list(range(0, size, 2)) + list(range(1, size, 2))[::-1]


def along_ring(array, size, step=1):
    ring = folded(size)
    return lax.ppermute(array, "pb", [(ring[i], ring[(i + step) % size]) for i in range(size)])


def ring_source(at, size, hops):
    place = jnp.where(at % 2 == 0, at // 2, size - 1 - at // 2)
    place = lax.rem(place + (size - hops), size)
    return jnp.where(place < (size + 1) // 2, 2 * place, 2 * (size - 1 - place) + 1)


def turn(array, size, cores, ring_step, core_step):
    rings = size // cores
    pairs = []
    for ring in range(rings):
        for core in range(cores):
            to = ((ring + ring_step) % rings) * cores + (core + core_step) % cores
            pairs.append((ring * cores + core, to))
    return lax.ppermute(array, "ka", pairs)


def dot(a, b, b_dim):
    return lax.dot_general(a, b, (((1,), (b_dim,)), ((), ())), preferred_element_type=jnp.float32)


def copy_rows(source, target, sems):
    step = source.shape[0] // PARTS
    copies = [
        pltpu.make_async_copy(
            source.at[pl.ds(i * step, step)], target.at[pl.ds(i * step, step)], sems.at[i]
        )
        for i in range(PARTS)
    ]
    for copy in copies:
        copy.start()
    return copies


def attend_stage(plan, first, last, ahead, table_ref, q_ref, *refs):
    pb, ka, cores, class_local, places, earlier, slots, turned = plan
    count = len(places)
    pieces, refs = refs[:count], refs[count:]
    old_pieces, refs = refs[:ahead], refs[ahead:]
    if not first:
        refs = refs[1:]
    acc, refs = refs[0], refs[1:]
    if last:
        out_ref, refs = refs[0], refs[1:]
    k_pool, v_pool, held_weights, entries, units, refs = *refs[:5], refs[5:]
    rows = acc.shape[1]
    block_rows = q_ref.shape[0] // slots
    group = rows // block_rows
    rings = ka // cores
    own_slots = slots // cores
    p_at, k_at = lax.axis_index("pb"), lax.axis_index("ka")
    ring_at, core_at = k_at // cores, lax.rem(k_at, cores)
    scale = math.log2(math.e) / math.sqrt(HEAD_DIM)

    def ids(where):
        found = []
        for hops, y, offsets in where:
            ring = lax.rem(ring_at + (rings - y), rings)
            for z in hops:
                source = ring_source(p_at, pb, z)
                for c in offsets:
                    core = lax.rem(core_at + (cores - c), cores)
                    for t in range(class_local):
                        found.append((source * class_local + t) * ka + ring * cores + core)
        return found

    def pool_from(refs_in, at, k_out, v_out):
        for piece in refs_in:
            for i in range(0, piece.shape[0], 2 * class_local):
                span = slice(at, at + class_local)
                k_out[span] = piece[i : i + class_local]
                value = piece[i + class_local : i + 2 * class_local]
                v_out[span, :, :HEAD_DIM] = value
                v_out[span, :, HEAD_DIM:] = jnp.ones(value.shape, v_out.dtype)
                at += class_local

    nothing = sum(piece.shape[0] for piece in pieces) // 2

    if last:
        mine = lax.rem(core_at + turned, cores) * own_slots
        slot_ids = [mine + i for i in range(own_slots)]
    else:
        slot_ids = list(range(slots))

    row_id = lax.broadcasted_iota(jnp.int32, (block_rows, block_rows), 0)
    col_id = lax.broadcasted_iota(jnp.int32, (block_rows, block_rows), 1)
    pool_from(pieces, 0, k_pool, v_pool)
    k_pool[nothing] = jnp.zeros(k_pool.shape[1:], k_pool.dtype)
    v_pool[nothing] = jnp.zeros(v_pool.shape[1:], v_pool.dtype)

    blocks = ids(places)
    unit_count = jnp.int32(0)
    for s in slot_ids:
        row = ring_at * slots + s
        own = table_ref[row, 0]
        place = 2 * unit_count
        for index, block in enumerate(blocks):
            entries[place] = jnp.where(block == own, index + nothing + 1, index)
            place = place + table_ref[row, 1 + block]
        entries[place] = nothing
        ends = lax.div(place + 1, 2)
        if first:

            @pl.when(ends == unit_count)
            def _(s=s):
                acc[s] = jnp.zeros(acc.shape[1:], acc.dtype)


        def mark(u, carry, s=s):
            units[u] = s
            return carry

        lax.fori_loop(unit_count, ends, mark, 0)
        unit_count = ends
    def query_rows(s):
        return jnp.concatenate(
            [
                q_ref[
                    pl.ds(pl.multiple_of(s * block_rows, block_rows), block_rows),
                    x * HEAD_DIM : (x + 1) * HEAD_DIM,
                ]
                for x in range(group)
            ],
            axis=0,
        )

    def pair_of(u):
        raw = [entries[2 * u], entries[2 * u + 1]]
        owns = [entry > nothing for entry in raw]
        return owns, [jnp.where(o, e - (nothing + 1), e) for o, e in zip(owns, raw)]

    def weigh(u):
        owns, index = pair_of(u)
        keys = jnp.concatenate([k_pool[i] for i in index], axis=0)
        reach = jnp.concatenate(
            [
                jnp.where(col_id <= row_id + jnp.where(own, 0, block_rows), 0.0, HIDDEN)
                for own in owns
            ],
            axis=1,
        )
        power = dot(query_rows(units[u]), keys, 1) * scale
        power = power + jnp.concatenate([reach] * group, axis=0)
        held_weights[...] = jnp.exp2(power).astype(held_weights.dtype)

    def add(u):
        _, index = pair_of(u)
        s = units[u]
        values = jnp.concatenate([v_pool[i] for i in index], axis=0)
        added = dot(held_weights[...], values, 0)
        old = acc[s]
        if first:
            fresh = (u == 0) | (units[jnp.maximum(u - 1, 0)] != s)
            old = jnp.where(fresh, 0.0, old)
        acc[s] = old + added

    @pl.when(unit_count > 0)
    def _():
        weigh(0)

        def both(u, carry):
            add(u)
            weigh(u + 1)
            return carry

        lax.fori_loop(0, unit_count - 1, both, 0)
        add(unit_count - 1)

    if not last:
        return

    top, k_all, v_all = refs

    def finish(s, i):
        under = acc[s, :, HEAD_DIM:]
        result = (acc[s, :, :HEAD_DIM] / under).astype(out_ref.dtype)
        for x in range(group):
            out_ref[
                i * block_rows : (i + 1) * block_rows, x * HEAD_DIM : (x + 1) * HEAD_DIM
            ] = result[x * block_rows : (x + 1) * block_rows]
        low = high = [under[j : j + 8] for j in range(0, rows, 8)]
        while len(low) > 1:
            low = [functools.reduce(jnp.minimum, low[j : j + 2]) for j in range(0, len(low), 2)]
            high = [functools.reduce(jnp.maximum, high[j : j + 2]) for j in range(0, len(high), 2)]
        return low[0], high[0]

    low, high = zip(*[finish(s, i) for i, s in enumerate(slot_ids)])
    low, high = functools.reduce(jnp.minimum, low), functools.reduce(jnp.maximum, high)
    safe = (low > 2.0**-HEADROOM) & (high < 2.0**HEADROOM)

    @pl.when(jnp.min(jnp.where(safe, 1.0, 0.0)) < 0.5)
    def _():
        pool_from(old_pieces, 0, k_all, v_all)
        pool_from(pieces, sum(p.shape[0] for p in old_pieces) // 2, k_all, v_all)
        blocks_all = ids(earlier) + blocks
        for i, s in enumerate(slot_ids):
            row = ring_at * slots + s
            own = table_ref[row, 0]
            place = jnp.int32(0)
            for index, block in enumerate(blocks_all):
                entries[place] = jnp.where(block == own, index + len(blocks_all), index)
                place = place + table_ref[row, 1 + block]
            acc[s] = jnp.zeros(acc.shape[1:], acc.dtype)
            top[...] = jnp.full(top.shape, MASKED, top.dtype)

            def one_block(e, carry, s=s):
                is_own = entries[e] >= len(blocks_all)
                index = jnp.where(is_own, entries[e] - len(blocks_all), entries[e])
                reach = jnp.where(
                    col_id <= row_id + jnp.where(is_own, 0, block_rows), 0.0, HIDDEN
                )
                scores = dot(query_rows(s), k_all[index], 1)
                weights, shrinks = [], []
                for x in range(group):
                    span = slice(x * block_rows, (x + 1) * block_rows)
                    power = scores[span] * scale + reach
                    new = jnp.maximum(top[span], jnp.max(power, axis=1, keepdims=True))
                    shrink = jnp.exp2(top[span] - new)
                    top[span] = new
                    weights.append(jnp.exp2(power - new).astype(jnp.bfloat16))
                    shrinks.append(jnp.concatenate([shrink, shrink], axis=1))
                added = dot(jnp.concatenate(weights, axis=0), v_all[index], 0)
                acc[s] = acc[s] * jnp.concatenate(shrinks, axis=0) + added
                return carry

            lax.fori_loop(0, place, one_block, 0)
            finish(s, i)


def cut(cores, *refs):
    ins, out_ref = refs[:-1], refs[-1]
    count = ins[0].shape[0]
    width = out_ref.shape[2]
    core = lax.rem(lax.axis_index("ka"), cores)
    for c in range(cores):

        @pl.when(core == c)
        def _():
            for i, ref in enumerate(ins):
                out_ref[i * count : (i + 1) * count] = ref[
                    :, 0, :, c * width : (c + 1) * width
                ]


def fetch(cores, queries_ref, out_ref, sems):
    rows, width = out_ref.shape
    at = lax.axis_index("ka")
    copies = copy_rows(
        queries_ref.at[
            pl.ds(pl.multiple_of(at // cores * rows, HEAD_DIM), rows),
            pl.ds(pl.multiple_of(lax.rem(at, cores) * width, HEAD_DIM), width),
        ],
        out_ref,
        sems,
    )
    for copy in copies:
        copy.wait()


def join(cores, own_ref, other_ref, out_ref, sems):
    width = own_ref.shape[1]
    core = lax.rem(lax.axis_index("ka"), cores)
    copies = []
    for i, ref in enumerate((own_ref, other_ref)):
        at = pl.multiple_of(lax.rem(core + (cores - i), cores) * width, HEAD_DIM)
        copies += copy_rows(ref, out_ref.at[:, pl.ds(at, width)], sems.at[i])
    for copy in copies:
        copy.wait()


def on_device(queries, keys, values, q_order, block_mask):
    pb, ka = lax.axis_size("pb"), lax.axis_size("ka")
    class_local, _, block_rows, kv_width = keys.shape
    cores = 2 if ka % 2 == 0 and kv_width == 2 * HEAD_DIM else 1
    rings = ka // cores
    head_width = kv_width // cores
    width = queries.shape[1] // cores
    rows = width // head_width * block_rows
    own_slots = queries.shape[0] // block_rows // ka
    slots = own_slots * cores

    vmem = pl.BlockSpec(memory_space=pltpu.VMEM)
    smem = pl.BlockSpec(memory_space=pltpu.SMEM)

    anywhere = pl.BlockSpec(memory_space=pl.ANY)
    stages = min(STAGES, pb)
    sources = pb // stages

    own_queries = pl.pallas_call(
        functools.partial(fetch, cores),
        out_shape=jax.ShapeDtypeStruct((slots * block_rows, width), queries.dtype),
        in_specs=[anywhere],
        out_specs=vmem,
        scratch_shapes=[pltpu.SemaphoreType.DMA((PARTS,))],
        compiler_params=pltpu.CompilerParams(vmem_limit_bytes=50 * 2**20),
    )(queries)
    raw = [keys, values]
    for c in range(1, cores):
        raw += [turn(keys, ka, cores, 0, c), turn(values, ka, cores, 0, c)]
    start = pl.pallas_call(
        functools.partial(cut, cores),
        out_shape=jax.ShapeDtypeStruct(
            (2 * cores * class_local, block_rows, head_width), keys.dtype
        ),
        in_specs=[vmem] * len(raw),
        out_specs=vmem,
        compiler_params=pltpu.CompilerParams(vmem_limit_bytes=SMALL * 2**20),
    )(*raw)

    start, q_order = lax.optimization_barrier((start, q_order))
    table = jnp.concatenate([q_order[:, None], block_mask], axis=1)
    def blocks_of(where):
        return sum(len(hops) * len(offsets) * class_local for hops, _, offsets in where)

    def call(first, last, turned, pieces, places, earlier, own_queries, state, extra):
        held = blocks_of(places)
        everything = held + blocks_of(earlier)
        here = own_slots if last else slots
        outs = [jax.ShapeDtypeStruct((slots, rows, 2 * HEAD_DIM), jnp.float32)]
        scratch = [
            pltpu.VMEM((held + 1, block_rows, HEAD_DIM), jnp.bfloat16),
            pltpu.VMEM((held + 1, block_rows, 2 * HEAD_DIM), jnp.bfloat16),
            pltpu.VMEM((rows, 2 * block_rows), jnp.bfloat16),
            pltpu.SMEM((max(here * (held + 1) + 1, everything + 1),), jnp.int32),
            pltpu.SMEM((here * (held // 2 + 1),), jnp.int32),
        ]
        if last:
            outs.append(jax.ShapeDtypeStruct((own_slots * block_rows, width), queries.dtype))
            scratch += [
                pltpu.VMEM((rows, HEAD_DIM), jnp.float32),
                pltpu.VMEM((everything, block_rows, HEAD_DIM), jnp.bfloat16),
                pltpu.VMEM((everything, block_rows, 2 * HEAD_DIM), jnp.bfloat16),
            ]
        pooled = held + (everything if last else 0)
        room = LIMIT * 2**20 + pooled * block_rows * HEAD_DIM * 6
        state_at = 2 + len(places) + len(extra)
        return pl.pallas_call(
            functools.partial(
                attend_stage,
                (pb, ka, cores, class_local, places, earlier, slots, turned),
                first,
                last,
                len(extra),
            ),
            out_shape=outs,
            in_specs=[smem]
            + [vmem] * (1 + len(places))
            + [vmem] * (len(extra) + len(state)),
            out_specs=[vmem] * len(outs),
            input_output_aliases={state_at + i: i for i in range(len(state))},
            scratch_shapes=scratch,
            compiler_params=pltpu.CompilerParams(vmem_limit_bytes=room),
            cost_estimate=pl.CostEstimate(
                flops=2**31, bytes_accessed=2**22, transcendentals=2**20
            ),
        )(table, own_queries, *pieces, *extra, *state)

    def along(array, count):
        found = []
        for _ in range(count):
            array = along_ring(array, pb)
            found.append(array)
        return found

    def stacked(arrays):
        return arrays[0] if len(arrays) == 1 else jnp.concatenate(arrays, axis=0)

    def beside(array):
        found = []
        for _ in range(rings - 1):
            array = turn(array, ka, cores, 1, 0)
            found.append(array)
        return found

    every = list(range(cores))
    state, earlier, before = [], [], []

    def work(state, pieces, places):
        state = call(not earlier, False, 0, pieces, places, earlier, own_queries, state, [])
        earlier.extend(places)
        before.extend(pieces)
        return state

    if rings == cores == 2 and pb == STAGES:
        tie = lax.optimization_barrier
        half = start.shape[0] // 2
        on, others = along_ring(start, pb), beside(start)[0]
        state = work(state, [start], [([0], 0, every)])
        again, state = tie((start, state))
        back = along_ring(again, pb, -1)
        on, others, state = tie((on, others, state))
        on_others, two = beside(on)[0], along_ring(on, pb)
        state = work(state, [on, others], [([1], 0, every), ([0], 1, every)])
        back, state = tie((back, state))
        back_others = beside(back)[0]
        on_others, back, state = tie((on_others, back, state))
        two_high = along_ring(on_others[half:], pb)
        state = work(state, [back, on_others], [([pb - 1], 0, every), ([1], 1, every)])
        two, state = tie((two, state))
        two_low = turn(two[:half], ka, cores, 1, 0)
        state = work(state, [two], [([2], 0, every)])
        state = work(state, [back_others], [([pb - 1], 1, every)])
        pieces, places = [two_low, two_high], [([2], 1, [0]), ([2], 1, [1])]
    else:
        arrived = [start] + along(start, sources - 1)
        others, places = [], []
        for stage in range(stages):
            hops = range(stage * sources, (stage + 1) * sources)
            if stage:
                arrived, others, state = lax.optimization_barrier((arrived, others, state))
            near = stacked(arrived)
            pieces, places = [near] + others, [(hops, 0, every)] + places
            if stage < stages - 1:
                arrived = along(arrived[-1], sources)
            others = beside(near)
            state = work(state, pieces, places)
            places = [(hops, y, every) for y in range(1, rings)]
        pieces = others
    halves = []
    for c in reversed(range(cores)):
        *state, half = call(False, True, c, pieces, places, earlier, own_queries, state, before)
        halves.append(half)
    if cores == 1:
        return halves[0]
    return pl.pallas_call(
        functools.partial(join, cores),
        out_shape=jax.ShapeDtypeStruct((own_slots * block_rows, cores * width), queries.dtype),
        in_specs=[vmem] * 2,
        out_specs=anywhere,
        scratch_shapes=[pltpu.SemaphoreType.DMA((cores, PARTS))],
        compiler_params=pltpu.CompilerParams(vmem_limit_bytes=SMALL * 2**20),
    )(halves[1], turn(halves[0], ka, cores, 0, 1))


def solution(mesh):
    in_specs = (
        P("pb", "ha"),
        P("pb", "ka", None, "ha"),
        P("pb", "ka", None, "ha"),
        P("pb"),
        P("pb", None),
    )
    out_specs = P(("pb", "ka"), "ha")
    return jax.shard_map(
        on_device, mesh=mesh, in_specs=in_specs, out_specs=out_specs, check_vma=False
    )
```

```python
import functools
import math

import jax
import jax.numpy as jnp
from jax import lax
from jax.experimental import pallas as pl
from jax.experimental.pallas import tpu as pltpu
from jax.sharding import PartitionSpec as P

HEAD_DIM = 128
MASKED = -1e30
HIDDEN = -1e38
HEADROOM = 64.0
PARTS = 8
LIMIT = 10
SMALL = 4
STAGES = 4


def folded(size):
    return list(range(0, size, 2)) + list(range(1, size, 2))[::-1]


def along_ring(array, size, step=1):
    ring = folded(size)
    return lax.ppermute(array, "pb", [(ring[i], ring[(i + step) % size]) for i in range(size)])


def ring_source(at, size, hops):
    place = jnp.where(at % 2 == 0, at // 2, size - 1 - at // 2)
    place = lax.rem(place + (size - hops), size)
    return jnp.where(place < (size + 1) // 2, 2 * place, 2 * (size - 1 - place) + 1)


def turn(array, size, cores, ring_step, core_step):
    rings = size // cores
    pairs = []
    for ring in range(rings):
        for core in range(cores):
            to = ((ring + ring_step) % rings) * cores + (core + core_step) % cores
            pairs.append((ring * cores + core, to))
    return lax.ppermute(array, "ka", pairs)


def dot(a, b, b_dim):
    return lax.dot_general(a, b, (((1,), (b_dim,)), ((), ())), preferred_element_type=jnp.float32)


def copy_rows(source, target, sems):
    step = source.shape[0] // PARTS
    copies = [
        pltpu.make_async_copy(
            source.at[pl.ds(i * step, step)], target.at[pl.ds(i * step, step)], sems.at[i]
        )
        for i in range(PARTS)
    ]
    for copy in copies:
        copy.start()
    return copies


def attend_stage(plan, first, last, ahead, table_ref, q_ref, *refs):
    pb, ka, cores, class_local, places, earlier, slots, turned = plan
    count = len(places)
    pieces, refs = refs[:count], refs[count:]
    old_pieces, refs = refs[:ahead], refs[ahead:]
    if not first:
        refs = refs[1:]
    acc, refs = refs[0], refs[1:]
    if last:
        out_ref, refs = refs[0], refs[1:]
    k_pool, v_pool, held_weights, entries, units, refs = *refs[:5], refs[5:]
    rows = acc.shape[1]
    block_rows = q_ref.shape[0] // slots
    group = rows // block_rows
    rings = ka // cores
    own_slots = slots // cores
    p_at, k_at = lax.axis_index("pb"), lax.axis_index("ka")
    ring_at, core_at = k_at // cores, lax.rem(k_at, cores)
    scale = math.log2(math.e) / math.sqrt(HEAD_DIM)

    def ids(where):
        found = []
        for hops, y, offsets in where:
            ring = lax.rem(ring_at + (rings - y), rings)
            for z in hops:
                source = ring_source(p_at, pb, z)
                for c in offsets:
                    core = lax.rem(core_at + (cores - c), cores)
                    for t in range(class_local):
                        found.append((source * class_local + t) * ka + ring * cores + core)
        return found

    def pool_from(refs_in, at, k_out, v_out):
        for piece in refs_in:
            for i in range(0, piece.shape[0], 2 * class_local):
                span = slice(at, at + class_local)
                k_out[span] = piece[i : i + class_local]
                value = piece[i + class_local : i + 2 * class_local]
                v_out[span, :, :HEAD_DIM] = value
                v_out[span, :, HEAD_DIM:] = jnp.ones(value.shape, v_out.dtype)
                at += class_local

    nothing = sum(piece.shape[0] for piece in pieces) // 2

    if last:
        mine = lax.rem(core_at + turned, cores) * own_slots
        slot_ids = [mine + i for i in range(own_slots)]
    else:
        slot_ids = list(range(slots))

    row_id = lax.broadcasted_iota(jnp.int32, (block_rows, block_rows), 0)
    col_id = lax.broadcasted_iota(jnp.int32, (block_rows, block_rows), 1)
    pool_from(pieces, 0, k_pool, v_pool)
    k_pool[nothing] = jnp.zeros(k_pool.shape[1:], k_pool.dtype)
    v_pool[nothing] = jnp.zeros(v_pool.shape[1:], v_pool.dtype)

    blocks = ids(places)
    unit_count = jnp.int32(0)
    for s in slot_ids:
        row = ring_at * slots + s
        own = table_ref[row, 0]
        place = 2 * unit_count
        for index, block in enumerate(blocks):
            entries[place] = jnp.where(block == own, index + nothing + 1, index)
            place = place + table_ref[row, 1 + block]
        entries[place] = nothing
        ends = lax.div(place + 1, 2)
        if first:

            @pl.when(ends == unit_count)
            def _(s=s):
                acc[s] = jnp.zeros(acc.shape[1:], acc.dtype)


        def mark(u, carry, s=s):
            units[u] = s
            return carry

        lax.fori_loop(unit_count, ends, mark, 0)
        unit_count = ends
    def query_rows(s):
        return jnp.concatenate(
            [
                q_ref[
                    pl.ds(pl.multiple_of(s * block_rows, block_rows), block_rows),
                    x * HEAD_DIM : (x + 1) * HEAD_DIM,
                ]
                for x in range(group)
            ],
            axis=0,
        )

    def pair_of(u):
        raw = [entries[2 * u], entries[2 * u + 1]]
        owns = [entry > nothing for entry in raw]
        return owns, [jnp.where(o, e - (nothing + 1), e) for o, e in zip(owns, raw)]

    def weigh(u):
        owns, index = pair_of(u)
        keys = jnp.concatenate([k_pool[i] for i in index], axis=0)
        reach = jnp.concatenate(
            [
                jnp.where(col_id <= row_id + jnp.where(own, 0, block_rows), 0.0, HIDDEN)
                for own in owns
            ],
            axis=1,
        )
        power = dot(query_rows(units[u]), keys, 1) * scale
        power = power + jnp.concatenate([reach] * group, axis=0)
        held_weights[...] = jnp.exp2(power).astype(held_weights.dtype)

    def add(u):
        _, index = pair_of(u)
        s = units[u]
        values = jnp.concatenate([v_pool[i] for i in index], axis=0)
        added = dot(held_weights[...], values, 0)
        old = acc[s]
        if first:
            fresh = (u == 0) | (units[jnp.maximum(u - 1, 0)] != s)
            old = jnp.where(fresh, 0.0, old)
        acc[s] = old + added

    @pl.when(unit_count > 0)
    def _():
        weigh(0)

        def both(u, carry):
            add(u)
            weigh(u + 1)
            return carry

        lax.fori_loop(0, unit_count - 1, both, 0)
        add(unit_count - 1)

    if not last:
        return

    top, k_all, v_all = refs

    def finish(s, i):
        under = acc[s, :, HEAD_DIM:]
        result = (acc[s, :, :HEAD_DIM] / under).astype(out_ref.dtype)
        for x in range(group):
            out_ref[
                i * block_rows : (i + 1) * block_rows, x * HEAD_DIM : (x + 1) * HEAD_DIM
            ] = result[x * block_rows : (x + 1) * block_rows]
        low = high = [under[j : j + 8] for j in range(0, rows, 8)]
        while len(low) > 1:
            low = [functools.reduce(jnp.minimum, low[j : j + 2]) for j in range(0, len(low), 2)]
            high = [functools.reduce(jnp.maximum, high[j : j + 2]) for j in range(0, len(high), 2)]
        return low[0], high[0]

    low, high = zip(*[finish(s, i) for i, s in enumerate(slot_ids)])
    low, high = functools.reduce(jnp.minimum, low), functools.reduce(jnp.maximum, high)
    safe = (low > 2.0**-HEADROOM) & (high < 2.0**HEADROOM)

    @pl.when(jnp.min(jnp.where(safe, 1.0, 0.0)) < 0.5)
    def _():
        pool_from(old_pieces, 0, k_all, v_all)
        pool_from(pieces, sum(p.shape[0] for p in old_pieces) // 2, k_all, v_all)
        blocks_all = ids(earlier) + blocks
        for i, s in enumerate(slot_ids):
            row = ring_at * slots + s
            own = table_ref[row, 0]
            place = jnp.int32(0)
            for index, block in enumerate(blocks_all):
                entries[place] = jnp.where(block == own, index + len(blocks_all), index)
                place = place + table_ref[row, 1 + block]
            acc[s] = jnp.zeros(acc.shape[1:], acc.dtype)
            top[...] = jnp.full(top.shape, MASKED, top.dtype)

            def one_block(e, carry, s=s):
                is_own = entries[e] >= len(blocks_all)
                index = jnp.where(is_own, entries[e] - len(blocks_all), entries[e])
                reach = jnp.where(
                    col_id <= row_id + jnp.where(is_own, 0, block_rows), 0.0, HIDDEN
                )
                scores = dot(query_rows(s), k_all[index], 1)
                weights, shrinks = [], []
                for x in range(group):
                    span = slice(x * block_rows, (x + 1) * block_rows)
                    power = scores[span] * scale + reach
                    new = jnp.maximum(top[span], jnp.max(power, axis=1, keepdims=True))
                    shrink = jnp.exp2(top[span] - new)
                    top[span] = new
                    weights.append(jnp.exp2(power - new).astype(jnp.bfloat16))
                    shrinks.append(jnp.concatenate([shrink, shrink], axis=1))
                added = dot(jnp.concatenate(weights, axis=0), v_all[index], 0)
                acc[s] = acc[s] * jnp.concatenate(shrinks, axis=0) + added
                return carry

            lax.fori_loop(0, place, one_block, 0)
            finish(s, i)


def cut(cores, *refs):
    ins, out_ref = refs[:-1], refs[-1]
    count = ins[0].shape[0]
    width = out_ref.shape[2]
    core = lax.rem(lax.axis_index("ka"), cores)
    for c in range(cores):

        @pl.when(core == c)
        def _():
            for i, ref in enumerate(ins):
                out_ref[i * count : (i + 1) * count] = ref[
                    :, 0, :, c * width : (c + 1) * width
                ]


def fetch(cores, queries_ref, out_ref, sems):
    rows, width = out_ref.shape
    at = lax.axis_index("ka")
    copies = copy_rows(
        queries_ref.at[
            pl.ds(pl.multiple_of(at // cores * rows, HEAD_DIM), rows),
            pl.ds(pl.multiple_of(lax.rem(at, cores) * width, HEAD_DIM), width),
        ],
        out_ref,
        sems,
    )
    for copy in copies:
        copy.wait()


def join(cores, own_ref, other_ref, out_ref, sems):
    width = own_ref.shape[1]
    core = lax.rem(lax.axis_index("ka"), cores)
    copies = []
    for i, ref in enumerate((own_ref, other_ref)):
        at = pl.multiple_of(lax.rem(core + (cores - i), cores) * width, HEAD_DIM)
        copies += copy_rows(ref, out_ref.at[:, pl.ds(at, width)], sems.at[i])
    for copy in copies:
        copy.wait()


def on_device(queries, keys, values, q_order, block_mask):
    pb, ka = lax.axis_size("pb"), lax.axis_size("ka")
    class_local, _, block_rows, kv_width = keys.shape
    cores = 2 if ka % 2 == 0 and kv_width == 2 * HEAD_DIM else 1
    rings = ka // cores
    head_width = kv_width // cores
    width = queries.shape[1] // cores
    rows = width // head_width * block_rows
    own_slots = queries.shape[0] // block_rows // ka
    slots = own_slots * cores

    vmem = pl.BlockSpec(memory_space=pltpu.VMEM)
    smem = pl.BlockSpec(memory_space=pltpu.SMEM)

    anywhere = pl.BlockSpec(memory_space=pl.ANY)
    stages = min(STAGES, pb)
    sources = pb // stages

    own_queries = pl.pallas_call(
        functools.partial(fetch, cores),
        out_shape=jax.ShapeDtypeStruct((slots * block_rows, width), queries.dtype),
        in_specs=[anywhere],
        out_specs=vmem,
        scratch_shapes=[pltpu.SemaphoreType.DMA((PARTS,))],
        compiler_params=pltpu.CompilerParams(vmem_limit_bytes=50 * 2**20),
    )(queries)
    raw = [keys, values]
    for c in range(1, cores):
        raw += [turn(keys, ka, cores, 0, c), turn(values, ka, cores, 0, c)]
    start = pl.pallas_call(
        functools.partial(cut, cores),
        out_shape=jax.ShapeDtypeStruct(
            (2 * cores * class_local, block_rows, head_width), keys.dtype
        ),
        in_specs=[vmem] * len(raw),
        out_specs=vmem,
        compiler_params=pltpu.CompilerParams(vmem_limit_bytes=SMALL * 2**20),
    )(*raw)

    start, q_order = lax.optimization_barrier((start, q_order))
    table = jnp.concatenate([q_order[:, None], block_mask], axis=1)
    def blocks_of(where):
        return sum(len(hops) * len(offsets) * class_local for hops, _, offsets in where)

    def call(first, last, turned, pieces, places, earlier, own_queries, state, extra):
        held = blocks_of(places)
        everything = held + blocks_of(earlier)
        here = own_slots if last else slots
        outs = [jax.ShapeDtypeStruct((slots, rows, 2 * HEAD_DIM), jnp.float32)]
        scratch = [
            pltpu.VMEM((held + 1, block_rows, HEAD_DIM), jnp.bfloat16),
            pltpu.VMEM((held + 1, block_rows, 2 * HEAD_DIM), jnp.bfloat16),
            pltpu.VMEM((rows, 2 * block_rows), jnp.bfloat16),
            pltpu.SMEM((max(here * (held + 1) + 1, everything + 1),), jnp.int32),
            pltpu.SMEM((here * (held // 2 + 1),), jnp.int32),
        ]
        if last:
            outs.append(jax.ShapeDtypeStruct((own_slots * block_rows, width), queries.dtype))
            scratch += [
                pltpu.VMEM((rows, HEAD_DIM), jnp.float32),
                pltpu.VMEM((everything, block_rows, HEAD_DIM), jnp.bfloat16),
                pltpu.VMEM((everything, block_rows, 2 * HEAD_DIM), jnp.bfloat16),
            ]
        pooled = held + (everything if last else 0)
        room = LIMIT * 2**20 + pooled * block_rows * HEAD_DIM * 6
        state_at = 2 + len(places) + len(extra)
        return pl.pallas_call(
            functools.partial(
                attend_stage,
                (pb, ka, cores, class_local, places, earlier, slots, turned),
                first,
                last,
                len(extra),
            ),
            out_shape=outs,
            in_specs=[smem]
            + [vmem] * (1 + len(places))
            + [vmem] * (len(extra) + len(state)),
            out_specs=[vmem] * len(outs),
            input_output_aliases={state_at + i: i for i in range(len(state))},
            scratch_shapes=scratch,
            compiler_params=pltpu.CompilerParams(vmem_limit_bytes=room),
            cost_estimate=pl.CostEstimate(
                flops=2**31, bytes_accessed=2**22, transcendentals=2**20
            ),
        )(table, own_queries, *pieces, *extra, *state)

    def along(array, count):
        found = []
        for _ in range(count):
            array = along_ring(array, pb)
            found.append(array)
        return found

    def stacked(arrays):
        return arrays[0] if len(arrays) == 1 else jnp.concatenate(arrays, axis=0)

    def beside(array):
        found = []
        for _ in range(rings - 1):
            array = turn(array, ka, cores, 1, 0)
            found.append(array)
        return found

    every = list(range(cores))
    state, earlier, before = [], [], []

    def work(state, pieces, places):
        state = call(not earlier, False, 0, pieces, places, earlier, own_queries, state, [])
        earlier.extend(places)
        before.extend(pieces)
        return state

    if rings == cores == 2 and pb == STAGES:
        tie = lax.optimization_barrier
        half = start.shape[0] // 2
        on, others = along_ring(start, pb), beside(start)[0]
        state = work(state, [start], [([0], 0, every)])
        again, others, state = tie((start, others, state))
        back = along_ring(again, pb, -1)
        on_others = beside(on)[0]
        state = work(state, [on, others], [([1], 0, every), ([0], 1, every)])
        on, state = tie((on, state))
        two = along_ring(on, pb)
        back, state = tie((back, state))
        back_others = beside(back)[0]
        on_others, back, state = tie((on_others, back, state))
        two_high = along_ring(on_others[half:], pb)
        state = work(state, [back, on_others], [([pb - 1], 0, every), ([1], 1, every)])
        two, state = tie((two, state))
        two_low = turn(two[:half], ka, cores, 1, 0)
        state = work(state, [two], [([2], 0, every)])
        state = work(state, [back_others], [([pb - 1], 1, every)])
        pieces, places = [two_low, two_high], [([2], 1, [0]), ([2], 1, [1])]
    else:
        arrived = [start] + along(start, sources - 1)
        others, places = [], []
        for stage in range(stages):
            hops = range(stage * sources, (stage + 1) * sources)
            if stage:
                arrived, others, state = lax.optimization_barrier((arrived, others, state))
            near = stacked(arrived)
            pieces, places = [near] + others, [(hops, 0, every)] + places
            if stage < stages - 1:
                arrived = along(arrived[-1], sources)
            others = beside(near)
            state = work(state, pieces, places)
            places = [(hops, y, every) for y in range(1, rings)]
        pieces = others
    halves = []
    for c in reversed(range(cores)):
        *state, half = call(False, True, c, pieces, places, earlier, own_queries, state, before)
        halves.append(half)
    if cores == 1:
        return halves[0]
    return pl.pallas_call(
        functools.partial(join, cores),
        out_shape=jax.ShapeDtypeStruct((own_slots * block_rows, cores * width), queries.dtype),
        in_specs=[vmem] * 2,
        out_specs=anywhere,
        scratch_shapes=[pltpu.SemaphoreType.DMA((cores, PARTS))],
        compiler_params=pltpu.CompilerParams(vmem_limit_bytes=SMALL * 2**20),
    )(halves[1], turn(halves[0], ka, cores, 0, 1))


def solution(mesh):
    in_specs = (
        P("pb", "ha"),
        P("pb", "ka", None, "ha"),
        P("pb", "ka", None, "ha"),
        P("pb"),
        P("pb", None),
    )
    out_specs = P(("pb", "ka"), "ha")
    return jax.shard_map(
        on_device, mesh=mesh, in_specs=in_specs, out_specs=out_specs, check_vma=False
    )
```

```python
import functools
import math

import jax
import jax.numpy as jnp
from jax import lax
from jax.experimental import pallas as pl
from jax.experimental.pallas import tpu as pltpu
from jax.sharding import PartitionSpec as P

HEAD_DIM = 128
MASKED = -1e30
HIDDEN = -1e38
HEADROOM = 64.0
PARTS = 8
LIMIT = 10
SMALL = 4
STAGES = 4


def folded(size):
    return list(range(0, size, 2)) + list(range(1, size, 2))[::-1]


def along_ring(array, size, step=1):
    ring = folded(size)
    return lax.ppermute(array, "pb", [(ring[i], ring[(i + step) % size]) for i in range(size)])


def ring_source(at, size, hops):
    place = jnp.where(at % 2 == 0, at // 2, size - 1 - at // 2)
    place = lax.rem(place + (size - hops), size)
    return jnp.where(place < (size + 1) // 2, 2 * place, 2 * (size - 1 - place) + 1)


def turn(array, size, cores, ring_step, core_step):
    rings = size // cores
    pairs = []
    for ring in range(rings):
        for core in range(cores):
            to = ((ring + ring_step) % rings) * cores + (core + core_step) % cores
            pairs.append((ring * cores + core, to))
    return lax.ppermute(array, "ka", pairs)


def dot(a, b, b_dim):
    return lax.dot_general(a, b, (((1,), (b_dim,)), ((), ())), preferred_element_type=jnp.float32)


def copy_rows(source, target, sems):
    step = source.shape[0] // PARTS
    copies = [
        pltpu.make_async_copy(
            source.at[pl.ds(i * step, step)], target.at[pl.ds(i * step, step)], sems.at[i]
        )
        for i in range(PARTS)
    ]
    for copy in copies:
        copy.start()
    return copies


def attend_stage(plan, first, last, ahead, table_ref, q_ref, *refs):
    pb, ka, cores, class_local, places, earlier, slots, turned = plan
    count = len(places)
    pieces, refs = refs[:count], refs[count:]
    old_pieces, refs = refs[:ahead], refs[ahead:]
    if not first:
        refs = refs[1:]
    acc, refs = refs[0], refs[1:]
    if last:
        out_ref, refs = refs[0], refs[1:]
    k_pool, v_pool, held_weights, entries, units, refs = *refs[:5], refs[5:]
    rows = acc.shape[1]
    block_rows = q_ref.shape[0] // slots
    group = rows // block_rows
    rings = ka // cores
    own_slots = slots // cores
    p_at, k_at = lax.axis_index("pb"), lax.axis_index("ka")
    ring_at, core_at = k_at // cores, lax.rem(k_at, cores)
    scale = math.log2(math.e) / math.sqrt(HEAD_DIM)

    def ids(where):
        found = []
        for hops, y, offsets in where:
            ring = lax.rem(ring_at + (rings - y), rings)
            for z in hops:
                source = ring_source(p_at, pb, z)
                for c in offsets:
                    core = lax.rem(core_at + (cores - c), cores)
                    for t in range(class_local):
                        found.append((source * class_local + t) * ka + ring * cores + core)
        return found

    def pool_from(refs_in, at, k_out, v_out):
        for piece in refs_in:
            for i in range(0, piece.shape[0], 2 * class_local):
                span = slice(at, at + class_local)
                k_out[span] = piece[i : i + class_local]
                value = piece[i + class_local : i + 2 * class_local]
                v_out[span, :, :HEAD_DIM] = value
                v_out[span, :, HEAD_DIM:] = jnp.ones(value.shape, v_out.dtype)
                at += class_local

    nothing = sum(piece.shape[0] for piece in pieces) // 2

    if last:
        mine = lax.rem(core_at + turned, cores) * own_slots
        slot_ids = [mine + i for i in range(own_slots)]
    else:
        slot_ids = list(range(slots))

    row_id = lax.broadcasted_iota(jnp.int32, (block_rows, block_rows), 0)
    col_id = lax.broadcasted_iota(jnp.int32, (block_rows, block_rows), 1)
    pool_from(pieces, 0, k_pool, v_pool)
    k_pool[nothing] = jnp.zeros(k_pool.shape[1:], k_pool.dtype)
    v_pool[nothing] = jnp.zeros(v_pool.shape[1:], v_pool.dtype)

    blocks = ids(places)
    unit_count = jnp.int32(0)
    for s in slot_ids:
        row = ring_at * slots + s
        own = table_ref[row, 0]
        place = 2 * unit_count
        for index, block in enumerate(blocks):
            entries[place] = jnp.where(block == own, index + nothing + 1, index)
            place = place + table_ref[row, 1 + block]
        entries[place] = nothing
        ends = lax.div(place + 1, 2)
        if first:

            @pl.when(ends == unit_count)
            def _(s=s):
                acc[s] = jnp.zeros(acc.shape[1:], acc.dtype)


        def mark(u, carry, s=s):
            units[u] = s
            return carry

        lax.fori_loop(unit_count, ends, mark, 0)
        unit_count = ends
    def query_rows(s):
        return jnp.concatenate(
            [
                q_ref[
                    pl.ds(pl.multiple_of(s * block_rows, block_rows), block_rows),
                    x * HEAD_DIM : (x + 1) * HEAD_DIM,
                ]
                for x in range(group)
            ],
            axis=0,
        )

    def pair_of(u):
        raw = [entries[2 * u], entries[2 * u + 1]]
        owns = [entry > nothing for entry in raw]
        return owns, [jnp.where(o, e - (nothing + 1), e) for o, e in zip(owns, raw)]

    def weigh(u):
        owns, index = pair_of(u)
        keys = jnp.concatenate([k_pool[i] for i in index], axis=0)
        reach = jnp.concatenate(
            [
                jnp.where(col_id <= row_id + jnp.where(own, 0, block_rows), 0.0, HIDDEN)
                for own in owns
            ],
            axis=1,
        )
        power = dot(query_rows(units[u]), keys, 1) * scale
        power = power + jnp.concatenate([reach] * group, axis=0)
        held_weights[...] = jnp.exp2(power).astype(held_weights.dtype)

    def add(u):
        _, index = pair_of(u)
        s = units[u]
        values = jnp.concatenate([v_pool[i] for i in index], axis=0)
        added = dot(held_weights[...], values, 0)
        old = acc[s]
        if first:
            fresh = (u == 0) | (units[jnp.maximum(u - 1, 0)] != s)
            old = jnp.where(fresh, 0.0, old)
        acc[s] = old + added

    @pl.when(unit_count > 0)
    def _():
        weigh(0)

        def both(u, carry):
            add(u)
            weigh(u + 1)
            return carry

        lax.fori_loop(0, unit_count - 1, both, 0)
        add(unit_count - 1)

    if not last:
        return

    top, k_all, v_all = refs

    def finish(s, i):
        under = acc[s, :, HEAD_DIM:]
        result = (acc[s, :, :HEAD_DIM] / under).astype(out_ref.dtype)
        for x in range(group):
            out_ref[
                i * block_rows : (i + 1) * block_rows, x * HEAD_DIM : (x + 1) * HEAD_DIM
            ] = result[x * block_rows : (x + 1) * block_rows]
        low = high = [under[j : j + 8] for j in range(0, rows, 8)]
        while len(low) > 1:
            low = [functools.reduce(jnp.minimum, low[j : j + 2]) for j in range(0, len(low), 2)]
            high = [functools.reduce(jnp.maximum, high[j : j + 2]) for j in range(0, len(high), 2)]
        return low[0], high[0]

    low, high = zip(*[finish(s, i) for i, s in enumerate(slot_ids)])
    low, high = functools.reduce(jnp.minimum, low), functools.reduce(jnp.maximum, high)
    safe = (low > 2.0**-HEADROOM) & (high < 2.0**HEADROOM)

    @pl.when(jnp.min(jnp.where(safe, 1.0, 0.0)) < 0.5)
    def _():
        pool_from(old_pieces, 0, k_all, v_all)
        pool_from(pieces, sum(p.shape[0] for p in old_pieces) // 2, k_all, v_all)
        blocks_all = ids(earlier) + blocks
        for i, s in enumerate(slot_ids):
            row = ring_at * slots + s
            own = table_ref[row, 0]
            place = jnp.int32(0)
            for index, block in enumerate(blocks_all):
                entries[place] = jnp.where(block == own, index + len(blocks_all), index)
                place = place + table_ref[row, 1 + block]
            acc[s] = jnp.zeros(acc.shape[1:], acc.dtype)
            top[...] = jnp.full(top.shape, MASKED, top.dtype)

            def one_block(e, carry, s=s):
                is_own = entries[e] >= len(blocks_all)
                index = jnp.where(is_own, entries[e] - len(blocks_all), entries[e])
                reach = jnp.where(
                    col_id <= row_id + jnp.where(is_own, 0, block_rows), 0.0, HIDDEN
                )
                scores = dot(query_rows(s), k_all[index], 1)
                weights, shrinks = [], []
                for x in range(group):
                    span = slice(x * block_rows, (x + 1) * block_rows)
                    power = scores[span] * scale + reach
                    new = jnp.maximum(top[span], jnp.max(power, axis=1, keepdims=True))
                    shrink = jnp.exp2(top[span] - new)
                    top[span] = new
                    weights.append(jnp.exp2(power - new).astype(jnp.bfloat16))
                    shrinks.append(jnp.concatenate([shrink, shrink], axis=1))
                added = dot(jnp.concatenate(weights, axis=0), v_all[index], 0)
                acc[s] = acc[s] * jnp.concatenate(shrinks, axis=0) + added
                return carry

            lax.fori_loop(0, place, one_block, 0)
            finish(s, i)


def cut(cores, *refs):
    ins, out_ref = refs[:-1], refs[-1]
    count = ins[0].shape[0]
    width = out_ref.shape[2]
    core = lax.rem(lax.axis_index("ka"), cores)
    for c in range(cores):

        @pl.when(core == c)
        def _():
            for i, ref in enumerate(ins):
                out_ref[i * count : (i + 1) * count] = ref[
                    :, 0, :, c * width : (c + 1) * width
                ]


def fetch(cores, queries_ref, out_ref, sems):
    rows, width = out_ref.shape
    at = lax.axis_index("ka")
    copies = copy_rows(
        queries_ref.at[
            pl.ds(pl.multiple_of(at // cores * rows, HEAD_DIM), rows),
            pl.ds(pl.multiple_of(lax.rem(at, cores) * width, HEAD_DIM), width),
        ],
        out_ref,
        sems,
    )
    for copy in copies:
        copy.wait()


def join(cores, own_ref, other_ref, out_ref, sems):
    width = own_ref.shape[1]
    core = lax.rem(lax.axis_index("ka"), cores)
    copies = []
    for i, ref in enumerate((own_ref, other_ref)):
        at = pl.multiple_of(lax.rem(core + (cores - i), cores) * width, HEAD_DIM)
        copies += copy_rows(ref, out_ref.at[:, pl.ds(at, width)], sems.at[i])
    for copy in copies:
        copy.wait()


def on_device(queries, keys, values, q_order, block_mask):
    pb, ka = lax.axis_size("pb"), lax.axis_size("ka")
    class_local, _, block_rows, kv_width = keys.shape
    cores = 2 if ka % 2 == 0 and kv_width == 2 * HEAD_DIM else 1
    rings = ka // cores
    head_width = kv_width // cores
    width = queries.shape[1] // cores
    rows = width // head_width * block_rows
    own_slots = queries.shape[0] // block_rows // ka
    slots = own_slots * cores

    vmem = pl.BlockSpec(memory_space=pltpu.VMEM)
    smem = pl.BlockSpec(memory_space=pltpu.SMEM)

    anywhere = pl.BlockSpec(memory_space=pl.ANY)
    stages = min(STAGES, pb)
    sources = pb // stages

    own_queries = pl.pallas_call(
        functools.partial(fetch, cores),
        out_shape=jax.ShapeDtypeStruct((slots * block_rows, width), queries.dtype),
        in_specs=[anywhere],
        out_specs=vmem,
        scratch_shapes=[pltpu.SemaphoreType.DMA((PARTS,))],
        compiler_params=pltpu.CompilerParams(vmem_limit_bytes=50 * 2**20),
    )(queries)
    raw = [keys, values]
    for c in range(1, cores):
        raw += [turn(keys, ka, cores, 0, c), turn(values, ka, cores, 0, c)]
    start = pl.pallas_call(
        functools.partial(cut, cores),
        out_shape=jax.ShapeDtypeStruct(
            (2 * cores * class_local, block_rows, head_width), keys.dtype
        ),
        in_specs=[vmem] * len(raw),
        out_specs=vmem,
        compiler_params=pltpu.CompilerParams(vmem_limit_bytes=SMALL * 2**20),
    )(*raw)

    start, q_order = lax.optimization_barrier((start, q_order))
    table = jnp.concatenate([q_order[:, None], block_mask], axis=1)
    def blocks_of(where):
        return sum(len(hops) * len(offsets) * class_local for hops, _, offsets in where)

    def call(first, last, turned, pieces, places, earlier, own_queries, state, extra):
        held = blocks_of(places)
        everything = held + blocks_of(earlier)
        here = own_slots if last else slots
        outs = [jax.ShapeDtypeStruct((slots, rows, 2 * HEAD_DIM), jnp.float32)]
        scratch = [
            pltpu.VMEM((held + 1, block_rows, HEAD_DIM), jnp.bfloat16),
            pltpu.VMEM((held + 1, block_rows, 2 * HEAD_DIM), jnp.bfloat16),
            pltpu.VMEM((rows, 2 * block_rows), jnp.bfloat16),
            pltpu.SMEM((max(here * (held + 1) + 1, everything + 1),), jnp.int32),
            pltpu.SMEM((here * (held // 2 + 1),), jnp.int32),
        ]
        if last:
            outs.append(jax.ShapeDtypeStruct((own_slots * block_rows, width), queries.dtype))
            scratch += [
                pltpu.VMEM((rows, HEAD_DIM), jnp.float32),
                pltpu.VMEM((everything, block_rows, HEAD_DIM), jnp.bfloat16),
                pltpu.VMEM((everything, block_rows, 2 * HEAD_DIM), jnp.bfloat16),
            ]
        pooled = held + (everything if last else 0)
        room = LIMIT * 2**20 + pooled * block_rows * HEAD_DIM * 6
        state_at = 2 + len(places) + len(extra)
        return pl.pallas_call(
            functools.partial(
                attend_stage,
                (pb, ka, cores, class_local, places, earlier, slots, turned),
                first,
                last,
                len(extra),
            ),
            out_shape=outs,
            in_specs=[smem]
            + [vmem] * (1 + len(places))
            + [vmem] * (len(extra) + len(state)),
            out_specs=[vmem] * len(outs),
            input_output_aliases={state_at + i: i for i in range(len(state))},
            scratch_shapes=scratch,
            compiler_params=pltpu.CompilerParams(vmem_limit_bytes=room),
            cost_estimate=pl.CostEstimate(
                flops=2**31, bytes_accessed=2**22, transcendentals=2**20
            ),
        )(table, own_queries, *pieces, *extra, *state)

    def along(array, count):
        found = []
        for _ in range(count):
            array = along_ring(array, pb)
            found.append(array)
        return found

    def stacked(arrays):
        return arrays[0] if len(arrays) == 1 else jnp.concatenate(arrays, axis=0)

    def beside(array):
        found = []
        for _ in range(rings - 1):
            array = turn(array, ka, cores, 1, 0)
            found.append(array)
        return found

    every = list(range(cores))
    state, earlier, before = [], [], []

    def work(state, pieces, places):
        state = call(not earlier, False, 0, pieces, places, earlier, own_queries, state, [])
        earlier.extend(places)
        before.extend(pieces)
        return state

    if rings == cores == 2 and pb == STAGES:
        tie = lax.optimization_barrier
        half = start.shape[0] // 2
        on = along_ring(start, pb)
        state = work(state, [start], [([0], 0, every)])
        again, state = tie((start, state))
        back, others = along_ring(again, pb, -1), beside(again)[0]
        on, state = tie((on, state))
        on_others, two = beside(on)[0], along_ring(on, pb)
        state = work(state, [on, others], [([1], 0, every), ([0], 1, every)])
        back, state = tie((back, state))
        back_others = beside(back)[0]
        on_others, back, state = tie((on_others, back, state))
        two_high = along_ring(on_others[half:], pb)
        state = work(state, [back, on_others], [([pb - 1], 0, every), ([1], 1, every)])
        two, state = tie((two, state))
        two_low = turn(two[:half], ka, cores, 1, 0)
        state = work(state, [two], [([2], 0, every)])
        state = work(state, [back_others], [([pb - 1], 1, every)])
        pieces, places = [two_low, two_high], [([2], 1, [0]), ([2], 1, [1])]
    else:
        arrived = [start] + along(start, sources - 1)
        others, places = [], []
        for stage in range(stages):
            hops = range(stage * sources, (stage + 1) * sources)
            if stage:
                arrived, others, state = lax.optimization_barrier((arrived, others, state))
            near = stacked(arrived)
            pieces, places = [near] + others, [(hops, 0, every)] + places
            if stage < stages - 1:
                arrived = along(arrived[-1], sources)
            others = beside(near)
            state = work(state, pieces, places)
            places = [(hops, y, every) for y in range(1, rings)]
        pieces = others
    halves = []
    for c in reversed(range(cores)):
        *state, half = call(False, True, c, pieces, places, earlier, own_queries, state, before)
        halves.append(half)
    if cores == 1:
        return halves[0]
    return pl.pallas_call(
        functools.partial(join, cores),
        out_shape=jax.ShapeDtypeStruct((own_slots * block_rows, cores * width), queries.dtype),
        in_specs=[vmem] * 2,
        out_specs=anywhere,
        scratch_shapes=[pltpu.SemaphoreType.DMA((cores, PARTS))],
        compiler_params=pltpu.CompilerParams(vmem_limit_bytes=SMALL * 2**20),
    )(halves[1], turn(halves[0], ka, cores, 0, 1))


def solution(mesh):
    in_specs = (
        P("pb", "ha"),
        P("pb", "ka", None, "ha"),
        P("pb", "ka", None, "ha"),
        P("pb"),
        P("pb", None),
    )
    out_specs = P(("pb", "ka"), "ha")
    return jax.shard_map(
        on_device, mesh=mesh, in_specs=in_specs, out_specs=out_specs, check_vma=False
    )
```

```python
import functools
import math

import jax
import jax.numpy as jnp
from jax import lax
from jax.experimental import pallas as pl
from jax.experimental.pallas import tpu as pltpu
from jax.sharding import PartitionSpec as P

HEAD_DIM = 128
MASKED = -1e30
HIDDEN = -1e38
HEADROOM = 64.0
PARTS = 8
LIMIT = 10
SMALL = 4
STAGES = 4


def folded(size):
    return list(range(0, size, 2)) + list(range(1, size, 2))[::-1]


def along_ring(array, size, step=1):
    ring = folded(size)
    return lax.ppermute(array, "pb", [(ring[i], ring[(i + step) % size]) for i in range(size)])


def ring_source(at, size, hops):
    place = jnp.where(at % 2 == 0, at // 2, size - 1 - at // 2)
    place = lax.rem(place + (size - hops), size)
    return jnp.where(place < (size + 1) // 2, 2 * place, 2 * (size - 1 - place) + 1)


def turn(array, size, cores, ring_step, core_step):
    rings = size // cores
    pairs = []
    for ring in range(rings):
        for core in range(cores):
            to = ((ring + ring_step) % rings) * cores + (core + core_step) % cores
            pairs.append((ring * cores + core, to))
    return lax.ppermute(array, "ka", pairs)


def dot(a, b, b_dim):
    return lax.dot_general(a, b, (((1,), (b_dim,)), ((), ())), preferred_element_type=jnp.float32)


def copy_rows(source, target, sems):
    step = source.shape[0] // PARTS
    copies = [
        pltpu.make_async_copy(
            source.at[pl.ds(i * step, step)], target.at[pl.ds(i * step, step)], sems.at[i]
        )
        for i in range(PARTS)
    ]
    for copy in copies:
        copy.start()
    return copies


def attend_stage(plan, first, last, ahead, table_ref, q_ref, *refs):
    pb, ka, cores, class_local, places, earlier, slots, turned = plan
    count = len(places)
    pieces, refs = refs[:count], refs[count:]
    old_pieces, refs = refs[:ahead], refs[ahead:]
    if not first:
        refs = refs[1:]
    acc, refs = refs[0], refs[1:]
    if last:
        out_ref, refs = refs[0], refs[1:]
    k_pool, v_pool, held_weights, entries, units, refs = *refs[:5], refs[5:]
    rows = acc.shape[1]
    block_rows = q_ref.shape[0] // slots
    group = rows // block_rows
    rings = ka // cores
    own_slots = slots // cores
    p_at, k_at = lax.axis_index("pb"), lax.axis_index("ka")
    ring_at, core_at = k_at // cores, lax.rem(k_at, cores)
    scale = math.log2(math.e) / math.sqrt(HEAD_DIM)

    def ids(where):
        found = []
        for hops, y, offsets in where:
            ring = lax.rem(ring_at + (rings - y), rings)
            for z in hops:
                source = ring_source(p_at, pb, z)
                for c in offsets:
                    core = lax.rem(core_at + (cores - c), cores)
                    for t in range(class_local):
                        found.append((source * class_local + t) * ka + ring * cores + core)
        return found

    def pool_from(refs_in, at, k_out, v_out):
        for piece in refs_in:
            for i in range(0, piece.shape[0], 2 * class_local):
                span = slice(at, at + class_local)
                k_out[span] = piece[i : i + class_local]
                value = piece[i + class_local : i + 2 * class_local]
                v_out[span, :, :HEAD_DIM] = value
                v_out[span, :, HEAD_DIM:] = jnp.ones(value.shape, v_out.dtype)
                at += class_local

    nothing = sum(piece.shape[0] for piece in pieces) // 2

    if last:
        mine = lax.rem(core_at + turned, cores) * own_slots
        slot_ids = [mine + i for i in range(own_slots)]
    else:
        slot_ids = list(range(slots))

    row_id = lax.broadcasted_iota(jnp.int32, (block_rows, block_rows), 0)
    col_id = lax.broadcasted_iota(jnp.int32, (block_rows, block_rows), 1)
    pool_from(pieces, 0, k_pool, v_pool)
    k_pool[nothing] = jnp.zeros(k_pool.shape[1:], k_pool.dtype)
    v_pool[nothing] = jnp.zeros(v_pool.shape[1:], v_pool.dtype)

    blocks = ids(places)
    unit_count = jnp.int32(0)
    for s in slot_ids:
        row = ring_at * slots + s
        own = table_ref[row, 0]
        place = 2 * unit_count
        for index, block in enumerate(blocks):
            entries[place] = jnp.where(block == own, index + nothing + 1, index)
            place = place + table_ref[row, 1 + block]
        entries[place] = nothing
        ends = lax.div(place + 1, 2)
        if first:

            @pl.when(ends == unit_count)
            def _(s=s):
                acc[s] = jnp.zeros(acc.shape[1:], acc.dtype)


        def mark(u, carry, s=s):
            units[u] = s
            return carry

        lax.fori_loop(unit_count, ends, mark, 0)
        unit_count = ends
    def query_rows(s):
        return jnp.concatenate(
            [
                q_ref[
                    pl.ds(pl.multiple_of(s * block_rows, block_rows), block_rows),
                    x * HEAD_DIM : (x + 1) * HEAD_DIM,
                ]
                for x in range(group)
            ],
            axis=0,
        )

    def pair_of(u):
        raw = [entries[2 * u], entries[2 * u + 1]]
        owns = [entry > nothing for entry in raw]
        return owns, [jnp.where(o, e - (nothing + 1), e) for o, e in zip(owns, raw)]

    def weigh(u):
        owns, index = pair_of(u)
        keys = jnp.concatenate([k_pool[i] for i in index], axis=0)
        reach = jnp.concatenate(
            [
                jnp.where(col_id <= row_id + jnp.where(own, 0, block_rows), 0.0, HIDDEN)
                for own in owns
            ],
            axis=1,
        )
        power = dot(query_rows(units[u]), keys, 1) * scale
        power = power + jnp.concatenate([reach] * group, axis=0)
        held_weights[...] = jnp.exp2(power).astype(held_weights.dtype)

    def add(u):
        _, index = pair_of(u)
        s = units[u]
        values = jnp.concatenate([v_pool[i] for i in index], axis=0)
        added = dot(held_weights[...], values, 0)
        old = acc[s]
        if first:
            fresh = (u == 0) | (units[jnp.maximum(u - 1, 0)] != s)
            old = jnp.where(fresh, 0.0, old)
        acc[s] = old + added

    @pl.when(unit_count > 0)
    def _():
        weigh(0)

        def both(u, carry):
            add(u)
            weigh(u + 1)
            return carry

        lax.fori_loop(0, unit_count - 1, both, 0)
        add(unit_count - 1)

    if not last:
        return

    top, k_all, v_all = refs

    def finish(s, i):
        under = acc[s, :, HEAD_DIM:]
        result = (acc[s, :, :HEAD_DIM] / under).astype(out_ref.dtype)
        for x in range(group):
            out_ref[
                i * block_rows : (i + 1) * block_rows, x * HEAD_DIM : (x + 1) * HEAD_DIM
            ] = result[x * block_rows : (x + 1) * block_rows]
        low = high = [under[j : j + 8] for j in range(0, rows, 8)]
        while len(low) > 1:
            low = [functools.reduce(jnp.minimum, low[j : j + 2]) for j in range(0, len(low), 2)]
            high = [functools.reduce(jnp.maximum, high[j : j + 2]) for j in range(0, len(high), 2)]
        return low[0], high[0]

    low, high = zip(*[finish(s, i) for i, s in enumerate(slot_ids)])
    low, high = functools.reduce(jnp.minimum, low), functools.reduce(jnp.maximum, high)
    safe = (low > 2.0**-HEADROOM) & (high < 2.0**HEADROOM)

    @pl.when(jnp.min(jnp.where(safe, 1.0, 0.0)) < 0.5)
    def _():
        pool_from(old_pieces, 0, k_all, v_all)
        pool_from(pieces, sum(p.shape[0] for p in old_pieces) // 2, k_all, v_all)
        blocks_all = ids(earlier) + blocks
        for i, s in enumerate(slot_ids):
            row = ring_at * slots + s
            own = table_ref[row, 0]
            place = jnp.int32(0)
            for index, block in enumerate(blocks_all):
                entries[place] = jnp.where(block == own, index + len(blocks_all), index)
                place = place + table_ref[row, 1 + block]
            acc[s] = jnp.zeros(acc.shape[1:], acc.dtype)
            top[...] = jnp.full(top.shape, MASKED, top.dtype)

            def one_block(e, carry, s=s):
                is_own = entries[e] >= len(blocks_all)
                index = jnp.where(is_own, entries[e] - len(blocks_all), entries[e])
                reach = jnp.where(
                    col_id <= row_id + jnp.where(is_own, 0, block_rows), 0.0, HIDDEN
                )
                scores = dot(query_rows(s), k_all[index], 1)
                weights, shrinks = [], []
                for x in range(group):
                    span = slice(x * block_rows, (x + 1) * block_rows)
                    power = scores[span] * scale + reach
                    new = jnp.maximum(top[span], jnp.max(power, axis=1, keepdims=True))
                    shrink = jnp.exp2(top[span] - new)
                    top[span] = new
                    weights.append(jnp.exp2(power - new).astype(jnp.bfloat16))
                    shrinks.append(jnp.concatenate([shrink, shrink], axis=1))
                added = dot(jnp.concatenate(weights, axis=0), v_all[index], 0)
                acc[s] = acc[s] * jnp.concatenate(shrinks, axis=0) + added
                return carry

            lax.fori_loop(0, place, one_block, 0)
            finish(s, i)


def cut(cores, *refs):
    ins, out_ref = refs[:-1], refs[-1]
    count = ins[0].shape[0]
    width = out_ref.shape[2]
    core = lax.rem(lax.axis_index("ka"), cores)
    for c in range(cores):

        @pl.when(core == c)
        def _():
            for i, ref in enumerate(ins):
                out_ref[i * count : (i + 1) * count] = ref[
                    :, 0, :, c * width : (c + 1) * width
                ]


def fetch(cores, queries_ref, out_ref, sems):
    rows, width = out_ref.shape
    at = lax.axis_index("ka")
    copies = copy_rows(
        queries_ref.at[
            pl.ds(pl.multiple_of(at // cores * rows, HEAD_DIM), rows),
            pl.ds(pl.multiple_of(lax.rem(at, cores) * width, HEAD_DIM), width),
        ],
        out_ref,
        sems,
    )
    for copy in copies:
        copy.wait()


def join(cores, own_ref, other_ref, out_ref, sems):
    width = own_ref.shape[1]
    core = lax.rem(lax.axis_index("ka"), cores)
    copies = []
    for i, ref in enumerate((own_ref, other_ref)):
        at = pl.multiple_of(lax.rem(core + (cores - i), cores) * width, HEAD_DIM)
        copies += copy_rows(ref, out_ref.at[:, pl.ds(at, width)], sems.at[i])
    for copy in copies:
        copy.wait()


def on_device(queries, keys, values, q_order, block_mask):
    pb, ka = lax.axis_size("pb"), lax.axis_size("ka")
    class_local, _, block_rows, kv_width = keys.shape
    cores = 2 if ka % 2 == 0 and kv_width == 2 * HEAD_DIM else 1
    rings = ka // cores
    head_width = kv_width // cores
    width = queries.shape[1] // cores
    rows = width // head_width * block_rows
    own_slots = queries.shape[0] // block_rows // ka
    slots = own_slots * cores

    vmem = pl.BlockSpec(memory_space=pltpu.VMEM)
    smem = pl.BlockSpec(memory_space=pltpu.SMEM)

    anywhere = pl.BlockSpec(memory_space=pl.ANY)
    stages = min(STAGES, pb)
    sources = pb // stages

    own_queries = pl.pallas_call(
        functools.partial(fetch, cores),
        out_shape=jax.ShapeDtypeStruct((slots * block_rows, width), queries.dtype),
        in_specs=[anywhere],
        out_specs=vmem,
        scratch_shapes=[pltpu.SemaphoreType.DMA((PARTS,))],
        compiler_params=pltpu.CompilerParams(vmem_limit_bytes=50 * 2**20),
    )(queries)
    raw = [keys, values]
    for c in range(1, cores):
        raw += [turn(keys, ka, cores, 0, c), turn(values, ka, cores, 0, c)]
    start = pl.pallas_call(
        functools.partial(cut, cores),
        out_shape=jax.ShapeDtypeStruct(
            (2 * cores * class_local, block_rows, head_width), keys.dtype
        ),
        in_specs=[vmem] * len(raw),
        out_specs=vmem,
        compiler_params=pltpu.CompilerParams(vmem_limit_bytes=SMALL * 2**20),
    )(*raw)

    start, q_order = lax.optimization_barrier((start, q_order))
    table = jnp.concatenate([q_order[:, None], block_mask], axis=1)
    def blocks_of(where):
        return sum(len(hops) * len(offsets) * class_local for hops, _, offsets in where)

    def call(first, last, turned, pieces, places, earlier, own_queries, state, extra):
        held = blocks_of(places)
        everything = held + blocks_of(earlier)
        here = own_slots if last else slots
        outs = [jax.ShapeDtypeStruct((slots, rows, 2 * HEAD_DIM), jnp.float32)]
        scratch = [
            pltpu.VMEM((held + 1, block_rows, HEAD_DIM), jnp.bfloat16),
            pltpu.VMEM((held + 1, block_rows, 2 * HEAD_DIM), jnp.bfloat16),
            pltpu.VMEM((rows, 2 * block_rows), jnp.bfloat16),
            pltpu.SMEM((max(here * (held + 1) + 1, everything + 1),), jnp.int32),
            pltpu.SMEM((here * (held // 2 + 1),), jnp.int32),
        ]
        if last:
            outs.append(jax.ShapeDtypeStruct((own_slots * block_rows, width), queries.dtype))
            scratch += [
                pltpu.VMEM((rows, HEAD_DIM), jnp.float32),
                pltpu.VMEM((everything, block_rows, HEAD_DIM), jnp.bfloat16),
                pltpu.VMEM((everything, block_rows, 2 * HEAD_DIM), jnp.bfloat16),
            ]
        pooled = held + (everything if last else 0)
        room = LIMIT * 2**20 + pooled * block_rows * HEAD_DIM * 6
        state_at = 2 + len(places) + len(extra)
        return pl.pallas_call(
            functools.partial(
                attend_stage,
                (pb, ka, cores, class_local, places, earlier, slots, turned),
                first,
                last,
                len(extra),
            ),
            out_shape=outs,
            in_specs=[smem]
            + [vmem] * (1 + len(places))
            + [vmem] * (len(extra) + len(state)),
            out_specs=[vmem] * len(outs),
            input_output_aliases={state_at + i: i for i in range(len(state))},
            scratch_shapes=scratch,
            compiler_params=pltpu.CompilerParams(vmem_limit_bytes=room),
            cost_estimate=pl.CostEstimate(
                flops=2**31, bytes_accessed=2**22, transcendentals=2**20
            ),
        )(table, own_queries, *pieces, *extra, *state)

    def along(array, count):
        found = []
        for _ in range(count):
            array = along_ring(array, pb)
            found.append(array)
        return found

    def stacked(arrays):
        return arrays[0] if len(arrays) == 1 else jnp.concatenate(arrays, axis=0)

    def beside(array):
        found = []
        for _ in range(rings - 1):
            array = turn(array, ka, cores, 1, 0)
            found.append(array)
        return found

    every = list(range(cores))
    state, earlier, before = [], [], []

    def work(state, pieces, places):
        state = call(not earlier, False, 0, pieces, places, earlier, own_queries, state, [])
        earlier.extend(places)
        before.extend(pieces)
        return state

    if rings == cores == 2 and pb == STAGES:
        tie = lax.optimization_barrier
        half = start.shape[0] // 2
        on = along_ring(start, pb)
        state = work(state, [start], [([0], 0, every)])
        again, state = tie((start, state))
        back, others = along_ring(again, pb, -1), beside(again)[0]
        on, state = tie((on, state))
        on_others = beside(on)[0]
        state = work(state, [on, others], [([1], 0, every), ([0], 1, every)])
        on, state = tie((on, state))
        two = along_ring(on, pb)
        back, state = tie((back, state))
        back_others = beside(back)[0]
        on_others, back, state = tie((on_others, back, state))
        two_high = along_ring(on_others[half:], pb)
        state = work(state, [back, on_others], [([pb - 1], 0, every), ([1], 1, every)])
        two, state = tie((two, state))
        two_low = turn(two[:half], ka, cores, 1, 0)
        state = work(state, [two], [([2], 0, every)])
        state = work(state, [back_others], [([pb - 1], 1, every)])
        pieces, places = [two_low, two_high], [([2], 1, [0]), ([2], 1, [1])]
    else:
        arrived = [start] + along(start, sources - 1)
        others, places = [], []
        for stage in range(stages):
            hops = range(stage * sources, (stage + 1) * sources)
            if stage:
                arrived, others, state = lax.optimization_barrier((arrived, others, state))
            near = stacked(arrived)
            pieces, places = [near] + others, [(hops, 0, every)] + places
            if stage < stages - 1:
                arrived = along(arrived[-1], sources)
            others = beside(near)
            state = work(state, pieces, places)
            places = [(hops, y, every) for y in range(1, rings)]
        pieces = others
    halves = []
    for c in reversed(range(cores)):
        *state, half = call(False, True, c, pieces, places, earlier, own_queries, state, before)
        halves.append(half)
    if cores == 1:
        return halves[0]
    return pl.pallas_call(
        functools.partial(join, cores),
        out_shape=jax.ShapeDtypeStruct((own_slots * block_rows, cores * width), queries.dtype),
        in_specs=[vmem] * 2,
        out_specs=anywhere,
        scratch_shapes=[pltpu.SemaphoreType.DMA((cores, PARTS))],
        compiler_params=pltpu.CompilerParams(vmem_limit_bytes=SMALL * 2**20),
    )(halves[1], turn(halves[0], ka, cores, 0, 1))


def solution(mesh):
    in_specs = (
        P("pb", "ha"),
        P("pb", "ka", None, "ha"),
        P("pb", "ka", None, "ha"),
        P("pb"),
        P("pb", None),
    )
    out_specs = P(("pb", "ka"), "ha")
    return jax.shard_map(
        on_device, mesh=mesh, in_specs=in_specs, out_specs=out_specs, check_vma=False
    )
```

```python
import functools
import math

import jax
import jax.numpy as jnp
from jax import lax
from jax.experimental import pallas as pl
from jax.experimental.pallas import tpu as pltpu
from jax.sharding import PartitionSpec as P

HEAD_DIM = 128
MASKED = -1e30
HIDDEN = -1e38
HEADROOM = 64.0
PARTS = 8
LIMIT = 10
SMALL = 4
STAGES = 4


def folded(size):
    return list(range(0, size, 2)) + list(range(1, size, 2))[::-1]


def along_ring(array, size, step=1):
    ring = folded(size)
    return lax.ppermute(array, "pb", [(ring[i], ring[(i + step) % size]) for i in range(size)])


def ring_source(at, size, hops):
    place = jnp.where(at % 2 == 0, at // 2, size - 1 - at // 2)
    place = lax.rem(place + (size - hops), size)
    return jnp.where(place < (size + 1) // 2, 2 * place, 2 * (size - 1 - place) + 1)


def turn(array, size, cores, ring_step, core_step):
    rings = size // cores
    pairs = []
    for ring in range(rings):
        for core in range(cores):
            to = ((ring + ring_step) % rings) * cores + (core + core_step) % cores
            pairs.append((ring * cores + core, to))
    return lax.ppermute(array, "ka", pairs)


def dot(a, b, b_dim):
    return lax.dot_general(a, b, (((1,), (b_dim,)), ((), ())), preferred_element_type=jnp.float32)


def copy_rows(source, target, sems):
    step = source.shape[0] // PARTS
    copies = [
        pltpu.make_async_copy(
            source.at[pl.ds(i * step, step)], target.at[pl.ds(i * step, step)], sems.at[i]
        )
        for i in range(PARTS)
    ]
    for copy in copies:
        copy.start()
    return copies


def attend_stage(plan, first, last, ahead, table_ref, q_ref, *refs):
    pb, ka, cores, class_local, places, earlier, slots, turned = plan
    count = len(places)
    pieces, refs = refs[:count], refs[count:]
    old_pieces, refs = refs[:ahead], refs[ahead:]
    if not first:
        refs = refs[1:]
    acc, refs = refs[0], refs[1:]
    if last:
        out_ref, refs = refs[0], refs[1:]
    k_pool, v_pool, held_weights, entries, units, refs = *refs[:5], refs[5:]
    rows = acc.shape[1]
    block_rows = q_ref.shape[0] // slots
    group = rows // block_rows
    rings = ka // cores
    own_slots = slots // cores
    p_at, k_at = lax.axis_index("pb"), lax.axis_index("ka")
    ring_at, core_at = k_at // cores, lax.rem(k_at, cores)
    scale = math.log2(math.e) / math.sqrt(HEAD_DIM)

    def ids(where):
        found = []
        for hops, y, offsets in where:
            ring = lax.rem(ring_at + (rings - y), rings)
            for z in hops:
                source = ring_source(p_at, pb, z)
                for c in offsets:
                    core = lax.rem(core_at + (cores - c), cores)
                    for t in range(class_local):
                        found.append((source * class_local + t) * ka + ring * cores + core)
        return found

    def pool_from(refs_in, at, k_out, v_out):
        for piece in refs_in:
            for i in range(0, piece.shape[0], 2 * class_local):
                span = slice(at, at + class_local)
                k_out[span] = piece[i : i + class_local]
                value = piece[i + class_local : i + 2 * class_local]
                v_out[span, :, :HEAD_DIM] = value
                v_out[span, :, HEAD_DIM:] = jnp.ones(value.shape, v_out.dtype)
                at += class_local

    nothing = sum(piece.shape[0] for piece in pieces) // 2

    if last:
        mine = lax.rem(core_at + turned, cores) * own_slots
        slot_ids = [mine + i for i in range(own_slots)]
    else:
        slot_ids = list(range(slots))

    row_id = lax.broadcasted_iota(jnp.int32, (block_rows, block_rows), 0)
    col_id = lax.broadcasted_iota(jnp.int32, (block_rows, block_rows), 1)
    pool_from(pieces, 0, k_pool, v_pool)
    k_pool[nothing] = jnp.zeros(k_pool.shape[1:], k_pool.dtype)
    v_pool[nothing] = jnp.zeros(v_pool.shape[1:], v_pool.dtype)

    blocks = ids(places)
    unit_count = jnp.int32(0)
    for s in slot_ids:
        row = ring_at * slots + s
        own = table_ref[row, 0]
        place = 2 * unit_count
        for index, block in enumerate(blocks):
            entries[place] = jnp.where(block == own, index + nothing + 1, index)
            place = place + table_ref[row, 1 + block]
        entries[place] = nothing
        ends = lax.div(place + 1, 2)
        if first:

            @pl.when(ends == unit_count)
            def _(s=s):
                acc[s] = jnp.zeros(acc.shape[1:], acc.dtype)


        def mark(u, carry, s=s):
            units[u] = s
            return carry

        lax.fori_loop(unit_count, ends, mark, 0)
        unit_count = ends
    def query_rows(s):
        return jnp.concatenate(
            [
                q_ref[
                    pl.ds(pl.multiple_of(s * block_rows, block_rows), block_rows),
                    x * HEAD_DIM : (x + 1) * HEAD_DIM,
                ]
                for x in range(group)
            ],
            axis=0,
        )

    def pair_of(u):
        raw = [entries[2 * u], entries[2 * u + 1]]
        owns = [entry > nothing for entry in raw]
        return owns, [jnp.where(o, e - (nothing + 1), e) for o, e in zip(owns, raw)]

    def weigh(u):
        owns, index = pair_of(u)
        keys = jnp.concatenate([k_pool[i] for i in index], axis=0)
        reach = jnp.concatenate(
            [
                jnp.where(col_id <= row_id + jnp.where(own, 0, block_rows), 0.0, HIDDEN)
                for own in owns
            ],
            axis=1,
        )
        power = dot(query_rows(units[u]), keys, 1) * scale
        power = power + jnp.concatenate([reach] * group, axis=0)
        held_weights[...] = jnp.exp2(power).astype(held_weights.dtype)

    def add(u):
        _, index = pair_of(u)
        s = units[u]
        values = jnp.concatenate([v_pool[i] for i in index], axis=0)
        added = dot(held_weights[...], values, 0)
        old = acc[s]
        if first:
            fresh = (u == 0) | (units[jnp.maximum(u - 1, 0)] != s)
            old = jnp.where(fresh, 0.0, old)
        acc[s] = old + added

    @pl.when(unit_count > 0)
    def _():
        weigh(0)

        def both(u, carry):
            add(u)
            weigh(u + 1)
            return carry

        lax.fori_loop(0, unit_count - 1, both, 0)
        add(unit_count - 1)

    if not last:
        return

    top, k_all, v_all = refs

    def finish(s, i):
        under = acc[s, :, HEAD_DIM:]
        result = (acc[s, :, :HEAD_DIM] / under).astype(out_ref.dtype)
        for x in range(group):
            out_ref[
                i * block_rows : (i + 1) * block_rows, x * HEAD_DIM : (x + 1) * HEAD_DIM
            ] = result[x * block_rows : (x + 1) * block_rows]
        low = high = [under[j : j + 8] for j in range(0, rows, 8)]
        while len(low) > 1:
            low = [functools.reduce(jnp.minimum, low[j : j + 2]) for j in range(0, len(low), 2)]
            high = [functools.reduce(jnp.maximum, high[j : j + 2]) for j in range(0, len(high), 2)]
        return low[0], high[0]

    low, high = zip(*[finish(s, i) for i, s in enumerate(slot_ids)])
    low, high = functools.reduce(jnp.minimum, low), functools.reduce(jnp.maximum, high)
    safe = (low > 2.0**-HEADROOM) & (high < 2.0**HEADROOM)

    @pl.when(jnp.min(jnp.where(safe, 1.0, 0.0)) < 0.5)
    def _():
        pool_from(old_pieces, 0, k_all, v_all)
        pool_from(pieces, sum(p.shape[0] for p in old_pieces) // 2, k_all, v_all)
        blocks_all = ids(earlier) + blocks
        for i, s in enumerate(slot_ids):
            row = ring_at * slots + s
            own = table_ref[row, 0]
            place = jnp.int32(0)
            for index, block in enumerate(blocks_all):
                entries[place] = jnp.where(block == own, index + len(blocks_all), index)
                place = place + table_ref[row, 1 + block]
            acc[s] = jnp.zeros(acc.shape[1:], acc.dtype)
            top[...] = jnp.full(top.shape, MASKED, top.dtype)

            def one_block(e, carry, s=s):
                is_own = entries[e] >= len(blocks_all)
                index = jnp.where(is_own, entries[e] - len(blocks_all), entries[e])
                reach = jnp.where(
                    col_id <= row_id + jnp.where(is_own, 0, block_rows), 0.0, HIDDEN
                )
                scores = dot(query_rows(s), k_all[index], 1)
                weights, shrinks = [], []
                for x in range(group):
                    span = slice(x * block_rows, (x + 1) * block_rows)
                    power = scores[span] * scale + reach
                    new = jnp.maximum(top[span], jnp.max(power, axis=1, keepdims=True))
                    shrink = jnp.exp2(top[span] - new)
                    top[span] = new
                    weights.append(jnp.exp2(power - new).astype(jnp.bfloat16))
                    shrinks.append(jnp.concatenate([shrink, shrink], axis=1))
                added = dot(jnp.concatenate(weights, axis=0), v_all[index], 0)
                acc[s] = acc[s] * jnp.concatenate(shrinks, axis=0) + added
                return carry

            lax.fori_loop(0, place, one_block, 0)
            finish(s, i)


def cut(cores, *refs):
    ins, out_ref = refs[:-1], refs[-1]
    count = ins[0].shape[0]
    width = out_ref.shape[2]
    core = lax.rem(lax.axis_index("ka"), cores)
    for c in range(cores):

        @pl.when(core == c)
        def _():
            for i, ref in enumerate(ins):
                out_ref[i * count : (i + 1) * count] = ref[
                    :, 0, :, c * width : (c + 1) * width
                ]


def fetch(cores, queries_ref, out_ref, sems):
    rows, width = out_ref.shape
    at = lax.axis_index("ka")
    copies = copy_rows(
        queries_ref.at[
            pl.ds(pl.multiple_of(at // cores * rows, HEAD_DIM), rows),
            pl.ds(pl.multiple_of(lax.rem(at, cores) * width, HEAD_DIM), width),
        ],
        out_ref,
        sems,
    )
    for copy in copies:
        copy.wait()


def join(cores, own_ref, other_ref, out_ref, sems):
    width = own_ref.shape[1]
    core = lax.rem(lax.axis_index("ka"), cores)
    copies = []
    for i, ref in enumerate((own_ref, other_ref)):
        at = pl.multiple_of(lax.rem(core + (cores - i), cores) * width, HEAD_DIM)
        copies += copy_rows(ref, out_ref.at[:, pl.ds(at, width)], sems.at[i])
    for copy in copies:
        copy.wait()


def on_device(queries, keys, values, q_order, block_mask):
    pb, ka = lax.axis_size("pb"), lax.axis_size("ka")
    class_local, _, block_rows, kv_width = keys.shape
    cores = 2 if ka % 2 == 0 and kv_width == 2 * HEAD_DIM else 1
    rings = ka // cores
    head_width = kv_width // cores
    width = queries.shape[1] // cores
    rows = width // head_width * block_rows
    own_slots = queries.shape[0] // block_rows // ka
    slots = own_slots * cores

    vmem = pl.BlockSpec(memory_space=pltpu.VMEM)
    smem = pl.BlockSpec(memory_space=pltpu.SMEM)

    anywhere = pl.BlockSpec(memory_space=pl.ANY)
    stages = min(STAGES, pb)
    sources = pb // stages

    own_queries = pl.pallas_call(
        functools.partial(fetch, cores),
        out_shape=jax.ShapeDtypeStruct((slots * block_rows, width), queries.dtype),
        in_specs=[anywhere],
        out_specs=vmem,
        scratch_shapes=[pltpu.SemaphoreType.DMA((PARTS,))],
        compiler_params=pltpu.CompilerParams(vmem_limit_bytes=50 * 2**20),
    )(queries)
    raw = [keys, values]
    for c in range(1, cores):
        raw += [turn(keys, ka, cores, 0, c), turn(values, ka, cores, 0, c)]
    start = pl.pallas_call(
        functools.partial(cut, cores),
        out_shape=jax.ShapeDtypeStruct(
            (2 * cores * class_local, block_rows, head_width), keys.dtype
        ),
        in_specs=[vmem] * len(raw),
        out_specs=vmem,
        compiler_params=pltpu.CompilerParams(vmem_limit_bytes=SMALL * 2**20),
    )(*raw)

    start, q_order = lax.optimization_barrier((start, q_order))
    table = jnp.concatenate([q_order[:, None], block_mask], axis=1)
    def blocks_of(where):
        return sum(len(hops) * len(offsets) * class_local for hops, _, offsets in where)

    def call(first, last, turned, pieces, places, earlier, own_queries, state, extra):
        held = blocks_of(places)
        everything = held + blocks_of(earlier)
        here = own_slots if last else slots
        outs = [jax.ShapeDtypeStruct((slots, rows, 2 * HEAD_DIM), jnp.float32)]
        scratch = [
            pltpu.VMEM((held + 1, block_rows, HEAD_DIM), jnp.bfloat16),
            pltpu.VMEM((held + 1, block_rows, 2 * HEAD_DIM), jnp.bfloat16),
            pltpu.VMEM((rows, 2 * block_rows), jnp.bfloat16),
            pltpu.SMEM((max(here * (held + 1) + 1, everything + 1),), jnp.int32),
            pltpu.SMEM((here * (held // 2 + 1),), jnp.int32),
        ]
        if last:
            outs.append(jax.ShapeDtypeStruct((own_slots * block_rows, width), queries.dtype))
            scratch += [
                pltpu.VMEM((rows, HEAD_DIM), jnp.float32),
                pltpu.VMEM((everything, block_rows, HEAD_DIM), jnp.bfloat16),
                pltpu.VMEM((everything, block_rows, 2 * HEAD_DIM), jnp.bfloat16),
            ]
        pooled = held + (everything if last else 0)
        room = LIMIT * 2**20 + pooled * block_rows * HEAD_DIM * 6
        state_at = 2 + len(places) + len(extra)
        return pl.pallas_call(
            functools.partial(
                attend_stage,
                (pb, ka, cores, class_local, places, earlier, slots, turned),
                first,
                last,
                len(extra),
            ),
            out_shape=outs,
            in_specs=[smem]
            + [vmem] * (1 + len(places))
            + [vmem] * (len(extra) + len(state)),
            out_specs=[vmem] * len(outs),
            input_output_aliases={state_at + i: i for i in range(len(state))},
            scratch_shapes=scratch,
            compiler_params=pltpu.CompilerParams(vmem_limit_bytes=room),
            cost_estimate=pl.CostEstimate(
                flops=2**31, bytes_accessed=2**22, transcendentals=2**20
            ),
        )(table, own_queries, *pieces, *extra, *state)

    def along(array, count):
        found = []
        for _ in range(count):
            array = along_ring(array, pb)
            found.append(array)
        return found

    def stacked(arrays):
        return arrays[0] if len(arrays) == 1 else jnp.concatenate(arrays, axis=0)

    def beside(array):
        found = []
        for _ in range(rings - 1):
            array = turn(array, ka, cores, 1, 0)
            found.append(array)
        return found

    every = list(range(cores))
    state, earlier, before = [], [], []

    def work(state, pieces, places):
        state = call(not earlier, False, 0, pieces, places, earlier, own_queries, state, [])
        earlier.extend(places)
        before.extend(pieces)
        return state

    if rings == cores == 2 and pb == STAGES:
        tie = lax.optimization_barrier
        half = start.shape[0] // 2
        on = along_ring(start, pb)
        later, table = tie((start, table))
        others = beside(later)[0]
        state = work(state, [start], [([0], 0, every)])
        again, state = tie((start, state))
        back = along_ring(again, pb, -1)
        on, state = tie((on, state))
        on_others, two = beside(on)[0], along_ring(on, pb)
        state = work(state, [on, others], [([1], 0, every), ([0], 1, every)])
        back, state = tie((back, state))
        back_others = beside(back)[0]
        on_others, back, state = tie((on_others, back, state))
        two_high = along_ring(on_others[half:], pb)
        state = work(state, [back, on_others], [([pb - 1], 0, every), ([1], 1, every)])
        two, state = tie((two, state))
        two_low = turn(two[:half], ka, cores, 1, 0)
        state = work(state, [two], [([2], 0, every)])
        state = work(state, [back_others], [([pb - 1], 1, every)])
        pieces, places = [two_low, two_high], [([2], 1, [0]), ([2], 1, [1])]
    else:
        arrived = [start] + along(start, sources - 1)
        others, places = [], []
        for stage in range(stages):
            hops = range(stage * sources, (stage + 1) * sources)
            if stage:
                arrived, others, state = lax.optimization_barrier((arrived, others, state))
            near = stacked(arrived)
            pieces, places = [near] + others, [(hops, 0, every)] + places
            if stage < stages - 1:
                arrived = along(arrived[-1], sources)
            others = beside(near)
            state = work(state, pieces, places)
            places = [(hops, y, every) for y in range(1, rings)]
        pieces = others
    halves = []
    for c in reversed(range(cores)):
        *state, half = call(False, True, c, pieces, places, earlier, own_queries, state, before)
        halves.append(half)
    if cores == 1:
        return halves[0]
    return pl.pallas_call(
        functools.partial(join, cores),
        out_shape=jax.ShapeDtypeStruct((own_slots * block_rows, cores * width), queries.dtype),
        in_specs=[vmem] * 2,
        out_specs=anywhere,
        scratch_shapes=[pltpu.SemaphoreType.DMA((cores, PARTS))],
        compiler_params=pltpu.CompilerParams(vmem_limit_bytes=SMALL * 2**20),
    )(halves[1], turn(halves[0], ka, cores, 0, 1))


def solution(mesh):
    in_specs = (
        P("pb", "ha"),
        P("pb", "ka", None, "ha"),
        P("pb", "ka", None, "ha"),
        P("pb"),
        P("pb", None),
    )
    out_specs = P(("pb", "ka"), "ha")
    return jax.shard_map(
        on_device, mesh=mesh, in_specs=in_specs, out_specs=out_specs, check_vma=False
    )
```

```python
import functools
import math

import jax
import jax.numpy as jnp
from jax import lax
from jax.experimental import pallas as pl
from jax.experimental.pallas import tpu as pltpu
from jax.sharding import PartitionSpec as P

HEAD_DIM = 128
MASKED = -1e30
HIDDEN = -1e38
HEADROOM = 64.0
PARTS = 8
LIMIT = 10
SMALL = 4
STAGES = 4


def folded(size):
    return list(range(0, size, 2)) + list(range(1, size, 2))[::-1]


def along_ring(array, size, step=1):
    ring = folded(size)
    return lax.ppermute(array, "pb", [(ring[i], ring[(i + step) % size]) for i in range(size)])


def ring_source(at, size, hops):
    place = jnp.where(at % 2 == 0, at // 2, size - 1 - at // 2)
    place = lax.rem(place + (size - hops), size)
    return jnp.where(place < (size + 1) // 2, 2 * place, 2 * (size - 1 - place) + 1)


def turn(array, size, cores, ring_step, core_step):
    rings = size // cores
    pairs = []
    for ring in range(rings):
        for core in range(cores):
            to = ((ring + ring_step) % rings) * cores + (core + core_step) % cores
            pairs.append((ring * cores + core, to))
    return lax.ppermute(array, "ka", pairs)


def dot(a, b, b_dim):
    return lax.dot_general(a, b, (((1,), (b_dim,)), ((), ())), preferred_element_type=jnp.float32)


def copy_rows(source, target, sems):
    step = source.shape[0] // PARTS
    copies = [
        pltpu.make_async_copy(
            source.at[pl.ds(i * step, step)], target.at[pl.ds(i * step, step)], sems.at[i]
        )
        for i in range(PARTS)
    ]
    for copy in copies:
        copy.start()
    return copies


def attend_stage(plan, first, last, ahead, table_ref, q_ref, *refs):
    pb, ka, cores, class_local, places, earlier, slots, turned = plan
    count = len(places)
    pieces, refs = refs[:count], refs[count:]
    old_pieces, refs = refs[:ahead], refs[ahead:]
    if not first:
        refs = refs[1:]
    acc, refs = refs[0], refs[1:]
    if last:
        out_ref, refs = refs[0], refs[1:]
    k_pool, v_pool, held_weights, entries, units, refs = *refs[:5], refs[5:]
    rows = acc.shape[1]
    block_rows = q_ref.shape[0] // slots
    group = rows // block_rows
    rings = ka // cores
    own_slots = slots // cores
    p_at, k_at = lax.axis_index("pb"), lax.axis_index("ka")
    ring_at, core_at = k_at // cores, lax.rem(k_at, cores)
    scale = math.log2(math.e) / math.sqrt(HEAD_DIM)

    def ids(where):
        found = []
        for hops, y, offsets in where:
            ring = lax.rem(ring_at + (rings - y), rings)
            for z in hops:
                source = ring_source(p_at, pb, z)
                for c in offsets:
                    core = lax.rem(core_at + (cores - c), cores)
                    for t in range(class_local):
                        found.append((source * class_local + t) * ka + ring * cores + core)
        return found

    def pool_from(refs_in, at, k_out, v_out):
        for piece in refs_in:
            for i in range(0, piece.shape[0], 2 * class_local):
                span = slice(at, at + class_local)
                k_out[span] = piece[i : i + class_local]
                value = piece[i + class_local : i + 2 * class_local]
                v_out[span, :, :HEAD_DIM] = value
                v_out[span, :, HEAD_DIM:] = jnp.ones(value.shape, v_out.dtype)
                at += class_local

    nothing = sum(piece.shape[0] for piece in pieces) // 2

    if last:
        mine = lax.rem(core_at + turned, cores) * own_slots
        slot_ids = [mine + i for i in range(own_slots)]
    else:
        slot_ids = list(range(slots))

    row_id = lax.broadcasted_iota(jnp.int32, (block_rows, block_rows), 0)
    col_id = lax.broadcasted_iota(jnp.int32, (block_rows, block_rows), 1)
    pool_from(pieces, 0, k_pool, v_pool)
    k_pool[nothing] = jnp.zeros(k_pool.shape[1:], k_pool.dtype)
    v_pool[nothing] = jnp.zeros(v_pool.shape[1:], v_pool.dtype)

    blocks = ids(places)
    unit_count = jnp.int32(0)
    for s in slot_ids:
        row = ring_at * slots + s
        own = table_ref[row, 0]
        place = 2 * unit_count
        for index, block in enumerate(blocks):
            entries[place] = jnp.where(block == own, index + nothing + 1, index)
            place = place + table_ref[row, 1 + block]
        entries[place] = nothing
        ends = lax.div(place + 1, 2)
        if first:

            @pl.when(ends == unit_count)
            def _(s=s):
                acc[s] = jnp.zeros(acc.shape[1:], acc.dtype)


        def mark(u, carry, s=s):
            units[u] = s
            return carry

        lax.fori_loop(unit_count, ends, mark, 0)
        unit_count = ends
    def query_rows(s):
        return jnp.concatenate(
            [
                q_ref[
                    pl.ds(pl.multiple_of(s * block_rows, block_rows), block_rows),
                    x * HEAD_DIM : (x + 1) * HEAD_DIM,
                ]
                for x in range(group)
            ],
            axis=0,
        )

    def pair_of(u):
        raw = [entries[2 * u], entries[2 * u + 1]]
        owns = [entry > nothing for entry in raw]
        return owns, [jnp.where(o, e - (nothing + 1), e) for o, e in zip(owns, raw)]

    def weigh(u):
        owns, index = pair_of(u)
        keys = jnp.concatenate([k_pool[i] for i in index], axis=0)
        reach = jnp.concatenate(
            [
                jnp.where(col_id <= row_id + jnp.where(own, 0, block_rows), 0.0, HIDDEN)
                for own in owns
            ],
            axis=1,
        )
        power = dot(query_rows(units[u]), keys, 1) * scale
        power = power + jnp.concatenate([reach] * group, axis=0)
        held_weights[...] = jnp.exp2(power).astype(held_weights.dtype)

    def add(u):
        _, index = pair_of(u)
        s = units[u]
        values = jnp.concatenate([v_pool[i] for i in index], axis=0)
        added = dot(held_weights[...], values, 0)
        old = acc[s]
        if first:
            fresh = (u == 0) | (units[jnp.maximum(u - 1, 0)] != s)
            old = jnp.where(fresh, 0.0, old)
        acc[s] = old + added

    @pl.when(unit_count > 0)
    def _():
        weigh(0)

        def both(u, carry):
            add(u)
            weigh(u + 1)
            return carry

        lax.fori_loop(0, unit_count - 1, both, 0)
        add(unit_count - 1)

    if not last:
        return

    top, k_all, v_all = refs

    def finish(s, i):
        under = acc[s, :, HEAD_DIM:]
        result = (acc[s, :, :HEAD_DIM] / under).astype(out_ref.dtype)
        for x in range(group):
            out_ref[
                i * block_rows : (i + 1) * block_rows, x * HEAD_DIM : (x + 1) * HEAD_DIM
            ] = result[x * block_rows : (x + 1) * block_rows]
        low = high = [under[j : j + 8] for j in range(0, rows, 8)]
        while len(low) > 1:
            low = [functools.reduce(jnp.minimum, low[j : j + 2]) for j in range(0, len(low), 2)]
            high = [functools.reduce(jnp.maximum, high[j : j + 2]) for j in range(0, len(high), 2)]
        return low[0], high[0]

    low, high = zip(*[finish(s, i) for i, s in enumerate(slot_ids)])
    low, high = functools.reduce(jnp.minimum, low), functools.reduce(jnp.maximum, high)
    safe = (low > 2.0**-HEADROOM) & (high < 2.0**HEADROOM)

    @pl.when(jnp.min(jnp.where(safe, 1.0, 0.0)) < 0.5)
    def _():
        pool_from(old_pieces, 0, k_all, v_all)
        pool_from(pieces, sum(p.shape[0] for p in old_pieces) // 2, k_all, v_all)
        blocks_all = ids(earlier) + blocks
        for i, s in enumerate(slot_ids):
            row = ring_at * slots + s
            own = table_ref[row, 0]
            place = jnp.int32(0)
            for index, block in enumerate(blocks_all):
                entries[place] = jnp.where(block == own, index + len(blocks_all), index)
                place = place + table_ref[row, 1 + block]
            acc[s] = jnp.zeros(acc.shape[1:], acc.dtype)
            top[...] = jnp.full(top.shape, MASKED, top.dtype)

            def one_block(e, carry, s=s):
                is_own = entries[e] >= len(blocks_all)
                index = jnp.where(is_own, entries[e] - len(blocks_all), entries[e])
                reach = jnp.where(
                    col_id <= row_id + jnp.where(is_own, 0, block_rows), 0.0, HIDDEN
                )
                scores = dot(query_rows(s), k_all[index], 1)
                weights, shrinks = [], []
                for x in range(group):
                    span = slice(x * block_rows, (x + 1) * block_rows)
                    power = scores[span] * scale + reach
                    new = jnp.maximum(top[span], jnp.max(power, axis=1, keepdims=True))
                    shrink = jnp.exp2(top[span] - new)
                    top[span] = new
                    weights.append(jnp.exp2(power - new).astype(jnp.bfloat16))
                    shrinks.append(jnp.concatenate([shrink, shrink], axis=1))
                added = dot(jnp.concatenate(weights, axis=0), v_all[index], 0)
                acc[s] = acc[s] * jnp.concatenate(shrinks, axis=0) + added
                return carry

            lax.fori_loop(0, place, one_block, 0)
            finish(s, i)


def cut(cores, *refs):
    ins, out_ref = refs[:-1], refs[-1]
    count = ins[0].shape[0]
    width = out_ref.shape[2]
    core = lax.rem(lax.axis_index("ka"), cores)
    for c in range(cores):

        @pl.when(core == c)
        def _():
            for i, ref in enumerate(ins):
                out_ref[i * count : (i + 1) * count] = ref[
                    :, 0, :, c * width : (c + 1) * width
                ]


def fetch(cores, queries_ref, out_ref, sems):
    rows, width = out_ref.shape
    at = lax.axis_index("ka")
    copies = copy_rows(
        queries_ref.at[
            pl.ds(pl.multiple_of(at // cores * rows, HEAD_DIM), rows),
            pl.ds(pl.multiple_of(lax.rem(at, cores) * width, HEAD_DIM), width),
        ],
        out_ref,
        sems,
    )
    for copy in copies:
        copy.wait()


def join(cores, own_ref, other_ref, out_ref, sems):
    width = own_ref.shape[1]
    core = lax.rem(lax.axis_index("ka"), cores)
    copies = []
    for i, ref in enumerate((own_ref, other_ref)):
        at = pl.multiple_of(lax.rem(core + (cores - i), cores) * width, HEAD_DIM)
        copies += copy_rows(ref, out_ref.at[:, pl.ds(at, width)], sems.at[i])
    for copy in copies:
        copy.wait()


def on_device(queries, keys, values, q_order, block_mask):
    pb, ka = lax.axis_size("pb"), lax.axis_size("ka")
    class_local, _, block_rows, kv_width = keys.shape
    cores = 2 if ka % 2 == 0 and kv_width == 2 * HEAD_DIM else 1
    rings = ka // cores
    head_width = kv_width // cores
    width = queries.shape[1] // cores
    rows = width // head_width * block_rows
    own_slots = queries.shape[0] // block_rows // ka
    slots = own_slots * cores

    vmem = pl.BlockSpec(memory_space=pltpu.VMEM)
    smem = pl.BlockSpec(memory_space=pltpu.SMEM)

    anywhere = pl.BlockSpec(memory_space=pl.ANY)
    stages = min(STAGES, pb)
    sources = pb // stages

    own_queries = pl.pallas_call(
        functools.partial(fetch, cores),
        out_shape=jax.ShapeDtypeStruct((slots * block_rows, width), queries.dtype),
        in_specs=[anywhere],
        out_specs=vmem,
        scratch_shapes=[pltpu.SemaphoreType.DMA((PARTS,))],
        compiler_params=pltpu.CompilerParams(vmem_limit_bytes=50 * 2**20),
    )(queries)
    raw = [keys, values]
    for c in range(1, cores):
        raw += [turn(keys, ka, cores, 0, c), turn(values, ka, cores, 0, c)]
    start = pl.pallas_call(
        functools.partial(cut, cores),
        out_shape=jax.ShapeDtypeStruct(
            (2 * cores * class_local, block_rows, head_width), keys.dtype
        ),
        in_specs=[vmem] * len(raw),
        out_specs=vmem,
        compiler_params=pltpu.CompilerParams(vmem_limit_bytes=SMALL * 2**20),
    )(*raw)

    start, q_order = lax.optimization_barrier((start, q_order))
    table = jnp.concatenate([q_order[:, None], block_mask], axis=1)
    def blocks_of(where):
        return sum(len(hops) * len(offsets) * class_local for hops, _, offsets in where)

    def call(first, last, turned, pieces, places, earlier, own_queries, state, extra):
        held = blocks_of(places)
        everything = held + blocks_of(earlier)
        here = own_slots if last else slots
        outs = [jax.ShapeDtypeStruct((slots, rows, 2 * HEAD_DIM), jnp.float32)]
        scratch = [
            pltpu.VMEM((held + 1, block_rows, HEAD_DIM), jnp.bfloat16),
            pltpu.VMEM((held + 1, block_rows, 2 * HEAD_DIM), jnp.bfloat16),
            pltpu.VMEM((rows, 2 * block_rows), jnp.bfloat16),
            pltpu.SMEM((max(here * (held + 1) + 1, everything + 1),), jnp.int32),
            pltpu.SMEM((here * (held // 2 + 1),), jnp.int32),
        ]
        if last:
            outs.append(jax.ShapeDtypeStruct((own_slots * block_rows, width), queries.dtype))
            scratch += [
                pltpu.VMEM((rows, HEAD_DIM), jnp.float32),
                pltpu.VMEM((everything, block_rows, HEAD_DIM), jnp.bfloat16),
                pltpu.VMEM((everything, block_rows, 2 * HEAD_DIM), jnp.bfloat16),
            ]
        pooled = held + (everything if last else 0)
        room = LIMIT * 2**20 + pooled * block_rows * HEAD_DIM * 6
        state_at = 2 + len(places) + len(extra)
        return pl.pallas_call(
            functools.partial(
                attend_stage,
                (pb, ka, cores, class_local, places, earlier, slots, turned),
                first,
                last,
                len(extra),
            ),
            out_shape=outs,
            in_specs=[smem]
            + [vmem] * (1 + len(places))
            + [vmem] * (len(extra) + len(state)),
            out_specs=[vmem] * len(outs),
            input_output_aliases={state_at + i: i for i in range(len(state))},
            scratch_shapes=scratch,
            compiler_params=pltpu.CompilerParams(vmem_limit_bytes=room),
            cost_estimate=pl.CostEstimate(
                flops=2**31, bytes_accessed=2**22, transcendentals=2**20
            ),
        )(table, own_queries, *pieces, *extra, *state)

    def along(array, count):
        found = []
        for _ in range(count):
            array = along_ring(array, pb)
            found.append(array)
        return found

    def stacked(arrays):
        return arrays[0] if len(arrays) == 1 else jnp.concatenate(arrays, axis=0)

    def beside(array):
        found = []
        for _ in range(rings - 1):
            array = turn(array, ka, cores, 1, 0)
            found.append(array)
        return found

    every = list(range(cores))
    state, earlier, before = [], [], []

    def work(state, pieces, places):
        state = call(not earlier, False, 0, pieces, places, earlier, own_queries, state, [])
        earlier.extend(places)
        before.extend(pieces)
        return state

    if rings == cores == 2 and pb == STAGES:
        tie = lax.optimization_barrier
        half = start.shape[0] // 2
        on = along_ring(start, pb)
        later, table = tie((start, table))
        others = beside(later)[0]
        state = work(state, [start], [([0], 0, every)])
        again, state = tie((start, state))
        back = along_ring(again, pb, -1)
        on, state = tie((on, state))
        on_others = beside(on)[0]
        state = work(state, [on], [([1], 0, every)])
        on, back, state = tie((on, back, state))
        back_others, two = beside(back)[0], along_ring(on, pb)
        state = work(state, [back, others], [([pb - 1], 0, every), ([0], 1, every)])
        on_others, state = tie((on_others, state))
        two_high = along_ring(on_others[half:], pb)
        state = work(state, [on_others], [([1], 1, every)])
        two, state = tie((two, state))
        two_low = turn(two[:half], ka, cores, 1, 0)
        state = work(state, [two], [([2], 0, every)])
        state = work(state, [back_others], [([pb - 1], 1, every)])
        pieces, places = [two_low, two_high], [([2], 1, [0]), ([2], 1, [1])]
    else:
        arrived = [start] + along(start, sources - 1)
        others, places = [], []
        for stage in range(stages):
            hops = range(stage * sources, (stage + 1) * sources)
            if stage:
                arrived, others, state = lax.optimization_barrier((arrived, others, state))
            near = stacked(arrived)
            pieces, places = [near] + others, [(hops, 0, every)] + places
            if stage < stages - 1:
                arrived = along(arrived[-1], sources)
            others = beside(near)
            state = work(state, pieces, places)
            places = [(hops, y, every) for y in range(1, rings)]
        pieces = others
    halves = []
    for c in reversed(range(cores)):
        *state, half = call(False, True, c, pieces, places, earlier, own_queries, state, before)
        halves.append(half)
    if cores == 1:
        return halves[0]
    return pl.pallas_call(
        functools.partial(join, cores),
        out_shape=jax.ShapeDtypeStruct((own_slots * block_rows, cores * width), queries.dtype),
        in_specs=[vmem] * 2,
        out_specs=anywhere,
        scratch_shapes=[pltpu.SemaphoreType.DMA((cores, PARTS))],
        compiler_params=pltpu.CompilerParams(vmem_limit_bytes=SMALL * 2**20),
    )(halves[1], turn(halves[0], ka, cores, 0, 1))


def solution(mesh):
    in_specs = (
        P("pb", "ha"),
        P("pb", "ka", None, "ha"),
        P("pb", "ka", None, "ha"),
        P("pb"),
        P("pb", None),
    )
    out_specs = P(("pb", "ka"), "ha")
    return jax.shard_map(
        on_device, mesh=mesh, in_specs=in_specs, out_specs=out_specs, check_vma=False
    )
```

```python
import functools
import math

import jax
import jax.numpy as jnp
from jax import lax
from jax.experimental import pallas as pl
from jax.experimental.pallas import tpu as pltpu
from jax.sharding import PartitionSpec as P

HEAD_DIM = 128
MASKED = -1e30
HIDDEN = -1e38
HEADROOM = 64.0
PARTS = 8
LIMIT = 10
SMALL = 4
STAGES = 4


def folded(size):
    return list(range(0, size, 2)) + list(range(1, size, 2))[::-1]


def along_ring(array, size, step=1):
    ring = folded(size)
    return lax.ppermute(array, "pb", [(ring[i], ring[(i + step) % size]) for i in range(size)])


def ring_source(at, size, hops):
    place = jnp.where(at % 2 == 0, at // 2, size - 1 - at // 2)
    place = lax.rem(place + (size - hops), size)
    return jnp.where(place < (size + 1) // 2, 2 * place, 2 * (size - 1 - place) + 1)


def turn(array, size, cores, ring_step, core_step):
    rings = size // cores
    pairs = []
    for ring in range(rings):
        for core in range(cores):
            to = ((ring + ring_step) % rings) * cores + (core + core_step) % cores
            pairs.append((ring * cores + core, to))
    return lax.ppermute(array, "ka", pairs)


def dot(a, b, b_dim):
    return lax.dot_general(a, b, (((1,), (b_dim,)), ((), ())), preferred_element_type=jnp.float32)


def copy_rows(source, target, sems):
    step = source.shape[0] // PARTS
    copies = [
        pltpu.make_async_copy(
            source.at[pl.ds(i * step, step)], target.at[pl.ds(i * step, step)], sems.at[i]
        )
        for i in range(PARTS)
    ]
    for copy in copies:
        copy.start()
    return copies


def attend_stage(plan, first, last, ahead, table_ref, q_ref, *refs):
    pb, ka, cores, class_local, places, earlier, slots, turned = plan
    count = len(places)
    pieces, refs = refs[:count], refs[count:]
    old_pieces, refs = refs[:ahead], refs[ahead:]
    if not first:
        refs = refs[1:]
    acc, refs = refs[0], refs[1:]
    if last:
        out_ref, refs = refs[0], refs[1:]
    k_pool, v_pool, held_weights, entries, units, refs = *refs[:5], refs[5:]
    rows = acc.shape[1]
    block_rows = q_ref.shape[0] // slots
    group = rows // block_rows
    rings = ka // cores
    own_slots = slots // cores
    p_at, k_at = lax.axis_index("pb"), lax.axis_index("ka")
    ring_at, core_at = k_at // cores, lax.rem(k_at, cores)
    scale = math.log2(math.e) / math.sqrt(HEAD_DIM)

    def ids(where):
        found = []
        for hops, y, offsets in where:
            ring = lax.rem(ring_at + (rings - y), rings)
            for z in hops:
                source = ring_source(p_at, pb, z)
                for c in offsets:
                    core = lax.rem(core_at + (cores - c), cores)
                    for t in range(class_local):
                        found.append((source * class_local + t) * ka + ring * cores + core)
        return found

    def pool_from(refs_in, at, k_out, v_out):
        for piece in refs_in:
            for i in range(0, piece.shape[0], 2 * class_local):
                span = slice(at, at + class_local)
                k_out[span] = piece[i : i + class_local]
                value = piece[i + class_local : i + 2 * class_local]
                v_out[span, :, :HEAD_DIM] = value
                v_out[span, :, HEAD_DIM:] = jnp.ones(value.shape, v_out.dtype)
                at += class_local

    nothing = sum(piece.shape[0] for piece in pieces) // 2

    if last:
        mine = lax.rem(core_at + turned, cores) * own_slots
        slot_ids = [mine + i for i in range(own_slots)]
    else:
        slot_ids = list(range(slots))

    row_id = lax.broadcasted_iota(jnp.int32, (block_rows, block_rows), 0)
    col_id = lax.broadcasted_iota(jnp.int32, (block_rows, block_rows), 1)
    pool_from(pieces, 0, k_pool, v_pool)
    k_pool[nothing] = jnp.zeros(k_pool.shape[1:], k_pool.dtype)
    v_pool[nothing] = jnp.zeros(v_pool.shape[1:], v_pool.dtype)

    blocks = ids(places)
    unit_count = jnp.int32(0)
    for s in slot_ids:
        row = ring_at * slots + s
        own = table_ref[row, 0]
        place = 2 * unit_count
        for index, block in enumerate(blocks):
            entries[place] = jnp.where(block == own, index + nothing + 1, index)
            place = place + table_ref[row, 1 + block]
        entries[place] = nothing
        ends = lax.div(place + 1, 2)
        if first:

            @pl.when(ends == unit_count)
            def _(s=s):
                acc[s] = jnp.zeros(acc.shape[1:], acc.dtype)


        def mark(u, carry, s=s):
            units[u] = s
            return carry

        lax.fori_loop(unit_count, ends, mark, 0)
        unit_count = ends
    def query_rows(s):
        return jnp.concatenate(
            [
                q_ref[
                    pl.ds(pl.multiple_of(s * block_rows, block_rows), block_rows),
                    x * HEAD_DIM : (x + 1) * HEAD_DIM,
                ]
                for x in range(group)
            ],
            axis=0,
        )

    def pair_of(u):
        raw = [entries[2 * u], entries[2 * u + 1]]
        owns = [entry > nothing for entry in raw]
        return owns, [jnp.where(o, e - (nothing + 1), e) for o, e in zip(owns, raw)]

    def weigh(u):
        owns, index = pair_of(u)
        keys = jnp.concatenate([k_pool[i] for i in index], axis=0)
        reach = jnp.concatenate(
            [
                jnp.where(col_id <= row_id + jnp.where(own, 0, block_rows), 0.0, HIDDEN)
                for own in owns
            ],
            axis=1,
        )
        power = dot(query_rows(units[u]), keys, 1) * scale
        power = power + jnp.concatenate([reach] * group, axis=0)
        held_weights[...] = jnp.exp2(power).astype(held_weights.dtype)

    def add(u):
        _, index = pair_of(u)
        s = units[u]
        values = jnp.concatenate([v_pool[i] for i in index], axis=0)
        added = dot(held_weights[...], values, 0)
        old = acc[s]
        if first:
            fresh = (u == 0) | (units[jnp.maximum(u - 1, 0)] != s)
            old = jnp.where(fresh, 0.0, old)
        acc[s] = old + added

    @pl.when(unit_count > 0)
    def _():
        weigh(0)

        def both(u, carry):
            add(u)
            weigh(u + 1)
            return carry

        lax.fori_loop(0, unit_count - 1, both, 0)
        add(unit_count - 1)

    if not last:
        return

    top, k_all, v_all = refs

    def finish(s, i):
        under = acc[s, :, HEAD_DIM:]
        result = (acc[s, :, :HEAD_DIM] / under).astype(out_ref.dtype)
        for x in range(group):
            out_ref[
                i * block_rows : (i + 1) * block_rows, x * HEAD_DIM : (x + 1) * HEAD_DIM
            ] = result[x * block_rows : (x + 1) * block_rows]
        low = high = [under[j : j + 8] for j in range(0, rows, 8)]
        while len(low) > 1:
            low = [functools.reduce(jnp.minimum, low[j : j + 2]) for j in range(0, len(low), 2)]
            high = [functools.reduce(jnp.maximum, high[j : j + 2]) for j in range(0, len(high), 2)]
        return low[0], high[0]

    low, high = zip(*[finish(s, i) for i, s in enumerate(slot_ids)])
    low, high = functools.reduce(jnp.minimum, low), functools.reduce(jnp.maximum, high)
    safe = (low > 2.0**-HEADROOM) & (high < 2.0**HEADROOM)

    @pl.when(jnp.min(jnp.where(safe, 1.0, 0.0)) < 0.5)
    def _():
        pool_from(old_pieces, 0, k_all, v_all)
        pool_from(pieces, sum(p.shape[0] for p in old_pieces) // 2, k_all, v_all)
        blocks_all = ids(earlier) + blocks
        for i, s in enumerate(slot_ids):
            row = ring_at * slots + s
            own = table_ref[row, 0]
            place = jnp.int32(0)
            for index, block in enumerate(blocks_all):
                entries[place] = jnp.where(block == own, index + len(blocks_all), index)
                place = place + table_ref[row, 1 + block]
            acc[s] = jnp.zeros(acc.shape[1:], acc.dtype)
            top[...] = jnp.full(top.shape, MASKED, top.dtype)

            def one_block(e, carry, s=s):
                is_own = entries[e] >= len(blocks_all)
                index = jnp.where(is_own, entries[e] - len(blocks_all), entries[e])
                reach = jnp.where(
                    col_id <= row_id + jnp.where(is_own, 0, block_rows), 0.0, HIDDEN
                )
                scores = dot(query_rows(s), k_all[index], 1)
                weights, shrinks = [], []
                for x in range(group):
                    span = slice(x * block_rows, (x + 1) * block_rows)
                    power = scores[span] * scale + reach
                    new = jnp.maximum(top[span], jnp.max(power, axis=1, keepdims=True))
                    shrink = jnp.exp2(top[span] - new)
                    top[span] = new
                    weights.append(jnp.exp2(power - new).astype(jnp.bfloat16))
                    shrinks.append(jnp.concatenate([shrink, shrink], axis=1))
                added = dot(jnp.concatenate(weights, axis=0), v_all[index], 0)
                acc[s] = acc[s] * jnp.concatenate(shrinks, axis=0) + added
                return carry

            lax.fori_loop(0, place, one_block, 0)
            finish(s, i)


def cut(cores, *refs):
    ins, out_ref = refs[:-1], refs[-1]
    count = ins[0].shape[0]
    width = out_ref.shape[2]
    core = lax.rem(lax.axis_index("ka"), cores)
    for c in range(cores):

        @pl.when(core == c)
        def _():
            for i, ref in enumerate(ins):
                out_ref[i * count : (i + 1) * count] = ref[
                    :, 0, :, c * width : (c + 1) * width
                ]


def fetch(cores, queries_ref, out_ref, sems):
    rows, width = out_ref.shape
    at = lax.axis_index("ka")
    copies = copy_rows(
        queries_ref.at[
            pl.ds(pl.multiple_of(at // cores * rows, HEAD_DIM), rows),
            pl.ds(pl.multiple_of(lax.rem(at, cores) * width, HEAD_DIM), width),
        ],
        out_ref,
        sems,
    )
    for copy in copies:
        copy.wait()


def join(cores, own_ref, other_ref, out_ref, sems):
    width = own_ref.shape[1]
    core = lax.rem(lax.axis_index("ka"), cores)
    copies = []
    for i, ref in enumerate((own_ref, other_ref)):
        at = pl.multiple_of(lax.rem(core + (cores - i), cores) * width, HEAD_DIM)
        copies += copy_rows(ref, out_ref.at[:, pl.ds(at, width)], sems.at[i])
    for copy in copies:
        copy.wait()


def on_device(queries, keys, values, q_order, block_mask):
    pb, ka = lax.axis_size("pb"), lax.axis_size("ka")
    class_local, _, block_rows, kv_width = keys.shape
    cores = 2 if ka % 2 == 0 and kv_width == 2 * HEAD_DIM else 1
    rings = ka // cores
    head_width = kv_width // cores
    width = queries.shape[1] // cores
    rows = width // head_width * block_rows
    own_slots = queries.shape[0] // block_rows // ka
    slots = own_slots * cores

    vmem = pl.BlockSpec(memory_space=pltpu.VMEM)
    smem = pl.BlockSpec(memory_space=pltpu.SMEM)

    anywhere = pl.BlockSpec(memory_space=pl.ANY)
    stages = min(STAGES, pb)
    sources = pb // stages

    own_queries = pl.pallas_call(
        functools.partial(fetch, cores),
        out_shape=jax.ShapeDtypeStruct((slots * block_rows, width), queries.dtype),
        in_specs=[anywhere],
        out_specs=vmem,
        scratch_shapes=[pltpu.SemaphoreType.DMA((PARTS,))],
        compiler_params=pltpu.CompilerParams(vmem_limit_bytes=50 * 2**20),
    )(queries)
    raw = [keys, values]
    for c in range(1, cores):
        raw += [turn(keys, ka, cores, 0, c), turn(values, ka, cores, 0, c)]
    start = pl.pallas_call(
        functools.partial(cut, cores),
        out_shape=jax.ShapeDtypeStruct(
            (2 * cores * class_local, block_rows, head_width), keys.dtype
        ),
        in_specs=[vmem] * len(raw),
        out_specs=vmem,
        compiler_params=pltpu.CompilerParams(vmem_limit_bytes=SMALL * 2**20),
    )(*raw)

    start, q_order = lax.optimization_barrier((start, q_order))
    table = jnp.concatenate([q_order[:, None], block_mask], axis=1)
    def blocks_of(where):
        return sum(len(hops) * len(offsets) * class_local for hops, _, offsets in where)

    def call(first, last, turned, pieces, places, earlier, own_queries, state, extra):
        held = blocks_of(places)
        everything = held + blocks_of(earlier)
        here = own_slots if last else slots
        outs = [jax.ShapeDtypeStruct((slots, rows, 2 * HEAD_DIM), jnp.float32)]
        scratch = [
            pltpu.VMEM((held + 1, block_rows, HEAD_DIM), jnp.bfloat16),
            pltpu.VMEM((held + 1, block_rows, 2 * HEAD_DIM), jnp.bfloat16),
            pltpu.VMEM((rows, 2 * block_rows), jnp.bfloat16),
            pltpu.SMEM((max(here * (held + 1) + 1, everything + 1),), jnp.int32),
            pltpu.SMEM((here * (held // 2 + 1),), jnp.int32),
        ]
        if last:
            outs.append(jax.ShapeDtypeStruct((own_slots * block_rows, width), queries.dtype))
            scratch += [
                pltpu.VMEM((rows, HEAD_DIM), jnp.float32),
                pltpu.VMEM((everything, block_rows, HEAD_DIM), jnp.bfloat16),
                pltpu.VMEM((everything, block_rows, 2 * HEAD_DIM), jnp.bfloat16),
            ]
        pooled = held + (everything if last else 0)
        room = LIMIT * 2**20 + pooled * block_rows * HEAD_DIM * 6
        state_at = 2 + len(places) + len(extra)
        return pl.pallas_call(
            functools.partial(
                attend_stage,
                (pb, ka, cores, class_local, places, earlier, slots, turned),
                first,
                last,
                len(extra),
            ),
            out_shape=outs,
            in_specs=[smem]
            + [vmem] * (1 + len(places))
            + [vmem] * (len(extra) + len(state)),
            out_specs=[vmem] * len(outs),
            input_output_aliases={state_at + i: i for i in range(len(state))},
            scratch_shapes=scratch,
            compiler_params=pltpu.CompilerParams(vmem_limit_bytes=room),
            cost_estimate=pl.CostEstimate(
                flops=2**31, bytes_accessed=2**22, transcendentals=2**20
            ),
        )(table, own_queries, *pieces, *extra, *state)

    def along(array, count):
        found = []
        for _ in range(count):
            array = along_ring(array, pb)
            found.append(array)
        return found

    def stacked(arrays):
        return arrays[0] if len(arrays) == 1 else jnp.concatenate(arrays, axis=0)

    def beside(array):
        found = []
        for _ in range(rings - 1):
            array = turn(array, ka, cores, 1, 0)
            found.append(array)
        return found

    every = list(range(cores))
    state, earlier, before = [], [], []

    def work(state, pieces, places):
        state = call(not earlier, False, 0, pieces, places, earlier, own_queries, state, [])
        earlier.extend(places)
        before.extend(pieces)
        return state

    if rings == cores == 2 and pb == STAGES:
        tie = lax.optimization_barrier
        half = start.shape[0] // 2
        on = along_ring(start, pb)
        later, table = tie((start, table))
        others = beside(later)[0]
        state = work(state, [start], [([0], 0, every)])
        again, state = tie((start, state))
        back = along_ring(again, pb, -1)
        on, state = tie((on, state))
        on_others = beside(on)[0]
        state = work(state, [on], [([1], 0, every)])
        on, back, state = tie((on, back, state))
        back_others, two = beside(back)[0], along_ring(on, pb)
        state = work(state, [back, others], [([pb - 1], 0, every), ([0], 1, every)])
        on_others, state = tie((on_others, state))
        two_high = along_ring(on_others[half:], pb)
        state = work(state, [on_others], [([1], 1, every)])
        two, state = tie((two, state))
        two_low = turn(two[:half], ka, cores, 1, 0)
        state = work(state, [two, back_others], [([2], 0, every), ([pb - 1], 1, every)])
        pieces, places = [two_low, two_high], [([2], 1, [0]), ([2], 1, [1])]
    else:
        arrived = [start] + along(start, sources - 1)
        others, places = [], []
        for stage in range(stages):
            hops = range(stage * sources, (stage + 1) * sources)
            if stage:
                arrived, others, state = lax.optimization_barrier((arrived, others, state))
            near = stacked(arrived)
            pieces, places = [near] + others, [(hops, 0, every)] + places
            if stage < stages - 1:
                arrived = along(arrived[-1], sources)
            others = beside(near)
            state = work(state, pieces, places)
            places = [(hops, y, every) for y in range(1, rings)]
        pieces = others
    halves = []
    for c in reversed(range(cores)):
        *state, half = call(False, True, c, pieces, places, earlier, own_queries, state, before)
        halves.append(half)
    if cores == 1:
        return halves[0]
    return pl.pallas_call(
        functools.partial(join, cores),
        out_shape=jax.ShapeDtypeStruct((own_slots * block_rows, cores * width), queries.dtype),
        in_specs=[vmem] * 2,
        out_specs=anywhere,
        scratch_shapes=[pltpu.SemaphoreType.DMA((cores, PARTS))],
        compiler_params=pltpu.CompilerParams(vmem_limit_bytes=SMALL * 2**20),
    )(halves[1], turn(halves[0], ka, cores, 0, 1))


def solution(mesh):
    in_specs = (
        P("pb", "ha"),
        P("pb", "ka", None, "ha"),
        P("pb", "ka", None, "ha"),
        P("pb"),
        P("pb", None),
    )
    out_specs = P(("pb", "ka"), "ha")
    return jax.shard_map(
        on_device, mesh=mesh, in_specs=in_specs, out_specs=out_specs, check_vma=False
    )
```
